32 devices in a mesh: row: 8 (over z, core), col: 4 (over y, x), rep: 1.
Axes of the slice: x: 2, y: 2, z: 4, core: 2. Of those that a mesh axis runs over, the one named last changes fastest.
Arguments:
- momentum: float32 [1, 8192, 8192], P('rep', 'row', 'col'), may hold values from -6 to 6
- gradient: bfloat16 [1, 8192, 8192], P('rep', 'row', 'col'), may hold values from -6 to 6
- weight: float32 [8192, 8192], P('row', 'col'), may hold values from -0.0625 to 0.0625
- right_basis: float32 [8192, 256], P('col'), may hold values from -6 to 6
Outputs:
- new_momentum: float32 [1, 8192, 8192], P('rep', 'row', 'col')
- new_weight: float32 [8192, 8192], P('row', 'col')
- new_basis: float32 [8192, 256], P('col')
The draws below stay inside these ranges and needn't reach their ends.
All inputs are finite; a program needn't handle non-finite values.
Results may differ from the reference program's by a relative error of at most 0.0012.
Values sent between devices are 32-bit elements; how exact they have to be, the bound alone decides.
No kernel may reach another device: no remote copies, remote signals or barrier semaphores. Data moves between devices by JAX's collectives and lax.ppermute only.
A program may use at most 128 MiB of HBM per device.

```python
import jax
import jax.numpy as jnp
from jax import lax

D = 8192
RANK = 256
ITERS = 2
REPS = 1


def block_levels(key, extent, split, low, largest):
    loudness = 1.0
    for position, parts in split:
        draws = jax.random.uniform(jax.random.fold_in(jax.random.fold_in(key, 6), position), (parts,), jnp.float32, low / len(split), largest / len(split))
        loudness = loudness * jnp.repeat(jnp.exp(draws), extent[position] // parts).reshape((-1,) + (1,) * (len(extent) - 1 - position))
    return loudness


def scatter_about(stream_key, shape, scale, bound, shards=(), held_as=jnp.bfloat16):
    drawn = scale * jax.random.normal(stream_key, shape, jnp.float32)
    if shards:
        drawn = drawn * block_levels(stream_key, shape, shards, -0.22, 0.18)
    return jnp.clip(drawn, -bound, bound).astype(held_as)


def setup_inputs(seed: int = 0) -> dict:
    seeds = jax.random.split(jax.random.key(seed), 5)
    return {
        "momentum": scatter_about(seeds[0], (REPS, D, D), 1.0, 6.0, ((1, 8), (2, 4)), jnp.float32),
        "gradient": scatter_about(seeds[1], (REPS, D, D), 1.0, 6.0, ((1, 8), (2, 4))),
        "weight": scatter_about(seeds[2], (D, D), D ** -0.5, 0.0625, ((0, 8), (1, 4)), jnp.float32),
        "right_basis": scatter_about(seeds[3], (D, RANK), 1.0, 6.0, ((0, 4),), jnp.float32),
    }


beta_mom = 0.95
learn_rate = 0.05

def reference(momentum, gradient, weight, right_basis):
    highest = lax.Precision.HIGHEST
    buffer = momentum + gradient.astype(jnp.float32)
    mean_buffer = lax.optimization_barrier(jnp.mean(buffer, axis=0))
    basis_now = right_basis
    ortho = None
    factor = None
    for sweep in range(ITERS):
        left = jnp.dot(mean_buffer.astype(jnp.float32), basis_now.astype(jnp.float32), precision=highest, preferred_element_type=jnp.float32)
        gram_full = jnp.dot(left.T.astype(jnp.float32), left.astype(jnp.float32), precision=highest, preferred_element_type=jnp.float32)
        low_factor = jnp.linalg.cholesky(gram_full)
        ortho = jax.scipy.linalg.solve_triangular(low_factor, left.T, lower=True).T
        factor = jnp.dot(mean_buffer.T.astype(jnp.float32), ortho.astype(jnp.float32), precision=highest, preferred_element_type=jnp.float32)
        rms_cols = jnp.sqrt(lax.optimization_barrier(jnp.mean(factor * factor, axis=0)) + 1e-06)
        basis_now = factor / rms_cols
    feedback = jnp.dot(ortho.astype(jnp.float32), factor.T.astype(jnp.float32), precision=highest, preferred_element_type=jnp.float32)
    new_momentum = buffer - (1.0 - beta_mom) * feedback[None]
    update = jnp.dot(ortho.astype(jnp.float32), basis_now.T.astype(jnp.float32), precision=highest, preferred_element_type=jnp.float32)
    new_weight = weight - learn_rate * jnp.sqrt(jnp.float32(D) / jnp.float32(RANK)) * update
    return (new_momentum, new_weight, basis_now)
```

```python
import jax
import jax.numpy as jnp
from jax import lax
from jax.experimental import pallas as pl
from jax.experimental.pallas import tpu as pltpu
from jax.sharding import PartitionSpec as P

D = 8192
RANK = 256
ITERS = 2
HALF = RANK // 2
SUB = 8

beta_mom = 0.95
learn_rate = 0.05

HIGHEST = lax.Precision.HIGHEST
HIGH = lax.Precision.HIGH


def dot(a, b, dims=((1,), (0,)), precision=HIGH):
    return lax.dot_general(a, b, (dims, ((), ())), precision=precision, preferred_element_type=jnp.float32)


def inverse_factor(block):
    lanes = lax.broadcasted_iota(jnp.int32, (SUB, HALF), 1)
    subs = lax.broadcasted_iota(jnp.int32, (SUB, HALF), 0)
    tiles = [block[SUB * i:SUB * (i + 1), :] for i in range(HALF // SUB)]
    for k in range(HALF):
        t, s = divmod(k, SUB)
        row = jnp.broadcast_to(tiles[t][s:s + 1, :], (SUB, HALF))
        r = lax.rsqrt(jnp.broadcast_to(row[:, k:k + 1], (SUB, HALF)))
        here = lanes == k
        scaled = jnp.where(here, r, row * r)
        for i in range(t, HALF // SUB):
            mult = jnp.broadcast_to(tiles[i][:, k:k + 1], (SUB, HALF)) * r
            base = jnp.where(here, 0.0, tiles[i])
            new = base - mult * scaled
            if i == t:
                new = jnp.where(subs > s, new, jnp.where(subs == s, scaled, tiles[i]))
            tiles[i] = new
    full = jnp.concatenate(tiles, axis=0)
    rows = lax.broadcasted_iota(jnp.int32, (HALF, HALF), 0)
    cols = lax.broadcasted_iota(jnp.int32, (HALF, HALF), 1)
    return jnp.where(cols <= rows, full, 0.0)


def inverse_kernel(gram_ref, out_ref):
    first = inverse_factor(gram_ref[:HALF, :HALF])
    side = dot(gram_ref[HALF:, :HALF], first, ((1,), (1,)), HIGHEST)
    rest = gram_ref[HALF:, HALF:] - dot(side, side, ((1,), (1,)), HIGHEST)
    second = inverse_factor(rest)
    out_ref[:HALF, :HALF] = first
    out_ref[:HALF, HALF:] = jnp.zeros((HALF, HALF), jnp.float32)
    out_ref[HALF:, :HALF] = -dot(second, dot(side, first, precision=HIGHEST), precision=HIGHEST)
    out_ref[HALF:, HALF:] = second


def inverse_cholesky(gram):
    return pl.pallas_call(
        inverse_kernel,
        out_shape=jax.ShapeDtypeStruct((RANK, RANK), jnp.float32),
        in_specs=[pl.BlockSpec(memory_space=pltpu.VMEM)],
        out_specs=pl.BlockSpec(memory_space=pltpu.VMEM),
        cost_estimate=pl.CostEstimate(flops=20_000_000_000, bytes_accessed=2 * 4 * RANK * RANK, transcendentals=RANK),
        name="inverse_cholesky",
    )(gram)


def swap(x, axis, bit):
    size = lax.axis_size(axis)
    return lax.ppermute(x, axis, [(i, i ^ bit) for i in range(size)])


def four_sum(x, axis, bits):
    one, two = bits
    return (x + swap(x, axis, one)) + (swap(x, axis, two) + swap(x, axis, one ^ two))


def left_sum(x):
    if lax.axis_size("col") != 4 or lax.axis_size("rep") != 1:
        return lax.psum(x, ("col", "rep"))
    half = x.shape[0] // 2
    up, low = x[:half], x[half:]
    up = up + swap(up, "col", 1)
    low = low + swap(low, "col", 2)
    up = up + swap(up, "col", 2)
    low = low + swap(low, "col", 1)
    return jnp.concatenate([up, low], axis=0)


def gram_sum(left):
    if lax.axis_size("col") != 4 or lax.axis_size("row") != 8:
        return lax.psum(dot(left, left, ((0,), (0,)), HIGHEST), "row")
    quarter = RANK // 4
    me = lax.axis_index("col")
    mine = lax.dynamic_slice_in_dim(left, me * quarter, quarter, axis=1)
    part = dot(mine, left, ((0,), (0,)), HIGHEST)
    part = part + swap(part, "row", 1)
    part = four_sum(part, "row", (2, 4))
    whole = jnp.zeros((4, quarter, RANK), jnp.float32)
    for bit in range(4):
        piece = part if bit == 0 else swap(part, "col", bit)
        whole = lax.dynamic_update_slice(whole, piece[None], (me ^ bit, 0, 0))
    return whole.reshape(RANK, RANK)


CHUNKS = 4


def factor_sum(x):
    if lax.axis_size("row") != 8 or lax.axis_size("rep") != 1:
        return lax.psum(x, ("row", "rep"))
    n = x.shape[1]
    me = lax.axis_index("row")
    core = me % 2
    rows = HALF // CHUNKS
    middle = jnp.logical_or(me // 2 == 1, me // 2 == 2)
    halves = x.reshape(2, CHUNKS, rows, n)
    kept = lax.dynamic_index_in_dim(halves, core, 0, keepdims=False)
    given = lax.dynamic_index_in_dim(halves, 1 - core, 0, keepdims=False)
    inward = [(0, 2), (1, 3), (6, 4), (7, 5)]
    across = [(2, 4), (3, 5), (4, 2), (5, 3)]
    outward = [(2, 0), (3, 1), (4, 6), (5, 7)]
    done = []
    for c in range(CHUNKS):
        part = kept[c] + swap(given[c], "row", 1)
        side = part + lax.ppermute(part, "row", inward)
        total = side + lax.ppermute(side, "row", across)
        done.append(jnp.where(middle, total, lax.ppermute(total, "row", outward)))
    mine = jnp.concatenate(done, axis=0)
    other = swap(mine, "row", 1)
    low = jnp.where(core == 0, mine, other)
    high = jnp.where(core == 0, other, mine)
    return jnp.concatenate([low, high], axis=0)


def column_sum(x):
    if lax.axis_size("col") != 4:
        return lax.psum(x, "col")
    return four_sum(x, "col", (1, 2))


def on_device(momentum, gradient, weight, right_basis):
    replicas = lax.axis_size("rep")
    buffer = momentum[0] + gradient[0].astype(jnp.float32)
    left_part = dot(buffer, right_basis) / replicas
    rms = None
    for sweep in range(ITERS):
        left = left_sum(left_part)
        if sweep:
            left = left / rms
        gram = gram_sum(left)
        wide = factor_sum(dot(left, buffer, ((0,), (0,))) / replicas)
        inverse = inverse_cholesky(gram)
        factor_t = dot(inverse, wide, precision=HIGHEST)
        square_sum = column_sum(jnp.sum(factor_t * factor_t, axis=1)[None, :])
        rms = jnp.sqrt(square_sum / jnp.float32(D) + 1e-06)
        if sweep < ITERS - 1:
            left_part = dot(buffer, factor_t, ((1,), (1,))) / replicas
    ortho = dot(left, inverse, ((1,), (1,)), HIGHEST)
    feedback = dot(ortho, factor_t)
    new_momentum = (buffer - (1.0 - beta_mom) * feedback)[None]
    basis_t = factor_t / rms.T
    update = dot(ortho, basis_t)
    new_weight = weight - learn_rate * jnp.sqrt(jnp.float32(D) / jnp.float32(RANK)) * update
    return (new_momentum, new_weight, basis_t.T)


def solution(mesh):
    return jax.shard_map(
        on_device,
        mesh=mesh,
        in_specs=(P("rep", "row", "col"), P("rep", "row", "col"), P("row", "col"), P("col", None)),
        out_specs=(P("rep", "row", "col"), P("row", "col"), P("col", None)),
        check_vma=False,
    )
```

```python
import jax
import jax.numpy as jnp
from jax import lax
from jax.experimental import pallas as pl
from jax.experimental.pallas import tpu as pltpu
from jax.sharding import PartitionSpec as P

D = 8192
RANK = 256
ITERS = 2
HALF = RANK // 2
SUB = 8

beta_mom = 0.95
learn_rate = 0.05

HIGHEST = lax.Precision.HIGHEST
HIGH = lax.Precision.HIGH


def dot(a, b, dims=((1,), (0,)), precision=HIGH):
    return lax.dot_general(a, b, (dims, ((), ())), precision=precision, preferred_element_type=jnp.float32)


def inverse_factor(block):
    shape = (SUB, HALF)
    lanes = lax.broadcasted_iota(jnp.int32, shape, 1)
    subs = lax.broadcasted_iota(jnp.int32, shape, 0)
    count = HALF // SUB

    def spread(tile, lane):
        return jnp.broadcast_to(tile[:, lane:lane + 1], shape)

    def repeat(tile, sub):
        return jnp.broadcast_to(tile[sub:sub + 1, :], shape)

    tiles = [block[SUB * i:SUB * (i + 1), :] for i in range(count)]
    for t in range(count):
        low = SUB * t
        panel = jnp.logical_and(lanes >= low, lanes < low + SUB)
        cols = [spread(tiles[t], low + j) for j in range(SUB)]
        tile = jnp.where(panel, 0.0, tiles[t])
        scale, rows, upper = [], [], {}
        for j in range(SUB):
            r = lax.rsqrt(repeat(cols[j], j))
            mult = jnp.where(subs > j, cols[j] * r, 0.0)
            for k in range(j + 1, SUB):
                upper[j, k] = repeat(cols[k], j) * r
                cols[k] = cols[k] - mult * upper[j, k]
            row = jnp.where(lanes == low + j, r, repeat(tile, j) * r)
            tile = jnp.where(subs == j, row, tile - mult * row)
            scale.append(r)
            rows.append(row)
        tiles[t] = tile
        for i in range(t + 1, count):
            cols = [spread(tiles[i], low + j) for j in range(SUB)]
            tile = jnp.where(panel, 0.0, tiles[i])
            for j in range(SUB):
                mult = cols[j] * scale[j]
                for k in range(j + 1, SUB):
                    cols[k] = cols[k] - mult * upper[j, k]
                tile = tile - mult * rows[j]
            tiles[i] = tile
    full = jnp.concatenate(tiles, axis=0)
    down = lax.broadcasted_iota(jnp.int32, (HALF, HALF), 0)
    across = lax.broadcasted_iota(jnp.int32, (HALF, HALF), 1)
    return jnp.where(across <= down, full, 0.0)


def inverse_kernel(gram_ref, out_ref):
    first = inverse_factor(gram_ref[:HALF, :HALF])
    side = dot(gram_ref[HALF:, :HALF], first, ((1,), (1,)), HIGHEST)
    rest = gram_ref[HALF:, HALF:] - dot(side, side, ((1,), (1,)), HIGHEST)
    second = inverse_factor(rest)
    out_ref[:HALF, :HALF] = first
    out_ref[:HALF, HALF:] = jnp.zeros((HALF, HALF), jnp.float32)
    out_ref[HALF:, :HALF] = -dot(second, dot(side, first, precision=HIGHEST), precision=HIGHEST)
    out_ref[HALF:, HALF:] = second


def inverse_cholesky(gram):
    return pl.pallas_call(
        inverse_kernel,
        out_shape=jax.ShapeDtypeStruct((RANK, RANK), jnp.float32),
        in_specs=[pl.BlockSpec(memory_space=pltpu.VMEM)],
        out_specs=pl.BlockSpec(memory_space=pltpu.VMEM),
        cost_estimate=pl.CostEstimate(flops=12_000_000_000, bytes_accessed=2 * 4 * RANK * RANK, transcendentals=RANK),
        name="inverse_cholesky",
    )(gram)


def swap(x, axis, bit):
    size = lax.axis_size(axis)
    return lax.ppermute(x, axis, [(i, i ^ bit) for i in range(size)])


def four_sum(x, axis, bits):
    one, two = bits
    return (x + swap(x, axis, one)) + (swap(x, axis, two) + swap(x, axis, one ^ two))


def left_sum(up, low):
    if lax.axis_size("col") != 4 or lax.axis_size("rep") != 1:
        return lax.psum(jnp.concatenate([up, low], axis=0), ("col", "rep"))
    up = up + swap(up, "col", 1)
    low = low + swap(low, "col", 2)
    up = up + swap(up, "col", 2)
    low = low + swap(low, "col", 1)
    return jnp.concatenate([up, low], axis=0)


def blocks_from(x, me):
    parts = x.reshape((4, x.shape[0] // 4) + x.shape[1:])
    parts = jnp.where(me & 1, parts[jnp.array([1, 0, 3, 2])], parts)
    parts = jnp.where(me & 2, parts[jnp.array([2, 3, 0, 1])], parts)
    return parts.reshape(x.shape)


def row_sum(x, hold=None):
    quarter = RANK // 4
    part = x[:2 * quarter] + swap(x[2 * quarter:], "row", 1)
    side = part[:quarter] + swap(part[quarter:], "row", 2)
    total = side + swap(side, "row", 4)
    mine = jnp.concatenate([total, swap(total, "row", 2)], axis=0)
    if hold is not None:
        mine, hold = lax.optimization_barrier((mine, hold))
    return jnp.concatenate([mine, swap(mine, "row", 1)], axis=0), hold


def factor_sums(left, buffer):
    if lax.axis_size("row") != 8 or lax.axis_size("rep") != 1:
        gram = lax.psum(dot(left, left, ((0,), (0,)), HIGHEST), "row")
        wide = lax.psum(dot(left, buffer, ((0,), (0,))), ("row", "rep")) / lax.axis_size("rep")
        return inverse_cholesky(gram), wide
    row = lax.axis_index("row")
    me = 2 * (row & 1) + ((row >> 1) & 1)
    turned = blocks_from(left.T, me)
    first = buffer.shape[1] * 3 // 8
    gram_part = dot(turned, left, precision=HIGHEST)
    wide_first = dot(turned, buffer[:, :first])
    wide_rest = dot(turned, buffer[:, first:])
    done, _ = row_sum(jnp.concatenate([gram_part, wide_first], axis=1))
    gram = blocks_from(done[:, :RANK], me)
    inverse = inverse_cholesky(gram)
    rest, inverse = row_sum(wide_rest, inverse)
    return inverse, blocks_from(jnp.concatenate([done[:, RANK:], rest], axis=1), me)


def column_sum(x):
    if lax.axis_size("col") != 4:
        return lax.psum(x, "col")
    return four_sum(x, "col", (1, 2))


def on_device(momentum, gradient, weight, right_basis):
    replicas = lax.axis_size("rep")
    buffer = momentum[0] + gradient[0].astype(jnp.float32)
    half = buffer.shape[0] // 2
    basis, dims = right_basis, ((1,), (0,))
    for sweep in range(ITERS):
        left = left_sum(dot(buffer[:half], basis, dims) / replicas, dot(buffer[half:], basis, dims) / replicas)
        if sweep:
            left = left / rms
        inverse, wide = factor_sums(left, buffer)
        factor_t = dot(inverse, wide, precision=HIGHEST)
        square_sum = column_sum(jnp.sum(factor_t * factor_t, axis=1)[None, :])
        rms = jnp.sqrt(square_sum / jnp.float32(D) + 1e-06)
        basis, dims = factor_t, ((1,), (1,))
    ortho = dot(left, inverse, ((1,), (1,)), HIGHEST)
    feedback = dot(ortho, factor_t)
    new_momentum = (buffer - (1.0 - beta_mom) * feedback)[None]
    basis_t = factor_t / rms.T
    update = dot(ortho, basis_t)
    new_weight = weight - learn_rate * jnp.sqrt(jnp.float32(D) / jnp.float32(RANK)) * update
    return (new_momentum, new_weight, basis_t.T)


def solution(mesh):
    return jax.shard_map(
        on_device,
        mesh=mesh,
        in_specs=(P("rep", "row", "col"), P("rep", "row", "col"), P("row", "col"), P("col", None)),
        out_specs=(P("rep", "row", "col"), P("row", "col"), P("col", None)),
        check_vma=False,
    )
```

```python
import functools

import jax
import jax.numpy as jnp
from jax import lax
from jax.experimental import pallas as pl
from jax.experimental.pallas import tpu as pltpu
from jax.sharding import PartitionSpec as P

D = 8192
RANK = 256
ITERS = 2
HALF = RANK // 2
QUARTER = RANK // 4
SUB = 8
TILE = 256
FIRST = 2

beta_mom = 0.95
learn_rate = 0.05

F32 = jnp.float32
BF16 = jnp.bfloat16
HIGHEST = lax.Precision.HIGHEST
HIGH = lax.Precision.HIGH
NT = ((1,), (1,))
NN = ((1,), (0,))


def dot(a, b, dims=NN, precision=None):
    return lax.dot_general(a, b, (dims, ((), ())), precision=precision, preferred_element_type=F32)


def split(x):
    high = x.astype(BF16)
    return high, (x - high.astype(F32)).astype(BF16)


def dot3(a, b, dims=NN):
    return dot(a[0], b[0], dims) + (dot(a[1], b[0], dims) + dot(a[0], b[1], dims))


def call(kernel, name, flops, moved, **rest):
    rest.setdefault("compiler_params", pltpu.CompilerParams(vmem_limit_bytes=24 * 2**20))
    return pl.pallas_call(
        kernel,
        name=name,
        cost_estimate=pl.CostEstimate(flops=flops, bytes_accessed=moved, transcendentals=0),
        **rest,
    )


def shaped(*shape, dtype=F32):
    return jax.ShapeDtypeStruct(shape, dtype)


VMEM = pl.BlockSpec(memory_space=pltpu.VMEM)
SMEM = pl.BlockSpec(memory_space=pltpu.SMEM)


def inverse_factor(block):
    shape = (SUB, HALF)
    lanes = lax.broadcasted_iota(jnp.int32, shape, 1)
    subs = lax.broadcasted_iota(jnp.int32, shape, 0)
    count = HALF // SUB

    def spread(tile, lane):
        return jnp.broadcast_to(tile[:, lane:lane + 1], shape)

    def repeat(tile, sub):
        return jnp.broadcast_to(tile[sub:sub + 1, :], shape)

    tiles = [block[SUB * i:SUB * (i + 1), :] for i in range(count)]
    for t in range(count):
        low = SUB * t
        panel = jnp.logical_and(lanes >= low, lanes < low + SUB)
        cols = [spread(tiles[t], low + j) for j in range(SUB)]
        tile = jnp.where(panel, 0.0, tiles[t])
        scale, rows, upper = [], [], {}
        for j in range(SUB):
            r = lax.rsqrt(repeat(cols[j], j))
            mult = jnp.where(subs > j, cols[j] * r, 0.0)
            for k in range(j + 1, SUB):
                upper[j, k] = repeat(cols[k], j) * r
                cols[k] = cols[k] - mult * upper[j, k]
            row = jnp.where(lanes == low + j, r, repeat(tile, j) * r)
            tile = jnp.where(subs == j, row, tile - mult * row)
            scale.append(r)
            rows.append(row)
        tiles[t] = tile
        for i in range(t + 1, count):
            cols = [spread(tiles[i], low + j) for j in range(SUB)]
            tile = jnp.where(panel, 0.0, tiles[i])
            for j in range(SUB):
                mult = cols[j] * scale[j]
                for k in range(j + 1, SUB):
                    cols[k] = cols[k] - mult * upper[j, k]
                tile = tile - mult * rows[j]
            tiles[i] = tile
    full = jnp.concatenate(tiles, axis=0)
    down = lax.broadcasted_iota(jnp.int32, (HALF, HALF), 0)
    across = lax.broadcasted_iota(jnp.int32, (HALF, HALF), 1)
    return jnp.where(across <= down, full, 0.0)


def inverse_body(gram_ref, out_ref):
    first = inverse_factor(gram_ref[:HALF, :HALF])
    side = dot(gram_ref[HALF:, :HALF], first, NT, HIGHEST)
    rest = gram_ref[HALF:, HALF:] - dot(side, side, NT, HIGHEST)
    second = inverse_factor(rest)
    out_ref[:HALF, :HALF] = first
    out_ref[:HALF, HALF:] = jnp.zeros((HALF, HALF), F32)
    out_ref[HALF:, :HALF] = -dot(second, dot(side, first, precision=HIGHEST), precision=HIGHEST)
    out_ref[HALF:, HALF:] = second


def inverse_cholesky(gram):
    return call(
        inverse_body, "inverse_cholesky", 12_000_000_000, 2 * 4 * RANK * RANK,
        out_shape=shaped(RANK, RANK), in_specs=[VMEM], out_specs=VMEM,
    )(gram)


def place(out_ref, me, mine, other):
    for b in range(4):
        block = (mine, other)[b // 2][QUARTER * (b % 2):QUARTER * (b % 2 + 1), :]
        out_ref[pl.ds(pl.multiple_of((me ^ b) * QUARTER, QUARTER), QUARTER), :] = block


def inverse_blocks_kernel(me_ref, mine_ref, other_ref, out_ref, gram_ref):
    place(gram_ref, me_ref[0], mine_ref[...], other_ref[...])
    inverse_body(gram_ref, out_ref)


def inverse_cholesky_blocks(me, mine, other):
    block = pl.BlockSpec((HALF, RANK), lambda i: (0, 0))
    return call(
        inverse_blocks_kernel, "inverse_cholesky", 12_000_000_000, 2 * 4 * RANK * RANK,
        out_shape=shaped(RANK, RANK), grid=(1,),
        in_specs=[SMEM, block, block], out_specs=pl.BlockSpec((RANK, RANK), lambda i: (0, 0)),
        scratch_shapes=[pltpu.VMEM((RANK, RANK), F32)],
    )(me, mine, other)


def start_kernel(momentum_ref, gradient_ref, basis_ref, *refs):
    high_ref, low_ref, left_ref = refs[-3:]
    buffer = split(momentum_ref[...] + gradient_ref[...].astype(F32))
    high_ref[...], low_ref[...] = buffer
    part = dot3(buffer, split(basis_ref[...]))

    @pl.when(pl.program_id(0) == 0)
    def _():
        left_ref[...] = part

    @pl.when(pl.program_id(0) > 0)
    def _():
        left_ref[...] += part


def start(half, momentum, gradient, basis, held=()):
    rows, cols = momentum.shape
    step = 2 * TILE
    block = pl.BlockSpec((rows // 2, step), lambda i: (half, i))
    return call(
        start_kernel, "start", 6 * rows // 2 * cols * RANK, 5 * rows * cols,
        out_shape=[shaped(rows, cols, dtype=BF16)] * 2 + [shaped(rows // 2, RANK)],
        grid=(cols // step,),
        in_specs=[block, block, pl.BlockSpec((step, RANK), lambda i: (i, 0))] + [pl.BlockSpec(memory_space=pl.ANY)] * len(held),
        out_specs=[block, block, pl.BlockSpec((rows // 2, RANK), lambda i: (0, 0))],
        input_output_aliases={3: 0, 4: 1} if held else {},
    )(momentum, gradient, basis, *held)


def left_kernel(high_ref, low_ref, fhigh_ref, flow_ref, left_ref):
    part = dot3((high_ref[...], low_ref[...]), (fhigh_ref[...], flow_ref[...]), NT)

    @pl.when(pl.program_id(0) == 0)
    def _():
        left_ref[...] = part

    @pl.when(pl.program_id(0) > 0)
    def _():
        left_ref[...] += part


def left_product(half, buffer, factor):
    rows, cols = buffer[0].shape
    step = 2 * TILE
    block = pl.BlockSpec((rows // 2, step), lambda i: (half, i))
    fblock = pl.BlockSpec((RANK, step), lambda i: (0, i))
    return call(
        left_kernel, "left", 6 * rows // 2 * cols * RANK, 2 * rows * cols,
        out_shape=shaped(rows // 2, RANK), grid=(cols // step,),
        in_specs=[block, block, fblock, fblock],
        out_specs=pl.BlockSpec((rows // 2, RANK), lambda i: (0, 0)),
    )(*buffer, *factor)


def product_kernel(scaled, *refs):
    me_ref, refs = refs[0], refs[1:]
    squares, refs = (refs[:4], refs[4:]) if scaled else ((), refs)
    up, up_more, down, down_more, high_ref, low_ref = refs[:6]
    keep_ref, give_ref, thigh_ref, tlow_ref, left_ref, turned_ref, plain_ref = refs[6:]
    step = pl.program_id(0)

    @pl.when(step == 0)
    def _():
        rows = up.shape[0]
        top, bottom = up[...] + up_more[...], down[...] + down_more[...]
        if scaled:
            total = (squares[0][0:1, :] + squares[1][0:1, :]) + (squares[2][0:1, :] + squares[3][0:1, :])
            factor = 1.0 / jnp.sqrt(total / F32(D) + F32(1e-06))
            top, bottom = top * factor, bottom * factor
        left_ref[:rows, :] = top
        left_ref[rows:, :] = bottom
        plain_ref[:, :rows] = top.T
        plain_ref[:, rows:] = bottom.T
        me = me_ref[0]
        for b in range(4):
            block = plain_ref[pl.ds(pl.multiple_of((me ^ b) * QUARTER, QUARTER), QUARTER), :]
            where = pl.ds(QUARTER * b, QUARTER)
            turned_ref[where, :] = block
            thigh_ref[where, :], tlow_ref[where, :] = split(block)
        gram = dot(turned_ref[...], left_ref[...], precision=HIGHEST)
        keep_ref[:, :RANK] = gram[:HALF]
        give_ref[:, :RANK] = gram[HALF:]

    part = dot3((thigh_ref[...], tlow_ref[...]), (high_ref[...], low_ref[...]))
    lanes = pl.ds(pl.multiple_of(RANK + step * TILE, TILE), TILE)
    keep_ref[:, lanes] = part[:HALF]
    give_ref[:, lanes] = part[HALF:]


def first_product(me, squares, parts, buffer):
    rows, cols = buffer[0].shape
    width = RANK + FIRST * TILE
    whole = lambda *shape: pl.BlockSpec(shape, lambda i: (0,) * len(shape))
    block = pl.BlockSpec((rows, TILE), lambda i: (0, i))
    return call(
        functools.partial(product_kernel, bool(squares)), "first_product", 12 * rows * width * RANK, 4 * rows * width,
        out_shape=[shaped(HALF, width)] * 2 + [shaped(RANK, rows, dtype=BF16)] * 2 + [shaped(rows, RANK)],
        grid=(FIRST,),
        in_specs=[SMEM] + [whole(SUB, RANK)] * len(squares) + [whole(rows // 2, RANK)] * 4 + [block] * 2,
        out_specs=[whole(HALF, width)] * 2 + [whole(RANK, rows)] * 2 + [whole(rows, RANK)],
        scratch_shapes=[pltpu.VMEM((RANK, rows), F32)] * 2,
    )(me, *squares, *parts, *buffer)


def rest_kernel(thigh_ref, tlow_ref, high_ref, low_ref, keep_ref, give_ref):
    part = dot3((thigh_ref[...], tlow_ref[...]), (high_ref[...], low_ref[...]))
    keep_ref[...] = part[:HALF]
    give_ref[...] = part[HALF:]


def rest_product(turned, buffer):
    rows, cols = buffer[0].shape
    block = pl.BlockSpec((rows, TILE), lambda i: (0, i + FIRST))
    whole = pl.BlockSpec((RANK, rows), lambda i: (0, 0))
    out = pl.BlockSpec((HALF, TILE), lambda i: (0, i))
    width = cols - FIRST * TILE
    return call(
        rest_kernel, "rest_product", 6 * rows * width * RANK, 4 * rows * width,
        out_shape=[shaped(HALF, width)] * 2, grid=(width // TILE,),
        in_specs=[whole] * 2 + [block] * 2, out_specs=[out] * 2,
    )(*turned, *buffer)


def factor_kernel(me_ref, inverse_ref, mine0_ref, other0_ref, mine1_ref, other1_ref, out_ref, high_ref, low_ref, square_ref, wide_ref):
    me = me_ref[0]
    first = mine0_ref.shape[1] - RANK
    place(wide_ref.at[:, :first], me, mine0_ref[:, RANK:], other0_ref[:, RANK:])
    place(wide_ref.at[:, first:], me, mine1_ref[...], other1_ref[...])
    inverse = split(inverse_ref[...])
    square = jnp.zeros((RANK, 1), F32)
    step = 2 * TILE
    for c in range(wide_ref.shape[1] // step):
        lanes = pl.ds(step * c, step)
        part = dot3(inverse, split(wide_ref[:, lanes]))
        out_ref[:, lanes] = part
        high_ref[:, lanes], low_ref[:, lanes] = split(part)
        square = square + jnp.sum(part * part, axis=1, keepdims=True)
    square_ref[...] = jnp.broadcast_to(square, (RANK, HALF)).T[:SUB, :]


def factor_product(me, inverse, mine0, other0, mine1, other1):
    cols = mine0.shape[1] - RANK + mine1.shape[1]
    return call(
        factor_kernel, "factor", 6 * RANK * RANK * cols, 16 * RANK * cols,
        out_shape=[shaped(RANK, cols), shaped(RANK, cols, dtype=BF16), shaped(RANK, cols, dtype=BF16), shaped(SUB, RANK)],
        in_specs=[SMEM] + [VMEM] * 5, out_specs=[VMEM] * 4,
        scratch_shapes=[pltpu.VMEM((RANK, cols), F32)],
    )(me, inverse, mine0, other0, mine1, other1)


def momentum_kernel(left_ref, inverse_ref, fhigh_ref, high_ref, low_ref, out_ref, ortho_ref):
    ortho = dot3(split(left_ref[...]), split(inverse_ref[...]), NT)
    ortho_ref[...] = ortho
    feedback = dot(ortho.astype(BF16), fhigh_ref[...])
    out_ref[...] = (high_ref[...].astype(F32) + low_ref[...].astype(F32)) - F32(1.0 - beta_mom) * feedback


def momentum_update(left, inverse, fhigh, buffer):
    rows, cols = buffer[0].shape
    step = HALF
    block = pl.BlockSpec((step, cols), lambda i: (i, 0))
    narrow = pl.BlockSpec((step, RANK), lambda i: (i, 0))
    return call(
        momentum_kernel, "momentum", 2 * rows * cols * RANK, 8 * rows * cols,
        out_shape=[shaped(rows, cols), shaped(rows, RANK)], grid=(rows // step,),
        in_specs=[narrow, pl.BlockSpec((RANK, RANK), lambda i: (0, 0)), pl.BlockSpec((RANK, cols), lambda i: (0, 0)), block, block],
        out_specs=[block, narrow],
    )(left, inverse, fhigh, *buffer)


def weight_kernel(ortho_ref, s0, s1, s2, s3, fhigh_ref, flow_ref, factor_ref, weight_ref, out_ref, basis_ref):
    total = (s0[0:1, :] + s1[0:1, :]) + (s2[0:1, :] + s3[0:1, :])
    scale = 1.0 / jnp.sqrt(total / F32(D) + F32(1e-06))
    ortho = split(ortho_ref[...] * (scale * F32(learn_rate * (D / RANK) ** 0.5)))
    out_ref[...] = weight_ref[...] - dot3(ortho, (fhigh_ref[...], flow_ref[...]))
    basis_ref[...] = factor_ref[...].T * scale


def weight_update(ortho, squares, factor, fhigh, flow, weight):
    rows, cols = weight.shape
    step = HALF
    block = pl.BlockSpec((step, cols), lambda i: (i, 0))
    wide = pl.BlockSpec((RANK, cols), lambda i: (0, 0))
    count = rows // step
    return call(
        weight_kernel, "weight", 6 * rows * cols * RANK, 8 * rows * cols,
        out_shape=[shaped(rows, cols), shaped(cols, RANK)], grid=(count,),
        in_specs=[pl.BlockSpec((step, RANK), lambda i: (i, 0))] + [pl.BlockSpec((SUB, RANK), lambda i: (0, 0))] * 4
        + [wide, wide, pl.BlockSpec((RANK, cols // count), lambda i: (0, i)), block],
        out_specs=[block, pl.BlockSpec((cols // count, RANK), lambda i: (i, 0))],
    )(ortho, *squares, fhigh, flow, factor, weight)


def swap(x, axis, bit):
    size = lax.axis_size(axis)
    return lax.ppermute(x, axis, [(i, i ^ bit) for i in range(size)])


def after(x, *others):
    return lax.optimization_barrier((x,) + others)[0]


def left_parts(up, low):
    up = up + swap(up, "col", 1)
    low = low + swap(low, "col", 2)
    return up, swap(up, "col", 2), low, swap(low, "col", 1)


def tuned(momentum, gradient, weight, right_basis):
    row = lax.axis_index("row")
    me = (2 * (row & 1) + ((row >> 1) & 1)).astype(jnp.int32)[None]
    high, low, up = start(0, momentum[0], gradient[0], right_basis)
    high, low, down = start(1, momentum[0], gradient[0], right_basis, (high, low))
    buffer = (high, low)
    squares = ()
    for sweep in range(ITERS):
        parts = left_parts(up, down)
        keep0, give0, thigh, tlow, left = first_product(me, squares, parts, buffer)
        keep1, give1 = rest_product((thigh, tlow), buffer)
        part0 = keep0 + swap(give0, "row", 1)
        part1 = keep1 + swap(give1, "row", 1)
        pair0 = swap(part0[QUARTER:], "row", 2)
        side0 = part0[:QUARTER] + pair0
        pair1 = swap(after(part1[QUARTER:], pair0), "row", 2)
        total0 = side0 + swap(side0, "row", 4)
        side1 = part1[:QUARTER] + pair1
        total1 = side1 + swap(after(side1, total0), "row", 4)
        mine0 = jnp.concatenate([total0, swap(total0, "row", 2)], axis=0)
        other0 = swap(mine0, "row", 1)
        inverse = inverse_cholesky_blocks(me, mine0, other0)
        mine1 = jnp.concatenate([total1, swap(after(total1, inverse), "row", 2)], axis=0)
        other1 = swap(mine1, "row", 1)
        factor, fhigh, flow, square = factor_product(me, inverse, mine0, other0, mine1, other1)
        squares = (square, swap(square, "col", 1), swap(square, "col", 2), swap(square, "col", 3))
        if sweep < ITERS - 1:
            up = left_product(0, buffer, (fhigh, flow))
            down = left_product(1, buffer, (fhigh, flow))
    new_momentum, ortho = momentum_update(left, inverse, fhigh, buffer)
    new_weight, new_basis = weight_update(ortho, squares, factor, fhigh, flow, weight)
    return new_momentum[None], new_weight, new_basis


def general(momentum, gradient, weight, right_basis):
    replicas = lax.axis_size("rep")
    buffer = momentum[0] + gradient[0].astype(F32)
    basis, dims = right_basis, NN
    for sweep in range(ITERS):
        left = lax.psum(dot(buffer, basis, dims, HIGH) / replicas, ("col", "rep"))
        if sweep:
            left = left / rms
        gram = lax.psum(dot(left, left, ((0,), (0,)), HIGHEST), "row")
        wide = lax.psum(dot(left, buffer, ((0,), (0,)), HIGH) / replicas, ("row", "rep"))
        inverse = inverse_cholesky(gram)
        factor = dot(inverse, wide, precision=HIGHEST)
        rms = jnp.sqrt(lax.psum(jnp.sum(factor * factor, axis=1)[None, :], "col") / F32(D) + 1e-06)
        basis, dims = factor, NT
    ortho = dot(left, inverse, NT, HIGHEST)
    new_momentum = (buffer - (1.0 - beta_mom) * dot(ortho, factor, precision=HIGH))[None]
    basis = factor / rms.T
    new_weight = weight - learn_rate * jnp.sqrt(F32(D) / F32(RANK)) * dot(ortho, basis, precision=HIGH)
    return new_momentum, new_weight, basis.T


def solution(mesh):
    sizes = dict(mesh.shape)
    fits = sizes["row"] == 8 and sizes["col"] == 4 and sizes["rep"] == 1
    return jax.shard_map(
        tuned if fits else general,
        mesh=mesh,
        in_specs=(P("rep", "row", "col"), P("rep", "row", "col"), P("row", "col"), P("col", None)),
        out_specs=(P("rep", "row", "col"), P("row", "col"), P("col", None)),
        check_vma=False,
    )
```

```python
import functools

import jax
import jax.numpy as jnp
from jax import lax
from jax.experimental import pallas as pl
from jax.experimental.pallas import tpu as pltpu
from jax.sharding import PartitionSpec as P

D = 8192
RANK = 256
ITERS = 2
HALF = RANK // 2
QUARTER = RANK // 4
PART = RANK // 8
SUB = 8
TILE = 256

beta_mom = 0.95
learn_rate = 0.05

F32 = jnp.float32
BF16 = jnp.bfloat16
HIGHEST = lax.Precision.HIGHEST
HIGH = lax.Precision.HIGH
NT = ((1,), (1,))
NN = ((1,), (0,))


def dot(a, b, dims=NN, precision=None):
    return lax.dot_general(a, b, (dims, ((), ())), precision=precision, preferred_element_type=F32)


def split(x):
    high = x.astype(BF16)
    return high, (x - high.astype(F32)).astype(BF16)


def dot3(a, b, dims=NN):
    return dot(a[0], b[0], dims) + (dot(a[1], b[0], dims) + dot(a[0], b[1], dims))


def call(kernel, name, flops, moved, **rest):
    rest.setdefault("compiler_params", pltpu.CompilerParams(vmem_limit_bytes=24 * 2**20))
    return pl.pallas_call(
        kernel,
        name=name,
        cost_estimate=pl.CostEstimate(flops=flops, bytes_accessed=moved, transcendentals=0),
        **rest,
    )


def shaped(*shape, dtype=F32):
    return jax.ShapeDtypeStruct(shape, dtype)


VMEM = pl.BlockSpec(memory_space=pltpu.VMEM)
SMEM = pl.BlockSpec(memory_space=pltpu.SMEM)


def inverse_factor(block):
    shape = (SUB, HALF)
    lanes = lax.broadcasted_iota(jnp.int32, shape, 1)
    subs = lax.broadcasted_iota(jnp.int32, shape, 0)
    count = HALF // SUB

    def spread(tile, lane):
        return jnp.broadcast_to(tile[:, lane:lane + 1], shape)

    def repeat(tile, sub):
        return jnp.broadcast_to(tile[sub:sub + 1, :], shape)

    tiles = [block[SUB * i:SUB * (i + 1), :] for i in range(count)]
    for t in range(count):
        low = SUB * t
        panel = jnp.logical_and(lanes >= low, lanes < low + SUB)
        cols = [spread(tiles[t], low + j) for j in range(SUB)]
        tile = jnp.where(panel, 0.0, tiles[t])
        scale, rows, upper = [], [], {}
        for j in range(SUB):
            r = lax.rsqrt(repeat(cols[j], j))
            mult = jnp.where(subs > j, cols[j] * r, 0.0)
            for k in range(j + 1, SUB):
                upper[j, k] = repeat(cols[k], j) * r
                cols[k] = cols[k] - mult * upper[j, k]
            row = jnp.where(lanes == low + j, r, repeat(tile, j) * r)
            tile = jnp.where(subs == j, row, tile - mult * row)
            scale.append(r)
            rows.append(row)
        tiles[t] = tile
        for i in range(t + 1, count):
            cols = [spread(tiles[i], low + j) for j in range(SUB)]
            tile = jnp.where(panel, 0.0, tiles[i])
            for j in range(SUB):
                mult = cols[j] * scale[j]
                for k in range(j + 1, SUB):
                    cols[k] = cols[k] - mult * upper[j, k]
                tile = tile - mult * rows[j]
            tiles[i] = tile
    full = jnp.concatenate(tiles, axis=0)
    down = lax.broadcasted_iota(jnp.int32, (HALF, HALF), 0)
    across = lax.broadcasted_iota(jnp.int32, (HALF, HALF), 1)
    return jnp.where(across <= down, full, 0.0)


def inverse_body(gram_ref, out_ref):
    first = inverse_factor(gram_ref[:HALF, :HALF])
    side = dot(gram_ref[HALF:, :HALF], first, NT, HIGHEST)
    rest = gram_ref[HALF:, HALF:] - dot(side, side, NT, HIGHEST)
    second = inverse_factor(rest)
    out_ref[:HALF, :HALF] = first
    out_ref[:HALF, HALF:] = jnp.zeros((HALF, HALF), F32)
    out_ref[HALF:, :HALF] = -dot(second, dot(side, first, precision=HIGHEST), precision=HIGHEST)
    out_ref[HALF:, HALF:] = second


def inverse_cholesky(gram):
    return call(
        inverse_body, "inverse_cholesky", 12_000_000_000, 2 * 4 * RANK * RANK,
        out_shape=shaped(RANK, RANK), in_specs=[VMEM], out_specs=VMEM,
    )(gram)


def place(out_ref, me, mine, other):
    for b in range(4):
        block = (mine, other)[b // 2][PART * (b % 2):PART * (b % 2 + 1), :]
        out_ref[pl.ds(pl.multiple_of((me ^ b) * PART, PART), PART), :] = block


def start_kernel(momentum_ref, gradient_ref, basis_ref, high_ref, low_ref, a_ref, b_ref):
    step = pl.program_id(0)
    width = momentum_ref.shape[1]
    lanes = pl.ds(pl.multiple_of(step * width, width), width)
    buffer = split(momentum_ref[...] + gradient_ref[...].astype(F32))
    high_ref[:, lanes], low_ref[:, lanes] = buffer
    part = dot3(buffer, split(basis_ref[...]))

    @pl.when(step == 0)
    def _():
        a_ref[...] = part[:, :HALF]
        b_ref[...] = part[:, HALF:]

    @pl.when(step > 0)
    def _():
        a_ref[...] += part[:, :HALF]
        b_ref[...] += part[:, HALF:]


def start(half, momentum, gradient, basis):
    rows, cols = momentum.shape
    step = 2 * TILE
    block = pl.BlockSpec((rows // 2, step), lambda i: (half, i))
    return call(
        start_kernel, "start", 3 * rows * cols * RANK, 5 * rows * cols,
        out_shape=[shaped(rows // 2, cols, dtype=BF16)] * 2 + [shaped(rows // 2, HALF)] * 2,
        grid=(cols // step,),
        in_specs=[block, block, pl.BlockSpec((step, RANK), lambda i: (i, 0))], out_specs=[VMEM] * 4,
        compiler_params=pltpu.CompilerParams(vmem_limit_bytes=50 * 2**20),
    )(momentum, gradient, basis)


def left_kernel(high_ref, low_ref, factor_ref, *refs):
    left_ref = refs[-1]
    rows = high_ref.shape[0]
    both = dot(high_ref[...], factor_ref[...], NT)
    left_ref[:rows, :] = (both[:, :HALF] + both[:, HALF:]) + dot(low_ref[...], factor_ref[:HALF, :], NT)
    if len(refs) == 2:
        left_ref[rows:, :] = refs[0][...]


def left_product(buffer, factor, *square):
    rows, cols = buffer[0].shape
    return call(
        left_kernel, "left", 4 * rows * cols * RANK, 4 * rows * cols,
        out_shape=shaped(rows + SUB * len(square), HALF), in_specs=[VMEM] * (3 + len(square)), out_specs=VMEM,
    )(*buffer, factor, *square)


def product_kernel(first, scaled, me_ref, *refs):
    before, refs = ((), refs) if first else (refs[:1], refs[1:])
    up, up_more, down, down_more = refs[:4]
    highs, lows = refs[4:8:2], refs[5:8:2]
    keep_ref, give_ref, left_ref, plain_ref, turned_ref, pair_ref = refs[8:]
    rows = down.shape[0]
    top, bottom = up[:rows, :] + up_more[:rows, :], down[...] + down_more[...]
    if scaled:
        total = up[rows:rows + 1, :] + up_more[rows:rows + 1, :]
        scale = 1.0 / jnp.sqrt(total / F32(D) + F32(1e-06))
        top, bottom = top * scale, bottom * scale
    left_ref[:rows, :] = top
    left_ref[rows:, :] = bottom
    plain_ref[:, :rows] = top.T
    plain_ref[:, rows:] = bottom.T
    me = me_ref[0]
    for b in range(4):
        block = plain_ref[pl.ds(pl.multiple_of((me ^ b) * PART, PART), PART), :]
        turned_ref[PART * b:PART * (b + 1), :] = block
        pair_ref[PART * b:PART * (b + 1), :], pair_ref[HALF + PART * b:HALF + PART * (b + 1), :] = split(block)
    spot = 0
    for ref in (*before, left_ref):
        gram = dot(turned_ref[...], ref[...], precision=HIGHEST)
        keep_ref[:, spot:spot + HALF] = gram[:QUARTER]
        give_ref[:, spot:spot + HALF] = gram[QUARTER:]
        spot += HALF
    for c in range(highs[0].shape[1] // TILE):
        lanes = pl.ds(c * TILE, TILE)
        both = dot(pair_ref[:, :rows], highs[0][:, lanes]) + dot(pair_ref[:, rows:], highs[1][:, lanes])
        part = dot(pair_ref[:HALF, :rows], lows[0][:, lanes]) + dot(pair_ref[:HALF, rows:], lows[1][:, lanes])
        part = (both[:HALF] + both[HALF:]) + part
        lanes = pl.ds(spot + c * TILE, TILE)
        keep_ref[:, lanes] = part[:QUARTER]
        give_ref[:, lanes] = part[QUARTER:]


def product(scaled, me, before, parts, buffers):
    rows, cols = buffers[0].shape
    width = HALF * (len(before) + 1) + cols
    return call(
        functools.partial(product_kernel, not before, scaled), "product", 8 * rows * width * RANK, 8 * rows * width,
        out_shape=[shaped(QUARTER, width)] * 2 + [shaped(2 * rows, HALF)],
        in_specs=[SMEM] + [VMEM] * (8 + len(before)), out_specs=[VMEM] * 3,
        scratch_shapes=[pltpu.VMEM((HALF, 2 * rows), F32)] * 2 + [pltpu.VMEM((RANK, 2 * rows), BF16)],
    )(me, *before, *parts, *buffers)


def solved(inverse, wide_ref, out_ref, pair_ref):
    inverse = split(inverse)
    square = jnp.zeros((HALF, 1), F32)
    step = 2 * TILE
    for c in range(wide_ref.shape[1] // step):
        lanes = pl.ds(step * c, step)
        part = dot3(inverse, split(wide_ref[:, lanes]))
        out_ref[:, lanes] = part
        pair_ref[:HALF, lanes], pair_ref[HALF:, lanes] = split(part)
        square = square + jnp.sum(part * part, axis=1, keepdims=True)
    return jnp.broadcast_to(square, (HALF, HALF)).T[:SUB, :]


def first_kernel(me_ref, mine_ref, other_ref, inverse_ref, wide_ref, out_ref, pair_ref, square_ref, gram_ref):
    me = me_ref[0]
    place(gram_ref, me, mine_ref[:, :HALF], other_ref[:, :HALF])
    place(wide_ref, me, mine_ref[:, HALF:], other_ref[:, HALF:])
    inverse_ref[...] = inverse_factor(gram_ref[...])
    square_ref[...] = solved(inverse_ref[...], wide_ref, out_ref, pair_ref)


def first_solve(me, mine, other):
    cols = mine.shape[1] - HALF
    return call(
        first_kernel, "first_solve", 5_000_000_000, 20 * HALF * cols,
        out_shape=[shaped(HALF, HALF), shaped(HALF, cols), shaped(HALF, cols), shaped(RANK, cols, dtype=BF16), shaped(SUB, HALF)],
        in_specs=[SMEM, VMEM, VMEM], out_specs=[VMEM] * 5, scratch_shapes=[pltpu.VMEM((HALF, HALF), F32)],
    )(me, mine, other)


def second_kernel(me_ref, mine_ref, other_ref, first_ref, wide0_ref, inverse_ref, out_ref, pair_ref, square_ref, gram_ref, wide_ref):
    me = me_ref[0]
    place(gram_ref, me, mine_ref[:, :RANK], other_ref[:, :RANK])
    place(wide_ref.at[HALF:, :], me, mine_ref[:, RANK:], other_ref[:, RANK:])
    wide_ref[:HALF, :] = wide0_ref[...]
    first = first_ref[...]
    side = dot(gram_ref[:, :HALF], first, NT, HIGHEST)
    second = inverse_factor(gram_ref[:, HALF:] - dot(side, side, NT, HIGHEST))
    inverse_ref[:HALF, :HALF] = first
    inverse_ref[:HALF, HALF:] = jnp.zeros((HALF, HALF), F32)
    inverse_ref[HALF:, :HALF] = -dot(second, dot(side, first, precision=HIGHEST), precision=HIGHEST)
    inverse_ref[HALF:, HALF:] = second
    square_ref[...] = solved(inverse_ref[HALF:, :], wide_ref, out_ref, pair_ref)


def second_solve(me, mine, other, first, wide0):
    cols = mine.shape[1] - RANK
    return call(
        second_kernel, "second_solve", 6_000_000_000, 20 * HALF * cols,
        out_shape=[shaped(RANK, RANK), shaped(HALF, cols), shaped(RANK, cols, dtype=BF16), shaped(SUB, HALF)],
        in_specs=[SMEM] + [VMEM] * 4, out_specs=[VMEM] * 4,
        scratch_shapes=[pltpu.VMEM((HALF, RANK), F32), pltpu.VMEM((RANK, cols), F32)],
    )(me, mine, other, first, wide0)


def momentum_kernel(left0_ref, left1_ref, inverse_ref, pair0_ref, pair1_ref, *refs):
    highs, lows = refs[:4:2], refs[1:4:2]
    out_ref, ortho_ref, fhigh_ref, flow_ref = refs[4:]
    step, rows = pl.program_id(0), out_ref.shape[0]

    @pl.when(step == 0)
    def _():
        fhigh_ref[:HALF, :] = pair0_ref[:HALF, :]
        fhigh_ref[HALF:, :] = pair1_ref[:HALF, :]
        flow_ref[:HALF, :] = pair0_ref[HALF:, :]
        flow_ref[HALF:, :] = pair1_ref[HALF:, :]

    here = pl.ds(pl.multiple_of(step * rows, rows), rows)
    left = jnp.concatenate([left0_ref[here, :], left1_ref[here, :]], axis=1)
    ortho = dot3(split(left), split(inverse_ref[...]), NT)
    ortho_ref[here, :] = ortho
    feedback = F32(1.0 - beta_mom) * dot(ortho.astype(BF16), fhigh_ref[...])
    count = highs[0].shape[0] // rows
    for h in range(2):
        @pl.when(step // count == h)
        def _():
            mine = pl.ds(pl.multiple_of((step - h * count) * rows, rows), rows)
            out_ref[...] = (highs[h][mine, :].astype(F32) + lows[h][mine, :].astype(F32)) - feedback


def momentum_update(lefts, inverse, pairs, buffers):
    rows, cols = 2 * buffers[0].shape[0], buffers[0].shape[1]
    return call(
        momentum_kernel, "momentum", 2 * rows * cols * RANK, 4 * rows * cols,
        out_shape=[shaped(rows, cols), shaped(rows, RANK)] + [shaped(RANK, cols, dtype=BF16)] * 2, grid=(rows // HALF,),
        in_specs=[VMEM] * 9, out_specs=[pl.BlockSpec((HALF, cols), lambda i: (i, 0))] + [VMEM] * 3,
    )(*lefts, inverse, *pairs, *buffers)


def weight_kernel(ortho_ref, s0, s1, s2, s3, fhigh_ref, flow_ref, factor0_ref, factor1_ref, weight_ref, out_ref, basis_ref):
    total = (s0[0:1, :] + s1[0:1, :]) + (s2[0:1, :] + s3[0:1, :])
    scale = 1.0 / jnp.sqrt(total / F32(D) + F32(1e-06))
    step, rows, lanes = pl.program_id(0), out_ref.shape[0], basis_ref.shape[0]
    here = pl.ds(pl.multiple_of(step * rows, rows), rows)
    ortho = split(ortho_ref[here, :] * (scale * F32(learn_rate * (D / RANK) ** 0.5)))
    out_ref[...] = weight_ref[here, :] - dot3(ortho, (fhigh_ref[...], flow_ref[...]))
    there = pl.ds(pl.multiple_of(step * lanes, lanes), lanes)
    basis_ref[:, :HALF] = factor0_ref[:, there].T * scale[:, :HALF]
    basis_ref[:, HALF:] = factor1_ref[:, there].T * scale[:, HALF:]


def weight_update(ortho, squares, fhigh, flow, factors, weight):
    rows, cols = weight.shape
    count = rows // HALF
    return call(
        weight_kernel, "weight", 6 * rows * cols * RANK, 4 * rows * cols,
        out_shape=[shaped(rows, cols), shaped(cols, RANK)], grid=(count,),
        in_specs=[VMEM] * 10,
        out_specs=[pl.BlockSpec((HALF, cols), lambda i: (i, 0)), pl.BlockSpec((cols // count, RANK), lambda i: (i, 0))],
    )(ortho, *squares, fhigh, flow, *factors, weight)


def swap(x, axis, bit):
    size = lax.axis_size(axis)
    return lax.ppermute(x, axis, [(i, i ^ bit) for i in range(size)])


def after(x, *others):
    return lax.optimization_barrier((x,) + others)[0]


def left_parts(up, down):
    up = up + swap(up, "col", 1)
    down = down + swap(down, "col", 2)
    return up, swap(up, "col", 2), down, swap(down, "col", 1)


def row_sum(keep, give):
    part = keep + swap(give, "row", 1)
    side = part[:PART] + swap(part[PART:], "row", 2)
    total = side + swap(side, "row", 4)
    mine = jnp.concatenate([total, swap(total, "row", 2)], axis=0)
    return mine, swap(mine, "row", 1)


def tuned(momentum, gradient, weight, right_basis):
    row = lax.axis_index("row")
    me = (2 * (row & 1) + ((row >> 1) & 1)).astype(jnp.int32)[None]
    high0, low0, up0, up1 = start(0, momentum[0], gradient[0], right_basis)
    high1, low1, down0, down1 = start(1, momentum[0], gradient[0], right_basis)
    top, bottom = (high0, low0), (high1, low1)
    for sweep in range(ITERS):
        parts = left_parts(up0, down0)
        keep, give, left0 = product(sweep > 0, me, (), parts, (*top, *bottom))
        mine0, other0 = row_sum(keep, give)
        up1, down1 = after(up1, parts[3]), after(down1, parts[1])
        parts = left_parts(up1, down1)
        keep, give, left1 = product(sweep > 0, me, (left0,), parts, (*top, *bottom))
        mine1, other1 = row_sum(keep, give)
        first, wide, factor0, pair0, square0 = first_solve(me, mine0, other0)
        if sweep < ITERS - 1:
            up0, down0 = left_product(top, pair0, square0), left_product(bottom, pair0)
        inverse, factor1, pair1, square1 = second_solve(me, mine1, other1, first, wide)
        if sweep < ITERS - 1:
            up1, down1 = left_product(top, pair1, square1), left_product(bottom, pair1)
    square = jnp.concatenate([square0, square1], axis=1)
    squares = (square, swap(square, "col", 1), swap(square, "col", 2), swap(square, "col", 3))
    new_momentum, ortho, fhigh, flow = momentum_update((left0, left1), inverse, (pair0, pair1), (*top, *bottom))
    new_weight, new_basis = weight_update(ortho, squares, fhigh, flow, (factor0, factor1), weight)
    return new_momentum[None], new_weight, new_basis


def general(momentum, gradient, weight, right_basis):
    replicas = lax.axis_size("rep")
    buffer = momentum[0] + gradient[0].astype(F32)
    basis, dims = right_basis, NN
    for sweep in range(ITERS):
        left = lax.psum(dot(buffer, basis, dims, HIGH) / replicas, ("col", "rep"))
        if sweep:
            left = left / rms
        gram = lax.psum(dot(left, left, ((0,), (0,)), HIGHEST), "row")
        wide = lax.psum(dot(left, buffer, ((0,), (0,)), HIGH) / replicas, ("row", "rep"))
        inverse = inverse_cholesky(gram)
        factor = dot(inverse, wide, precision=HIGHEST)
        rms = jnp.sqrt(lax.psum(jnp.sum(factor * factor, axis=1)[None, :], "col") / F32(D) + 1e-06)
        basis, dims = factor, NT
    ortho = dot(left, inverse, NT, HIGHEST)
    new_momentum = (buffer - (1.0 - beta_mom) * dot(ortho, factor, precision=HIGH))[None]
    basis = factor / rms.T
    new_weight = weight - learn_rate * jnp.sqrt(F32(D) / F32(RANK)) * dot(ortho, basis, precision=HIGH)
    return new_momentum, new_weight, basis.T


def solution(mesh):
    sizes = dict(mesh.shape)
    fits = sizes["row"] == 8 and sizes["col"] == 4 and sizes["rep"] == 1
    return jax.shard_map(
        tuned if fits else general,
        mesh=mesh,
        in_specs=(P("rep", "row", "col"), P("rep", "row", "col"), P("row", "col"), P("col", None)),
        out_specs=(P("rep", "row", "col"), P("row", "col"), P("col", None)),
        check_vma=False,
    )
```

```python
import functools

import jax
import jax.numpy as jnp
from jax import lax
from jax.experimental import pallas as pl
from jax.experimental.pallas import tpu as pltpu
from jax.sharding import PartitionSpec as P

D = 8192
RANK = 256
ITERS = 2
HALF = RANK // 2
QUARTER = RANK // 4
PART = RANK // 8
SUB = 8
TILE = 256

beta_mom = 0.95
learn_rate = 0.05

F32 = jnp.float32
BF16 = jnp.bfloat16
HIGHEST = lax.Precision.HIGHEST
HIGH = lax.Precision.HIGH
NT = ((1,), (1,))
NN = ((1,), (0,))


def dot(a, b, dims=NN, precision=None):
    return lax.dot_general(a, b, (dims, ((), ())), precision=precision, preferred_element_type=F32)


def split(x):
    high = x.astype(BF16)
    return high, (x - high.astype(F32)).astype(BF16)


def dot3(a, b, dims=NN):
    return dot(a[0], b[0], dims) + (dot(a[1], b[0], dims) + dot(a[0], b[1], dims))


def call(kernel, name, flops, moved, **rest):
    rest.setdefault("compiler_params", pltpu.CompilerParams(vmem_limit_bytes=24 * 2**20))
    return pl.pallas_call(
        kernel,
        name=name,
        cost_estimate=pl.CostEstimate(flops=flops, bytes_accessed=moved, transcendentals=0),
        **rest,
    )


def shaped(*shape, dtype=F32):
    return jax.ShapeDtypeStruct(shape, dtype)


VMEM = pl.BlockSpec(memory_space=pltpu.VMEM)
SMEM = pl.BlockSpec(memory_space=pltpu.SMEM)


def inverse_factor(block):
    shape = (SUB, HALF)
    lanes = lax.broadcasted_iota(jnp.int32, shape, 1)
    subs = lax.broadcasted_iota(jnp.int32, shape, 0)
    count = HALF // SUB

    def spread(tile, lane):
        return jnp.broadcast_to(tile[:, lane:lane + 1], shape)

    def repeat(tile, sub):
        return jnp.broadcast_to(tile[sub:sub + 1, :], shape)

    tiles = [block[SUB * i:SUB * (i + 1), :] for i in range(count)]
    for t in range(count):
        low = SUB * t
        panel = jnp.logical_and(lanes >= low, lanes < low + SUB)
        cols = [spread(tiles[t], low + j) for j in range(SUB)]
        tile = jnp.where(panel, 0.0, tiles[t])
        scale, rows, upper = [], [], {}
        for j in range(SUB):
            r = lax.rsqrt(repeat(cols[j], j))
            mult = jnp.where(subs > j, cols[j] * r, 0.0)
            for k in range(j + 1, SUB):
                upper[j, k] = repeat(cols[k], j) * r
                cols[k] = cols[k] - mult * upper[j, k]
            row = jnp.where(lanes == low + j, r, repeat(tile, j) * r)
            tile = jnp.where(subs == j, row, tile - mult * row)
            scale.append(r)
            rows.append(row)
        tiles[t] = tile
        for i in range(t + 1, count):
            cols = [spread(tiles[i], low + j) for j in range(SUB)]
            tile = jnp.where(panel, 0.0, tiles[i])
            for j in range(SUB):
                mult = cols[j] * scale[j]
                for k in range(j + 1, SUB):
                    cols[k] = cols[k] - mult * upper[j, k]
                tile = tile - mult * rows[j]
            tiles[i] = tile
    full = jnp.concatenate(tiles, axis=0)
    down = lax.broadcasted_iota(jnp.int32, (HALF, HALF), 0)
    across = lax.broadcasted_iota(jnp.int32, (HALF, HALF), 1)
    return jnp.where(across <= down, full, 0.0)


def inverse_body(gram_ref, out_ref):
    first = inverse_factor(gram_ref[:HALF, :HALF])
    side = dot(gram_ref[HALF:, :HALF], first, NT, HIGHEST)
    rest = gram_ref[HALF:, HALF:] - dot(side, side, NT, HIGHEST)
    second = inverse_factor(rest)
    out_ref[:HALF, :HALF] = first
    out_ref[:HALF, HALF:] = jnp.zeros((HALF, HALF), F32)
    out_ref[HALF:, :HALF] = -dot(second, dot(side, first, precision=HIGHEST), precision=HIGHEST)
    out_ref[HALF:, HALF:] = second


def inverse_cholesky(gram):
    return call(
        inverse_body, "inverse_cholesky", 12_000_000_000, 2 * 4 * RANK * RANK,
        out_shape=shaped(RANK, RANK), in_specs=[VMEM], out_specs=VMEM,
    )(gram)


def place(out_ref, me, mine, other):
    for b in range(4):
        block = (mine, other)[b // 2][PART * (b % 2):PART * (b % 2 + 1), :]
        out_ref[pl.ds(pl.multiple_of((me ^ b) * PART, PART), PART), :] = block


def start_kernel(momentum_ref, gradient_ref, basis_ref, high_ref, low_ref, up0, down0, up1, down1, bhigh_ref, blow_ref):
    rows, cols = momentum_ref.shape
    count = up0.shape[0] // HALF

    def body(momentum, gradient, basis):
        step = pl.program_id(0)

        @pl.when(step == 0)
        def _():
            bhigh_ref[...], blow_ref[...] = split(basis[...])

        here = pl.ds(pl.multiple_of(step * HALF, HALF), HALF)
        buffer = split(momentum[...] + gradient[...].astype(F32))
        high_ref[here, :], low_ref[here, :] = buffer
        part = dot3(buffer, (bhigh_ref[...], blow_ref[...]))
        there = pl.ds(pl.multiple_of(lax.rem(step, count) * HALF, HALF), HALF)

        @pl.when(step < count)
        def _():
            up0[there, :] = part[:, :HALF]
            up1[there, :] = part[:, HALF:]

        @pl.when(step >= count)
        def _():
            down0[there, :] = part[:, :HALF]
            down1[there, :] = part[:, HALF:]

    block = pl.BlockSpec((HALF, cols), lambda i: (i, 0))
    pltpu.emit_pipeline(
        body, grid=(rows // HALF,), in_specs=[block, block, pl.BlockSpec((cols, RANK), lambda i: (0, 0))],
    )(momentum_ref, gradient_ref, basis_ref)


def start(*args):
    rows, cols = args[0].shape
    return call(
        start_kernel, "start", 6 * rows * cols * RANK, 6 * rows * cols,
        out_shape=[shaped(rows, cols, dtype=BF16)] * 2 + [shaped(rows // 2, HALF)] * 4,
        in_specs=[pl.BlockSpec(memory_space=pltpu.HBM)] * 3, out_specs=[VMEM] * 6,
        scratch_shapes=[pltpu.VMEM((cols, RANK), BF16)] * 2,
    )(*(pltpu.with_memory_space_constraint(x, pltpu.HBM) for x in args))


def left_kernel(high_ref, low_ref, factor_ref, *refs):
    up_ref, down_ref = refs[-2:]
    half = down_ref.shape[0]

    for ref, base in ((up_ref, 0), (down_ref, half)):
        @pl.loop(0, half // TILE)
        def _(c):
            here = pl.ds(pl.multiple_of(base + c * TILE, TILE), TILE)
            both = dot(high_ref[here, :], factor_ref[...], NT)
            part = (both[:, :HALF] + both[:, HALF:]) + dot(low_ref[here, :], factor_ref[:HALF, :], NT)
            ref[pl.ds(pl.multiple_of(c * TILE, TILE), TILE), :] = part

    if len(refs) == 3:
        up_ref[half:, :] = refs[0][...]


def left_product(buffer, factor, square):
    rows, cols = buffer[0].shape
    return call(
        left_kernel, "left", 4 * rows * cols * RANK, 4 * rows * cols,
        out_shape=[shaped(rows // 2 + SUB, HALF), shaped(rows // 2, HALF)], in_specs=[VMEM] * 4, out_specs=[VMEM] * 2,
    )(*buffer, factor, square)


def product_kernel(first, scaled, me_ref, *refs):
    before, refs = ((), refs) if first else (refs[:1], refs[1:])
    up, up_more, down, down_more, high_ref, low_ref, keep_ref, give_ref, left_ref, plain_ref, turned_ref, pair_ref = refs
    rows = down.shape[0]
    top, bottom = up[:rows, :] + up_more[:rows, :], down[...] + down_more[...]
    if scaled:
        total = up[rows:rows + 1, :] + up_more[rows:rows + 1, :]
        scale = 1.0 / jnp.sqrt(total / F32(D) + F32(1e-06))
        top, bottom = top * scale, bottom * scale
    left_ref[:rows, :] = top
    left_ref[rows:, :] = bottom
    plain_ref[:, :rows] = top.T
    plain_ref[:, rows:] = bottom.T
    me = me_ref[0]
    for b in range(4):
        block = plain_ref[pl.ds(pl.multiple_of((me ^ b) * PART, PART), PART), :]
        turned_ref[PART * b:PART * (b + 1), :] = block
        pair_ref[PART * b:PART * (b + 1), :], pair_ref[HALF + PART * b:HALF + PART * (b + 1), :] = split(block)
    spot = 0
    for ref in (*before, left_ref):
        gram = dot(turned_ref[...], ref[...], precision=HIGHEST)
        keep_ref[:, spot:spot + HALF] = gram[:QUARTER]
        give_ref[:, spot:spot + HALF] = gram[QUARTER:]
        spot += HALF
    step = 2 * TILE

    @pl.loop(0, high_ref.shape[1] // step)
    def _(c):
        lanes = pl.ds(pl.multiple_of(c * step, step), step)
        both = dot(pair_ref[...], high_ref[:, lanes])
        part = (both[:HALF] + both[HALF:]) + dot(pair_ref[:HALF, :], low_ref[:, lanes])
        lanes = pl.ds(pl.multiple_of(spot + c * step, HALF), step)
        keep_ref[:, lanes] = part[:QUARTER]
        give_ref[:, lanes] = part[QUARTER:]


def product(scaled, me, before, parts, buffer):
    rows, cols = buffer[0].shape
    width = HALF * (len(before) + 1) + cols
    return call(
        functools.partial(product_kernel, not before, scaled), "product", 4 * rows * width * RANK, 4 * rows * width,
        out_shape=[shaped(QUARTER, width)] * 2 + [shaped(rows, HALF)],
        in_specs=[SMEM] + [VMEM] * (6 + len(before)), out_specs=[VMEM] * 3,
        scratch_shapes=[pltpu.VMEM((HALF, rows), F32)] * 2 + [pltpu.VMEM((RANK, rows), BF16)],
    )(me, *before, *parts, *buffer)


def solved(inverse, wide_ref, out_ref, pair_ref):
    inverse = split(inverse)
    square = jnp.zeros((HALF, 1), F32)
    step = 2 * TILE
    for c in range(wide_ref.shape[1] // step):
        lanes = pl.ds(step * c, step)
        part = dot3(inverse, split(wide_ref[:, lanes]))
        out_ref[:, lanes] = part
        pair_ref[:HALF, lanes], pair_ref[HALF:, lanes] = split(part)
        square = square + jnp.sum(part * part, axis=1, keepdims=True)
    return jnp.broadcast_to(square, (HALF, HALF)).T[:SUB, :]


def first_kernel(me_ref, mine_ref, other_ref, inverse_ref, wide_ref, out_ref, pair_ref, square_ref, gram_ref):
    me = me_ref[0]
    place(gram_ref, me, mine_ref[:, :HALF], other_ref[:, :HALF])
    place(wide_ref, me, mine_ref[:, HALF:], other_ref[:, HALF:])
    inverse_ref[...] = inverse_factor(gram_ref[...])
    square_ref[...] = solved(inverse_ref[...], wide_ref, out_ref, pair_ref)


def first_solve(me, mine, other):
    cols = mine.shape[1] - HALF
    return call(
        first_kernel, "first_solve", 5_000_000_000, 20 * HALF * cols,
        out_shape=[shaped(HALF, HALF), shaped(HALF, cols), shaped(HALF, cols), shaped(RANK, cols, dtype=BF16), shaped(SUB, HALF)],
        in_specs=[SMEM, VMEM, VMEM], out_specs=[VMEM] * 5, scratch_shapes=[pltpu.VMEM((HALF, HALF), F32)],
    )(me, mine, other)


def second_kernel(me_ref, mine_ref, other_ref, first_ref, wide0_ref, inverse_ref, out_ref, pair_ref, square_ref, gram_ref, wide_ref):
    me = me_ref[0]
    place(gram_ref, me, mine_ref[:, :RANK], other_ref[:, :RANK])
    place(wide_ref.at[HALF:, :], me, mine_ref[:, RANK:], other_ref[:, RANK:])
    wide_ref[:HALF, :] = wide0_ref[...]
    first = first_ref[...]
    side = dot(gram_ref[:, :HALF], first, NT, HIGHEST)
    second = inverse_factor(gram_ref[:, HALF:] - dot(side, side, NT, HIGHEST))
    inverse_ref[:HALF, :HALF] = first
    inverse_ref[:HALF, HALF:] = jnp.zeros((HALF, HALF), F32)
    inverse_ref[HALF:, :HALF] = -dot(second, dot(side, first, precision=HIGHEST), precision=HIGHEST)
    inverse_ref[HALF:, HALF:] = second
    square_ref[...] = solved(inverse_ref[HALF:, :], wide_ref, out_ref, pair_ref)


def second_solve(me, mine, other, first, wide0):
    cols = mine.shape[1] - RANK
    return call(
        second_kernel, "second_solve", 6_000_000_000, 20 * HALF * cols,
        out_shape=[shaped(RANK, RANK), shaped(HALF, cols), shaped(RANK, cols, dtype=BF16), shaped(SUB, HALF)],
        in_specs=[SMEM] + [VMEM] * 4, out_specs=[VMEM] * 4,
        scratch_shapes=[pltpu.VMEM((HALF, RANK), F32), pltpu.VMEM((RANK, cols), F32)],
    )(me, mine, other, first, wide0)


def momentum_kernel(left0_ref, left1_ref, inverse_ref, pair0_ref, pair1_ref, high_ref, low_ref, out_ref, ortho_ref, half_ref):
    step, width = pl.program_id(0), out_ref.shape[1]

    @pl.when(step == 0)
    def _():
        left = jnp.concatenate([left0_ref[...], left1_ref[...]], axis=1)
        ortho = dot3(split(left), split(inverse_ref[...]), NT)
        ortho_ref[...] = ortho
        half_ref[...] = ortho.astype(BF16)

    lanes = pl.ds(pl.multiple_of(step * width, width), width)
    factor = jnp.concatenate([pair0_ref[:HALF, lanes], pair1_ref[:HALF, lanes]], axis=0)
    feedback = F32(1.0 - beta_mom) * dot(half_ref[...], factor)
    out_ref[...] = (high_ref[:, lanes].astype(F32) + low_ref[:, lanes].astype(F32)) - feedback


def momentum_update(lefts, inverse, pairs, buffer):
    rows, cols = buffer[0].shape
    return call(
        momentum_kernel, "momentum", 2 * rows * cols * RANK, 4 * rows * cols,
        out_shape=[shaped(rows, cols), shaped(rows, RANK)], grid=(cols // TILE,),
        in_specs=[VMEM] * 7, out_specs=[pl.BlockSpec((rows, TILE), lambda i: (0, i)), VMEM],
        scratch_shapes=[pltpu.VMEM((rows, RANK), BF16)],
    )(*lefts, inverse, *pairs, *buffer)


def weight_kernel(ortho_ref, s0, s1, s2, s3, pair0_ref, pair1_ref, factor0_ref, factor1_ref, weight_ref, out_ref, basis_ref, high_ref, low_ref):
    total = (s0[0:1, :] + s1[0:1, :]) + (s2[0:1, :] + s3[0:1, :])
    scale = 1.0 / jnp.sqrt(total / F32(D) + F32(1e-06))
    step, width = pl.program_id(0), out_ref.shape[1]

    @pl.when(step == 0)
    def _():
        high_ref[...], low_ref[...] = split(ortho_ref[...] * (scale * F32(learn_rate * (D / RANK) ** 0.5)))

    lanes = pl.ds(pl.multiple_of(step * width, width), width)
    fhigh = jnp.concatenate([pair0_ref[:HALF, lanes], pair1_ref[:HALF, lanes]], axis=0)
    flow = jnp.concatenate([pair0_ref[HALF:, lanes], pair1_ref[HALF:, lanes]], axis=0)
    out_ref[...] = weight_ref[:, lanes] - dot3((high_ref[...], low_ref[...]), (fhigh, flow))
    basis_ref[:, :HALF] = factor0_ref[:, lanes].T * scale[:, :HALF]
    basis_ref[:, HALF:] = factor1_ref[:, lanes].T * scale[:, HALF:]


def weight_update(ortho, squares, pairs, factors, weight):
    rows, cols = weight.shape
    return call(
        weight_kernel, "weight", 6 * rows * cols * RANK, 4 * rows * cols,
        out_shape=[shaped(rows, cols), shaped(cols, RANK)], grid=(cols // TILE,), in_specs=[VMEM] * 10,
        out_specs=[pl.BlockSpec((rows, TILE), lambda i: (0, i)), pl.BlockSpec((TILE, RANK), lambda i: (i, 0))],
        scratch_shapes=[pltpu.VMEM((rows, RANK), BF16)] * 2,
    )(ortho, *squares, *pairs, *factors, weight)


def swap(x, axis, bit):
    size = lax.axis_size(axis)
    return lax.ppermute(x, axis, [(i, i ^ bit) for i in range(size)])


def together(*arrays):
    return lax.optimization_barrier(arrays)


def tuned(momentum, gradient, weight, right_basis):
    row = lax.axis_index("row")
    me = (2 * (row & 1) + ((row >> 1) & 1)).astype(jnp.int32)[None]
    high, low, up0, down0, up1, down1 = start(momentum[0], gradient[0], right_basis)
    buffer = (high, low)
    got0 = swap(up0, "col", 1), swap(down0, "col", 2)
    up0, down0, got0, up1, down1 = together(up0, down0, got0, up1, down1)
    for sweep in range(ITERS):
        last, scaled = sweep == ITERS - 1, sweep > 0

        up0, down0 = up0 + got0[0], down0 + got0[1]
        got0 = swap(up0, "col", 2), swap(down0, "col", 1)
        if sweep:
            up1, down1 = left_product(buffer, split1, square1)
        got1 = swap(up1, "col", 1), swap(down1, "col", 2)
        up0, down0, got0, up1, down1, got1 = together(up0, down0, got0, up1, down1, got1)

        up1, down1 = up1 + got1[0], down1 + got1[1]
        got1 = swap(up1, "col", 2), swap(down1, "col", 1)
        keep0, give0, left0 = product(scaled, me, (), (up0, got0[0], down0, got0[1]), buffer)
        core0 = swap(give0, "row", 1)
        up1, down1, got1, keep0, core0, left0 = together(up1, down1, got1, keep0, core0, left0)

        part0 = keep0 + core0
        pair0 = swap(part0[PART:], "row", 2)
        keep1, give1, left1 = product(scaled, me, (left0,), (up1, got1[0], down1, got1[1]), buffer)
        core1 = swap(give1, "row", 1)
        part0, pair0, keep1, core1 = together(part0, pair0, keep1, core1)

        side0 = part0[:PART] + pair0
        cross0 = swap(side0, "row", 4)
        part1 = keep1 + core1
        pair1 = swap(part1[PART:], "row", 2)
        side0, cross0, part1, pair1 = together(side0, cross0, part1, pair1)

        total0 = side0 + cross0
        back0 = swap(total0, "row", 2)
        side1 = part1[:PART] + pair1
        cross1 = swap(side1, "row", 4)
        total0, back0, side1, cross1 = together(total0, back0, side1, cross1)

        mine0 = jnp.concatenate([total0, back0], axis=0)
        other0 = swap(mine0, "row", 1)
        total1 = side1 + cross1
        back1 = swap(total1, "row", 2)
        first, wide, factor0, split0, square0 = first_solve(me, mine0, other0)
        total1, back1, first, wide, split0, square0 = together(total1, back1, first, wide, split0, square0)

        mine1 = jnp.concatenate([total1, back1], axis=0)
        other1 = swap(mine1, "row", 1)
        if not last:
            up0, down0 = left_product(buffer, split0, square0)
            got0 = swap(up0, "col", 1), swap(down0, "col", 2)
        inverse, factor1, split1, square1 = second_solve(me, mine1, other1, first, wide)
        if not last:
            up0, down0, got0, split1, square1 = together(up0, down0, got0, split1, square1)

    square = jnp.concatenate([square0, square1], axis=1)
    squares = (square, swap(square, "col", 1), swap(square, "col", 2), swap(square, "col", 3))
    new_momentum, ortho = momentum_update((left0, left1), inverse, (split0, split1), buffer)
    new_weight, new_basis = weight_update(ortho, squares, (split0, split1), (factor0, factor1), weight)
    return new_momentum[None], new_weight, new_basis


def general(momentum, gradient, weight, right_basis):
    replicas = lax.axis_size("rep")
    buffer = momentum[0] + gradient[0].astype(F32)
    basis, dims = right_basis, NN
    for sweep in range(ITERS):
        left = lax.psum(dot(buffer, basis, dims, HIGH) / replicas, ("col", "rep"))
        if sweep:
            left = left / rms
        gram = lax.psum(dot(left, left, ((0,), (0,)), HIGHEST), "row")
        wide = lax.psum(dot(left, buffer, ((0,), (0,)), HIGH) / replicas, ("row", "rep"))
        inverse = inverse_cholesky(gram)
        factor = dot(inverse, wide, precision=HIGHEST)
        rms = jnp.sqrt(lax.psum(jnp.sum(factor * factor, axis=1)[None, :], "col") / F32(D) + 1e-06)
        basis, dims = factor, NT
    ortho = dot(left, inverse, NT, HIGHEST)
    new_momentum = (buffer - (1.0 - beta_mom) * dot(ortho, factor, precision=HIGH))[None]
    basis = factor / rms.T
    new_weight = weight - learn_rate * jnp.sqrt(F32(D) / F32(RANK)) * dot(ortho, basis, precision=HIGH)
    return new_momentum, new_weight, basis.T


def solution(mesh):
    sizes = dict(mesh.shape)
    fits = sizes["row"] == 8 and sizes["col"] == 4 and sizes["rep"] == 1
    return jax.shard_map(
        tuned if fits else general,
        mesh=mesh,
        in_specs=(P("rep", "row", "col"), P("rep", "row", "col"), P("row", "col"), P("col", None)),
        out_specs=(P("rep", "row", "col"), P("row", "col"), P("col", None)),
        check_vma=False,
    )
```

```python
import functools

import jax
import jax.numpy as jnp
from jax import lax
from jax.experimental import pallas as pl
from jax.experimental.pallas import tpu as pltpu
from jax.sharding import PartitionSpec as P

D = 8192
RANK = 256
ITERS = 2
HALF = RANK // 2
QUARTER = RANK // 4
PART = RANK // 8
SUB = 8
TILE = 256
STEP = 512

beta_mom = 0.95
learn_rate = 0.05

F32 = jnp.float32
BF16 = jnp.bfloat16
HIGHEST = lax.Precision.HIGHEST
HIGH = lax.Precision.HIGH
NT = ((1,), (1,))
NN = ((1,), (0,))


def dot(a, b, dims=NN, precision=None):
    return lax.dot_general(a, b, (dims, ((), ())), precision=precision, preferred_element_type=F32)


def split(x):
    high = x.astype(BF16)
    return high, (x - high.astype(F32)).astype(BF16)


def dot3(a, b, dims=NN):
    return dot(a[0], b[0], dims) + (dot(a[1], b[0], dims) + dot(a[0], b[1], dims))


def call(kernel, name, flops, moved, **rest):
    rest.setdefault("compiler_params", pltpu.CompilerParams(vmem_limit_bytes=24 * 2**20))
    return pl.pallas_call(
        kernel,
        name=name,
        cost_estimate=pl.CostEstimate(flops=flops, bytes_accessed=moved, transcendentals=0),
        **rest,
    )


def shaped(*shape, dtype=F32):
    return jax.ShapeDtypeStruct(shape, dtype)


VMEM = pl.BlockSpec(memory_space=pltpu.VMEM)
SMEM = pl.BlockSpec(memory_space=pltpu.SMEM)


def inverse_factor(block):
    shape = (SUB, HALF)
    lanes = lax.broadcasted_iota(jnp.int32, shape, 1)
    subs = lax.broadcasted_iota(jnp.int32, shape, 0)
    count = HALF // SUB

    def spread(tile, lane):
        return jnp.broadcast_to(tile[:, lane:lane + 1], shape)

    def repeat(tile, sub):
        return jnp.broadcast_to(tile[sub:sub + 1, :], shape)

    tiles = [block[SUB * i:SUB * (i + 1), :] for i in range(count)]
    for t in range(count):
        low = SUB * t
        panel = jnp.logical_and(lanes >= low, lanes < low + SUB)
        cols = [spread(tiles[t], low + j) for j in range(SUB)]
        tile = jnp.where(panel, 0.0, tiles[t])
        scale, rows, upper = [], [], {}
        for j in range(SUB):
            r = lax.rsqrt(repeat(cols[j], j))
            mult = jnp.where(subs > j, cols[j] * r, 0.0)
            for k in range(j + 1, SUB):
                upper[j, k] = repeat(cols[k], j) * r
                cols[k] = cols[k] - mult * upper[j, k]
            row = jnp.where(lanes == low + j, r, repeat(tile, j) * r)
            tile = jnp.where(subs == j, row, tile - mult * row)
            scale.append(r)
            rows.append(row)
        tiles[t] = tile
        for i in range(t + 1, count):
            cols = [spread(tiles[i], low + j) for j in range(SUB)]
            tile = jnp.where(panel, 0.0, tiles[i])
            for j in range(SUB):
                mult = cols[j] * scale[j]
                for k in range(j + 1, SUB):
                    cols[k] = cols[k] - mult * upper[j, k]
                tile = tile - mult * rows[j]
            tiles[i] = tile
    full = jnp.concatenate(tiles, axis=0)
    down = lax.broadcasted_iota(jnp.int32, (HALF, HALF), 0)
    across = lax.broadcasted_iota(jnp.int32, (HALF, HALF), 1)
    return jnp.where(across <= down, full, 0.0)


def inverse_body(gram_ref, out_ref):
    first = inverse_factor(gram_ref[:HALF, :HALF])
    side = dot(gram_ref[HALF:, :HALF], first, NT, HIGHEST)
    rest = gram_ref[HALF:, HALF:] - dot(side, side, NT, HIGHEST)
    second = inverse_factor(rest)
    out_ref[:HALF, :HALF] = first
    out_ref[:HALF, HALF:] = jnp.zeros((HALF, HALF), F32)
    out_ref[HALF:, :HALF] = -dot(second, dot(side, first, precision=HIGHEST), precision=HIGHEST)
    out_ref[HALF:, HALF:] = second


def inverse_cholesky(gram):
    return call(
        inverse_body, "inverse_cholesky", 12_000_000_000, 2 * 4 * RANK * RANK,
        out_shape=shaped(RANK, RANK), in_specs=[VMEM], out_specs=VMEM,
    )(gram)


def place(out_ref, me, mine, other):
    for b in range(4):
        block = (mine, other)[b // 2][PART * (b % 2):PART * (b % 2 + 1), :]
        out_ref[pl.ds(pl.multiple_of((me ^ b) * PART, PART), PART), :] = block


def start_kernel(momentum_ref, gradient_ref, basis_ref, high_ref, low_ref, up0, down0, up1, down1, pair_ref):
    rows, cols = momentum_ref.shape
    count = up0.shape[0] // TILE

    def body(momentum, gradient, basis):
        step = pl.program_id(0)

        @pl.when(step == 0)
        def _():
            pair_ref[:, :RANK], pair_ref[:, RANK:] = split(basis[...])

        here = pl.ds(pl.multiple_of(step * TILE, TILE), TILE)
        high, low = split(momentum[...] + gradient[...].astype(F32))
        high_ref[here, :], low_ref[here, :] = high, low
        both = dot(high, pair_ref[...])
        part = (both[:, :RANK] + both[:, RANK:]) + dot(low, pair_ref[:, :RANK])
        there = pl.ds(pl.multiple_of(lax.rem(step, count) * TILE, TILE), TILE)

        @pl.when(step < count)
        def _():
            up0[there, :] = part[:, :HALF]
            up1[there, :] = part[:, HALF:]

        @pl.when(step >= count)
        def _():
            down0[there, :] = part[:, :HALF]
            down1[there, :] = part[:, HALF:]

    block = pl.BlockSpec((TILE, cols), lambda i: (i, 0))
    pltpu.emit_pipeline(
        body, grid=(rows // TILE,), in_specs=[block, block, pl.BlockSpec((cols, RANK), lambda i: (0, 0))],
    )(momentum_ref, gradient_ref, basis_ref)


def start(*args):
    rows, cols = args[0].shape
    high, low, *parts = call(
        start_kernel, "start", 6 * rows * cols * RANK, 6 * rows * cols,
        out_shape=[shaped(rows, cols, dtype=BF16)] * 2 + [shaped(rows // 2, HALF)] * 4,
        in_specs=[pl.BlockSpec(memory_space=pltpu.HBM)] * 3, out_specs=[VMEM] * 6,
        scratch_shapes=[pltpu.VMEM((cols, 2 * RANK), BF16)],
    )(*(pltpu.with_memory_space_constraint(x, pltpu.HBM) for x in args))
    return (*(pltpu.with_memory_space_constraint(x, pltpu.VMEM) for x in (high, low)), *parts)


def left_kernel(high_ref, low_ref, factor_ref, *refs):
    up_ref, down_ref = refs[-2:]
    half = down_ref.shape[0]

    for ref, base in ((up_ref, 0), (down_ref, half)):
        @pl.loop(0, half // TILE)
        def _(c):
            here = pl.ds(pl.multiple_of(base + c * TILE, TILE), TILE)
            both = dot(high_ref[here, :], factor_ref[...], NT)
            part = (both[:, :HALF] + both[:, HALF:]) + dot(low_ref[here, :], factor_ref[:HALF, :], NT)
            ref[pl.ds(pl.multiple_of(c * TILE, TILE), TILE), :] = part

    if len(refs) == 3:
        up_ref[half:, :] = refs[0][...]


def left_product(buffer, factor, square):
    rows, cols = buffer[0].shape
    return call(
        left_kernel, "left", 4 * rows * cols * RANK, 4 * rows * cols,
        out_shape=[shaped(rows // 2 + SUB, HALF), shaped(rows // 2, HALF)], in_specs=[VMEM] * 4, out_specs=[VMEM] * 2,
    )(*buffer, factor, square)


def product_kernel(first, scaled, me_ref, *refs):
    before, refs = ((), refs) if first else (refs[:1], refs[1:])
    up, up_more, down, down_more, high_ref, low_ref, keep_ref, give_ref, left_ref, plain_ref, turned_ref, pair_ref = refs
    rows = down.shape[0]
    top, bottom = up[:rows, :] + up_more[:rows, :], down[...] + down_more[...]
    if scaled:
        total = up[rows:rows + 1, :] + up_more[rows:rows + 1, :]
        scale = 1.0 / jnp.sqrt(total / F32(D) + F32(1e-06))
        top, bottom = top * scale, bottom * scale
    left_ref[:rows, :] = top
    left_ref[rows:, :] = bottom
    plain_ref[:, :rows] = top.T
    plain_ref[:, rows:] = bottom.T
    me = me_ref[0]
    for b in range(4):
        block = plain_ref[pl.ds(pl.multiple_of((me ^ b) * PART, PART), PART), :]
        turned_ref[PART * b:PART * (b + 1), :] = block
        pair_ref[PART * b:PART * (b + 1), :], pair_ref[HALF + PART * b:HALF + PART * (b + 1), :] = split(block)
    spot = 0
    for ref in (*before, left_ref):
        gram = dot(turned_ref[...], ref[...], precision=HIGHEST)
        keep_ref[:, spot:spot + HALF] = gram[:QUARTER]
        give_ref[:, spot:spot + HALF] = gram[QUARTER:]
        spot += HALF
    step = 2 * TILE
    for c in range(high_ref.shape[1] // step):
        lanes = pl.ds(c * step, step)
        both = dot(pair_ref[...], high_ref[:, lanes])
        part = (both[:HALF] + both[HALF:]) + dot(pair_ref[:HALF, :], low_ref[:, lanes])
        lanes = pl.ds(spot + c * step, step)
        keep_ref[:, lanes] = part[:QUARTER]
        give_ref[:, lanes] = part[QUARTER:]


def product(scaled, me, before, parts, buffer):
    rows, cols = buffer[0].shape
    width = HALF * (len(before) + 1) + cols
    return call(
        functools.partial(product_kernel, not before, scaled), "product", 4 * rows * width * RANK, 4 * rows * width,
        out_shape=[shaped(QUARTER, width)] * 2 + [shaped(rows, HALF)],
        in_specs=[SMEM] + [VMEM] * (6 + len(before)), out_specs=[VMEM] * 3,
        scratch_shapes=[pltpu.VMEM((HALF, rows), F32)] * 2 + [pltpu.VMEM((RANK, rows), BF16)],
    )(me, *before, *parts, *buffer)


def solved(inverse, wide_ref, out_ref, pair_ref):
    inverse = split(inverse)
    square = jnp.zeros((HALF, 1), F32)
    step = 2 * TILE
    for c in range(wide_ref.shape[1] // step):
        lanes = pl.ds(step * c, step)
        part = dot3(inverse, split(wide_ref[:, lanes]))
        out_ref[:, lanes] = part
        pair_ref[:HALF, lanes], pair_ref[HALF:, lanes] = split(part)
        square = square + jnp.sum(part * part, axis=1, keepdims=True)
    return jnp.broadcast_to(square, (HALF, HALF)).T[:SUB, :]


def first_kernel(me_ref, mine_ref, other_ref, inverse_ref, wide_ref, out_ref, pair_ref, square_ref, gram_ref):
    me = me_ref[0]
    place(gram_ref, me, mine_ref[:, :HALF], other_ref[:, :HALF])
    place(wide_ref, me, mine_ref[:, HALF:], other_ref[:, HALF:])
    inverse_ref[...] = inverse_factor(gram_ref[...])
    square_ref[...] = solved(inverse_ref[...], wide_ref, out_ref, pair_ref)


def first_solve(me, mine, other):
    cols = mine.shape[1] - HALF
    return call(
        first_kernel, "first_solve", 5_000_000_000, 20 * HALF * cols,
        out_shape=[shaped(HALF, HALF), shaped(HALF, cols), shaped(HALF, cols), shaped(RANK, cols, dtype=BF16), shaped(SUB, HALF)],
        in_specs=[SMEM, VMEM, VMEM], out_specs=[VMEM] * 5, scratch_shapes=[pltpu.VMEM((HALF, HALF), F32)],
    )(me, mine, other)


def second_kernel(me_ref, mine_ref, other_ref, first_ref, wide0_ref, inverse_ref, out_ref, pair_ref, square_ref, gram_ref, wide_ref):
    me = me_ref[0]
    place(gram_ref, me, mine_ref[:, :RANK], other_ref[:, :RANK])
    place(wide_ref.at[HALF:, :], me, mine_ref[:, RANK:], other_ref[:, RANK:])
    wide_ref[:HALF, :] = wide0_ref[...]
    first = first_ref[...]
    side = dot(gram_ref[:, :HALF], first, NT, HIGHEST)
    second = inverse_factor(gram_ref[:, HALF:] - dot(side, side, NT, HIGHEST))
    inverse_ref[:HALF, :HALF] = first
    inverse_ref[:HALF, HALF:] = jnp.zeros((HALF, HALF), F32)
    inverse_ref[HALF:, :HALF] = -dot(second, dot(side, first, precision=HIGHEST), precision=HIGHEST)
    inverse_ref[HALF:, HALF:] = second
    square_ref[...] = solved(inverse_ref[HALF:, :], wide_ref, out_ref, pair_ref)


def second_solve(me, mine, other, first, wide0):
    cols = mine.shape[1] - RANK
    return call(
        second_kernel, "second_solve", 6_000_000_000, 20 * HALF * cols,
        out_shape=[shaped(RANK, RANK), shaped(HALF, cols), shaped(RANK, cols, dtype=BF16), shaped(SUB, HALF)],
        in_specs=[SMEM] + [VMEM] * 4, out_specs=[VMEM] * 4,
        scratch_shapes=[pltpu.VMEM((HALF, RANK), F32), pltpu.VMEM((RANK, cols), F32)],
    )(me, mine, other, first, wide0)


def momentum_kernel(left0_ref, left1_ref, inverse_ref, pair0_ref, pair1_ref, high_ref, low_ref, out_ref, ortho_ref, half_ref):
    step, width = pl.program_id(0), out_ref.shape[1]

    @pl.when(step == 0)
    def _():
        left = jnp.concatenate([left0_ref[...], left1_ref[...]], axis=1)
        ortho = dot3(split(left), split(inverse_ref[...]), NT)
        ortho_ref[...] = ortho
        half_ref[...] = ortho.astype(BF16)

    lanes = pl.ds(pl.multiple_of(step * width, width), width)
    factor = jnp.concatenate([pair0_ref[:HALF, lanes], pair1_ref[:HALF, lanes]], axis=0)
    feedback = F32(1.0 - beta_mom) * dot(half_ref[...], factor)
    out_ref[...] = (high_ref[:, lanes].astype(F32) + low_ref[:, lanes].astype(F32)) - feedback


def momentum_update(lefts, inverse, pairs, buffer):
    rows, cols = buffer[0].shape
    return call(
        momentum_kernel, "momentum", 2 * rows * cols * RANK, 4 * rows * cols,
        out_shape=[shaped(rows, cols), shaped(rows, RANK)], grid=(cols // STEP,),
        in_specs=[VMEM] * 7, out_specs=[pl.BlockSpec((rows, STEP), lambda i: (0, i)), VMEM],
        scratch_shapes=[pltpu.VMEM((rows, RANK), BF16)],
    )(*lefts, inverse, *pairs, *buffer)


def weight_kernel(ortho_ref, s0, s1, s2, s3, pair0_ref, pair1_ref, factor0_ref, factor1_ref, weight_ref, out_ref, basis_ref, triple_ref):
    total = (s0[0:1, :] + s1[0:1, :]) + (s2[0:1, :] + s3[0:1, :])
    scale = 1.0 / jnp.sqrt(total / F32(D) + F32(1e-06))
    step, width = pl.program_id(0), out_ref.shape[1]

    @pl.when(step == 0)
    def _():
        high, low = split(ortho_ref[...] * (scale * F32(learn_rate * (D / RANK) ** 0.5)))
        triple_ref[:, :RANK] = high
        triple_ref[:, RANK:2 * RANK] = low
        triple_ref[:, 2 * RANK:] = high

    lanes = pl.ds(pl.multiple_of(step * width, width), width)
    high = [pair0_ref[:HALF, lanes], pair1_ref[:HALF, lanes]]
    factor = jnp.concatenate([*high, *high, pair0_ref[HALF:, lanes], pair1_ref[HALF:, lanes]], axis=0)
    out_ref[...] = weight_ref[:, lanes] - dot(triple_ref[...], factor)
    basis_ref[:, :HALF] = factor0_ref[:, lanes].T * scale[:, :HALF]
    basis_ref[:, HALF:] = factor1_ref[:, lanes].T * scale[:, HALF:]


def weight_update(ortho, squares, pairs, factors, weight):
    rows, cols = weight.shape
    return call(
        weight_kernel, "weight", 6 * rows * cols * RANK, 4 * rows * cols,
        out_shape=[shaped(rows, cols), shaped(cols, RANK)], grid=(cols // STEP,), in_specs=[VMEM] * 10,
        out_specs=[pl.BlockSpec((rows, STEP), lambda i: (0, i)), pl.BlockSpec((STEP, RANK), lambda i: (i, 0))],
        scratch_shapes=[pltpu.VMEM((rows, 3 * RANK), BF16)],
    )(ortho, *squares, *pairs, *factors, weight)


def swap(x, axis, bit):
    size = lax.axis_size(axis)
    return lax.ppermute(x, axis, [(i, i ^ bit) for i in range(size)])


def together(*arrays):
    return lax.optimization_barrier(arrays)


def tuned(momentum, gradient, weight, right_basis):
    row = lax.axis_index("row")
    me = (2 * (row & 1) + ((row >> 1) & 1)).astype(jnp.int32)[None]
    high, low, up0, down0, up1, down1 = start(momentum[0], gradient[0], right_basis)
    buffer = (high, low)
    got0 = swap(up0, "col", 1), swap(down0, "col", 2)
    up0, down0, got0, up1, down1 = together(up0, down0, got0, up1, down1)
    for sweep in range(ITERS):
        last, scaled = sweep == ITERS - 1, sweep > 0

        up0, down0 = up0 + got0[0], down0 + got0[1]
        got0 = swap(up0, "col", 2), swap(down0, "col", 1)
        if not sweep:
            got1 = swap(up1, "col", 1), swap(down1, "col", 2)
            up0, down0, got0, up1, down1, got1 = together(up0, down0, got0, up1, down1, got1)
            up1, down1 = up1 + got1[0], down1 + got1[1]
            got1 = swap(up1, "col", 2), swap(down1, "col", 1)
        else:
            up1, down1 = left_product(buffer, split1, square1)
            up0, down0, got0, up1, down1 = together(up0, down0, got0, up1, down1)
            got1 = swap(up1, "col", 1), swap(down1, "col", 2)
        keep0, give0, left0 = product(scaled, me, (), (up0, got0[0], down0, got0[1]), buffer)
        up1, down1, got1, keep0, give0, left0 = together(up1, down1, got1, keep0, give0, left0)

        core0 = swap(give0, "row", 1)
        if sweep:
            up1, down1 = up1 + got1[0], down1 + got1[1]
            got1 = swap(up1, "col", 2), swap(down1, "col", 1)
        up1, down1, got1, keep0, core0, left0 = together(up1, down1, got1, keep0, core0, left0)

        part0 = keep0 + core0
        pair0 = swap(part0[PART:], "row", 2)
        keep1, give1, left1 = product(scaled, me, (left0,), (up1, got1[0], down1, got1[1]), buffer)
        part0, pair0, keep1, give1 = together(part0, pair0, keep1, give1)

        side0 = part0[:PART] + pair0
        cross0 = swap(side0, "row", 4)
        part1 = keep1 + swap(give1, "row", 1)
        pair1 = swap(part1[PART:], "row", 2)
        side0, cross0, part1, pair1 = together(side0, cross0, part1, pair1)

        total0 = side0 + cross0
        back0 = swap(total0, "row", 2)
        side1 = part1[:PART] + pair1
        cross1 = swap(side1, "row", 4)
        total0, back0, side1, cross1 = together(total0, back0, side1, cross1)

        mine0 = jnp.concatenate([total0, back0], axis=0)
        other0 = swap(mine0, "row", 1)
        total1 = side1 + cross1
        back1 = swap(total1, "row", 2)
        first, wide, factor0, split0, square0 = first_solve(me, mine0, other0)
        total1, back1, first, wide, split0, square0 = together(total1, back1, first, wide, split0, square0)

        mine1 = jnp.concatenate([total1, back1], axis=0)
        other1 = swap(mine1, "row", 1)
        if not last:
            up0, down0 = left_product(buffer, split0, square0)
            got0 = swap(up0, "col", 1), swap(down0, "col", 2)
        inverse, factor1, split1, square1 = second_solve(me, mine1, other1, first, wide)
        if not last:
            up0, down0, got0, split1, square1 = together(up0, down0, got0, split1, square1)

    square = jnp.concatenate([square0, square1], axis=1)
    squares = (square, swap(square, "col", 1), swap(square, "col", 2), swap(square, "col", 3))
    new_momentum, ortho = momentum_update((left0, left1), inverse, (split0, split1), buffer)
    new_weight, new_basis = weight_update(ortho, squares, (split0, split1), (factor0, factor1), weight)
    return new_momentum[None], new_weight, new_basis


def general(momentum, gradient, weight, right_basis):
    replicas = lax.axis_size("rep")
    buffer = momentum[0] + gradient[0].astype(F32)
    basis, dims = right_basis, NN
    for sweep in range(ITERS):
        left = lax.psum(dot(buffer, basis, dims, HIGH) / replicas, ("col", "rep"))
        if sweep:
            left = left / rms
        gram = lax.psum(dot(left, left, ((0,), (0,)), HIGHEST), "row")
        wide = lax.psum(dot(left, buffer, ((0,), (0,)), HIGH) / replicas, ("row", "rep"))
        inverse = inverse_cholesky(gram)
        factor = dot(inverse, wide, precision=HIGHEST)
        rms = jnp.sqrt(lax.psum(jnp.sum(factor * factor, axis=1)[None, :], "col") / F32(D) + 1e-06)
        basis, dims = factor, NT
    ortho = dot(left, inverse, NT, HIGHEST)
    new_momentum = (buffer - (1.0 - beta_mom) * dot(ortho, factor, precision=HIGH))[None]
    basis = factor / rms.T
    new_weight = weight - learn_rate * jnp.sqrt(F32(D) / F32(RANK)) * dot(ortho, basis, precision=HIGH)
    return new_momentum, new_weight, basis.T


def solution(mesh):
    sizes = dict(mesh.shape)
    fits = sizes["row"] == 8 and sizes["col"] == 4 and sizes["rep"] == 1
    return jax.shard_map(
        tuned if fits else general,
        mesh=mesh,
        in_specs=(P("rep", "row", "col"), P("rep", "row", "col"), P("row", "col"), P("col", None)),
        out_specs=(P("rep", "row", "col"), P("row", "col"), P("col", None)),
        check_vma=False,
    )
```

```python
import functools

import jax
import jax.numpy as jnp
from jax import lax
from jax.experimental import pallas as pl
from jax.experimental.pallas import tpu as pltpu
from jax.sharding import PartitionSpec as P

D = 8192
RANK = 256
ITERS = 2
HALF = RANK // 2
QUARTER = RANK // 4
PART = RANK // 8
SUB = 8
TILE = 256
STEP = 512

beta_mom = 0.95
learn_rate = 0.05

F32 = jnp.float32
BF16 = jnp.bfloat16
HIGHEST = lax.Precision.HIGHEST
HIGH = lax.Precision.HIGH
NT = ((1,), (1,))
NN = ((1,), (0,))


def dot(a, b, dims=NN, precision=None):
    return lax.dot_general(a, b, (dims, ((), ())), precision=precision, preferred_element_type=F32)


def split(x):
    high = x.astype(BF16)
    return high, (x - high.astype(F32)).astype(BF16)


def dot3(a, b, dims=NN):
    return dot(a[0], b[0], dims) + (dot(a[1], b[0], dims) + dot(a[0], b[1], dims))


def call(kernel, name, flops, moved, **rest):
    rest.setdefault("compiler_params", pltpu.CompilerParams(vmem_limit_bytes=24 * 2**20))
    return pl.pallas_call(
        kernel,
        name=name,
        cost_estimate=pl.CostEstimate(flops=flops, bytes_accessed=moved, transcendentals=0),
        **rest,
    )


def shaped(*shape, dtype=F32):
    return jax.ShapeDtypeStruct(shape, dtype)


VMEM = pl.BlockSpec(memory_space=pltpu.VMEM)
HBM = pl.BlockSpec(memory_space=pltpu.HBM)
SMEM = pl.BlockSpec(memory_space=pltpu.SMEM)


def inverse_factor(block):
    shape = (SUB, HALF)
    lanes = lax.broadcasted_iota(jnp.int32, shape, 1)
    subs = lax.broadcasted_iota(jnp.int32, shape, 0)
    count = HALF // SUB

    def spread(tile, lane):
        return jnp.broadcast_to(tile[:, lane:lane + 1], shape)

    def repeat(tile, sub):
        return jnp.broadcast_to(tile[sub:sub + 1, :], shape)

    tiles = [block[SUB * i:SUB * (i + 1), :] for i in range(count)]
    for t in range(count):
        low = SUB * t
        panel = jnp.logical_and(lanes >= low, lanes < low + SUB)
        cols = [spread(tiles[t], low + j) for j in range(SUB)]
        tile = jnp.where(panel, 0.0, tiles[t])
        scale, rows, upper = [], [], {}
        for j in range(SUB):
            r = lax.rsqrt(repeat(cols[j], j))
            mult = jnp.where(subs > j, cols[j] * r, 0.0)
            for k in range(j + 1, SUB):
                upper[j, k] = repeat(cols[k], j) * r
                cols[k] = cols[k] - mult * upper[j, k]
            row = jnp.where(lanes == low + j, r, repeat(tile, j) * r)
            tile = jnp.where(subs == j, row, tile - mult * row)
            scale.append(r)
            rows.append(row)
        tiles[t] = tile
        for i in range(t + 1, count):
            cols = [spread(tiles[i], low + j) for j in range(SUB)]
            tile = jnp.where(panel, 0.0, tiles[i])
            for j in range(SUB):
                mult = cols[j] * scale[j]
                for k in range(j + 1, SUB):
                    cols[k] = cols[k] - mult * upper[j, k]
                tile = tile - mult * rows[j]
            tiles[i] = tile
    full = jnp.concatenate(tiles, axis=0)
    down = lax.broadcasted_iota(jnp.int32, (HALF, HALF), 0)
    across = lax.broadcasted_iota(jnp.int32, (HALF, HALF), 1)
    return jnp.where(across <= down, full, 0.0)


def inverse_body(gram_ref, out_ref):
    first = inverse_factor(gram_ref[:HALF, :HALF])
    side = dot(gram_ref[HALF:, :HALF], first, NT, HIGHEST)
    rest = gram_ref[HALF:, HALF:] - dot(side, side, NT, HIGHEST)
    second = inverse_factor(rest)
    out_ref[:HALF, :HALF] = first
    out_ref[:HALF, HALF:] = jnp.zeros((HALF, HALF), F32)
    out_ref[HALF:, :HALF] = -dot(second, dot(side, first, precision=HIGHEST), precision=HIGHEST)
    out_ref[HALF:, HALF:] = second


def inverse_cholesky(gram):
    return call(
        inverse_body, "inverse_cholesky", 12_000_000_000, 2 * 4 * RANK * RANK,
        out_shape=shaped(RANK, RANK), in_specs=[VMEM], out_specs=VMEM,
    )(gram)


def place(out_ref, me, mine, other):
    for b in range(4):
        block = (mine, other)[b // 2][PART * (b % 2):PART * (b % 2 + 1), :]
        out_ref[pl.ds(pl.multiple_of((me ^ b) * PART, PART), PART), :] = block


def start_kernel(momentum_ref, gradient_ref, basis_ref, high_ref, low_ref, up0, down0, up1, down1, pair_ref):
    rows, cols = momentum_ref.shape
    count = up0.shape[0] // TILE

    def body(momentum, gradient, basis, high_out, low_out):
        step = pl.program_id(0)

        @pl.when(step == 0)
        def _():
            pair_ref[:, :RANK], pair_ref[:, RANK:] = split(basis[...])

        high, low = split(momentum[...] + gradient[...].astype(F32))
        high_out[...], low_out[...] = high, low
        both = dot(high, pair_ref[...])
        part = (both[:, :RANK] + both[:, RANK:]) + dot(low, pair_ref[:, :RANK])
        there = pl.ds(pl.multiple_of(lax.rem(step, count) * TILE, TILE), TILE)

        @pl.when(step < count)
        def _():
            up0[there, :] = part[:, :HALF]
            up1[there, :] = part[:, HALF:]

        @pl.when(step >= count)
        def _():
            down0[there, :] = part[:, :HALF]
            down1[there, :] = part[:, HALF:]

    block = pl.BlockSpec((TILE, cols), lambda i: (i, 0))
    pltpu.emit_pipeline(
        body, grid=(rows // TILE,), in_specs=[block, block, pl.BlockSpec((cols, RANK), lambda i: (0, 0))], out_specs=[block] * 2,
    )(momentum_ref, gradient_ref, basis_ref, high_ref, low_ref)


def in_hbm(*arrays):
    return tuple(pltpu.with_memory_space_constraint(x, pltpu.HBM) for x in arrays)


def start(*args):
    rows, cols = args[0].shape
    high, low, *parts = call(
        start_kernel, "start", 6 * rows * cols * RANK, 10 * rows * cols,
        out_shape=[pltpu.HBM((rows, cols), BF16)] * 2 + [shaped(rows // 2, HALF)] * 4,
        in_specs=[HBM] * 3, out_specs=[HBM] * 2 + [VMEM] * 4,
        scratch_shapes=[pltpu.VMEM((cols, 2 * RANK), BF16)],
    )(*in_hbm(*args))
    return high, low, *parts


def left_kernel(high_ref, low_ref, factor_ref, *refs):
    up_ref, down_ref = refs[-2:]
    half = down_ref.shape[0]

    for ref, base in ((up_ref, 0), (down_ref, half)):
        @pl.loop(0, half // TILE)
        def _(c):
            here = pl.ds(pl.multiple_of(base + c * TILE, TILE), TILE)
            both = dot(high_ref[here, :], factor_ref[...], NT)
            part = (both[:, :HALF] + both[:, HALF:]) + dot(low_ref[here, :], factor_ref[:HALF, :], NT)
            ref[pl.ds(pl.multiple_of(c * TILE, TILE), TILE), :] = part

    if len(refs) == 3:
        up_ref[half:, :] = refs[0][...]


def left_product(buffer, factor, square):
    rows, cols = buffer[0].shape
    return call(
        left_kernel, "left", 4 * rows * cols * RANK, 4 * rows * cols,
        out_shape=[shaped(rows // 2 + SUB, HALF), shaped(rows // 2, HALF)], in_specs=[VMEM] * 4, out_specs=[VMEM] * 2,
    )(*buffer, factor, square)


def product_kernel(first, scaled, me_ref, *refs):
    before, refs = ((), refs) if first else (refs[:1], refs[1:])
    up, up_more, down, down_more, high_ref, low_ref, keep_ref, give_ref, left_ref, plain_ref, turned_ref, pair_ref = refs
    rows = down.shape[0]
    top, bottom = up[:rows, :] + up_more[:rows, :], down[...] + down_more[...]
    if scaled:
        total = up[rows:rows + 1, :] + up_more[rows:rows + 1, :]
        scale = 1.0 / jnp.sqrt(total / F32(D) + F32(1e-06))
        top, bottom = top * scale, bottom * scale
    left_ref[:rows, :] = top
    left_ref[rows:, :] = bottom
    plain_ref[:, :rows] = top.T
    plain_ref[:, rows:] = bottom.T
    me = me_ref[0]
    for b in range(4):
        block = plain_ref[pl.ds(pl.multiple_of((me ^ b) * PART, PART), PART), :]
        turned_ref[PART * b:PART * (b + 1), :] = block
        pair_ref[PART * b:PART * (b + 1), :], pair_ref[HALF + PART * b:HALF + PART * (b + 1), :] = split(block)
    spot = 0
    for ref in (*before, left_ref):
        gram = dot(turned_ref[...], ref[...], precision=HIGHEST)
        keep_ref[:, spot:spot + HALF] = gram[:QUARTER]
        give_ref[:, spot:spot + HALF] = gram[QUARTER:]
        spot += HALF
    cols = high_ref.shape[1]

    def multiply(c, high, low):
        both = dot(pair_ref[...], high)
        part = (both[:HALF] + both[HALF:]) + dot(pair_ref[:HALF, :], low)
        lanes = pl.ds(spot + c * STEP, STEP)
        keep_ref[:, lanes] = part[:QUARTER]
        give_ref[:, lanes] = part[QUARTER:]

    if scaled:
        for c in range(cols // STEP):
            lanes = pl.ds(c * STEP, STEP)
            multiply(c, high_ref[:, lanes], low_ref[:, lanes])
    else:
        block = pl.BlockSpec((2 * rows, STEP), lambda i: (0, i))

        def body(high, low):
            step = pl.program_id(0)
            for c in range(cols // STEP):
                @pl.when(step == c)
                def _():
                    multiply(c, high[...], low[...])

        pltpu.emit_pipeline(body, grid=(cols // STEP,), in_specs=[block] * 2)(high_ref, low_ref)


def product(scaled, me, before, parts, buffer):
    rows, cols = buffer[0].shape
    width = HALF * (len(before) + 1) + cols
    return call(
        functools.partial(product_kernel, not before, scaled), "product", 4 * rows * width * RANK, 4 * rows * width,
        out_shape=[shaped(QUARTER, width)] * 2 + [shaped(rows, HALF)],
        in_specs=[SMEM] + [VMEM] * (4 + len(before)) + [VMEM if scaled else HBM] * 2, out_specs=[VMEM] * 3,
        scratch_shapes=[pltpu.VMEM((HALF, rows), F32)] * 2 + [pltpu.VMEM((RANK, rows), BF16)],
    )(me, *before, *parts, *(buffer if scaled else in_hbm(*buffer)))


def solved(inverse, wide_ref, out_ref, pair_ref):
    inverse = split(inverse)
    square = jnp.zeros((HALF, 1), F32)
    step = 2 * TILE
    for c in range(wide_ref.shape[1] // step):
        lanes = pl.ds(step * c, step)
        part = dot3(inverse, split(wide_ref[:, lanes]))
        out_ref[:, lanes] = part
        pair_ref[:HALF, lanes], pair_ref[HALF:, lanes] = split(part)
        square = square + jnp.sum(part * part, axis=1, keepdims=True)
    return jnp.broadcast_to(square, (HALF, HALF)).T[:SUB, :]


def first_kernel(me_ref, mine_ref, other_ref, inverse_ref, wide_ref, out_ref, pair_ref, square_ref, gram_ref):
    me = me_ref[0]
    place(gram_ref, me, mine_ref[:, :HALF], other_ref[:, :HALF])
    place(wide_ref, me, mine_ref[:, HALF:], other_ref[:, HALF:])
    inverse_ref[...] = inverse_factor(gram_ref[...])
    square_ref[...] = solved(inverse_ref[...], wide_ref, out_ref, pair_ref)


def first_solve(me, mine, other):
    cols = mine.shape[1] - HALF
    return call(
        first_kernel, "first_solve", 5_000_000_000, 20 * HALF * cols,
        out_shape=[shaped(HALF, HALF), shaped(HALF, cols), shaped(HALF, cols), shaped(RANK, cols, dtype=BF16), shaped(SUB, HALF)],
        in_specs=[SMEM, VMEM, VMEM], out_specs=[VMEM] * 5, scratch_shapes=[pltpu.VMEM((HALF, HALF), F32)],
    )(me, mine, other)


def second_kernel(me_ref, mine_ref, other_ref, first_ref, wide0_ref, inverse_ref, out_ref, pair_ref, square_ref, gram_ref, wide_ref):
    me = me_ref[0]
    place(gram_ref, me, mine_ref[:, :RANK], other_ref[:, :RANK])
    place(wide_ref.at[HALF:, :], me, mine_ref[:, RANK:], other_ref[:, RANK:])
    wide_ref[:HALF, :] = wide0_ref[...]
    first = first_ref[...]
    side = dot(gram_ref[:, :HALF], first, NT, HIGHEST)
    second = inverse_factor(gram_ref[:, HALF:] - dot(side, side, NT, HIGHEST))
    inverse_ref[:HALF, :HALF] = first
    inverse_ref[:HALF, HALF:] = jnp.zeros((HALF, HALF), F32)
    inverse_ref[HALF:, :HALF] = -dot(second, dot(side, first, precision=HIGHEST), precision=HIGHEST)
    inverse_ref[HALF:, HALF:] = second
    square_ref[...] = solved(inverse_ref[HALF:, :], wide_ref, out_ref, pair_ref)


def second_solve(me, mine, other, first, wide0):
    cols = mine.shape[1] - RANK
    return call(
        second_kernel, "second_solve", 6_000_000_000, 20 * HALF * cols,
        out_shape=[shaped(RANK, RANK), shaped(HALF, cols), shaped(RANK, cols, dtype=BF16), shaped(SUB, HALF)],
        in_specs=[SMEM] + [VMEM] * 4, out_specs=[VMEM] * 4,
        scratch_shapes=[pltpu.VMEM((HALF, RANK), F32), pltpu.VMEM((RANK, cols), F32)],
    )(me, mine, other, first, wide0)


def momentum_kernel(left0_ref, left1_ref, inverse_ref, pair0_ref, pair1_ref, high_ref, low_ref, out_ref, ortho_ref, half_ref):
    step, width = pl.program_id(0), out_ref.shape[1]

    @pl.when(step == 0)
    def _():
        left = jnp.concatenate([left0_ref[...], left1_ref[...]], axis=1)
        ortho = dot3(split(left), split(inverse_ref[...]), NT)
        ortho_ref[...] = ortho
        half_ref[...] = ortho.astype(BF16)

    lanes = pl.ds(pl.multiple_of(step * width, width), width)
    factor = jnp.concatenate([pair0_ref[:HALF, lanes], pair1_ref[:HALF, lanes]], axis=0)
    feedback = F32(1.0 - beta_mom) * dot(half_ref[...], factor)
    out_ref[...] = (high_ref[:, lanes].astype(F32) + low_ref[:, lanes].astype(F32)) - feedback


def momentum_update(lefts, inverse, pairs, buffer):
    rows, cols = buffer[0].shape
    return call(
        momentum_kernel, "momentum", 2 * rows * cols * RANK, 4 * rows * cols,
        out_shape=[shaped(rows, cols), shaped(rows, RANK)], grid=(cols // STEP,),
        in_specs=[VMEM] * 7, out_specs=[pl.BlockSpec((rows, STEP), lambda i: (0, i)), VMEM],
        scratch_shapes=[pltpu.VMEM((rows, RANK), BF16)],
    )(*lefts, inverse, *pairs, *buffer)


def weight_kernel(ortho_ref, s0, s1, s2, s3, pair0_ref, pair1_ref, factor0_ref, factor1_ref, weight_ref, out_ref, basis_ref, triple_ref):
    total = (s0[0:1, :] + s1[0:1, :]) + (s2[0:1, :] + s3[0:1, :])
    scale = 1.0 / jnp.sqrt(total / F32(D) + F32(1e-06))
    step, width = pl.program_id(0), out_ref.shape[1]

    @pl.when(step == 0)
    def _():
        high, low = split(ortho_ref[...] * (scale * F32(learn_rate * (D / RANK) ** 0.5)))
        triple_ref[:, :RANK] = high
        triple_ref[:, RANK:2 * RANK] = low
        triple_ref[:, 2 * RANK:] = high

    lanes = pl.ds(pl.multiple_of(step * width, width), width)
    high = [pair0_ref[:HALF, lanes], pair1_ref[:HALF, lanes]]
    factor = jnp.concatenate([*high, *high, pair0_ref[HALF:, lanes], pair1_ref[HALF:, lanes]], axis=0)
    out_ref[...] = weight_ref[:, lanes] - dot(triple_ref[...], factor)
    basis_ref[:, :HALF] = factor0_ref[:, lanes].T * scale[:, :HALF]
    basis_ref[:, HALF:] = factor1_ref[:, lanes].T * scale[:, HALF:]


def weight_update(ortho, squares, pairs, factors, weight):
    rows, cols = weight.shape
    return call(
        weight_kernel, "weight", 6 * rows * cols * RANK, 4 * rows * cols,
        out_shape=[shaped(rows, cols), shaped(cols, RANK)], grid=(cols // STEP,), in_specs=[VMEM] * 10,
        out_specs=[pl.BlockSpec((rows, STEP), lambda i: (0, i)), pl.BlockSpec((STEP, RANK), lambda i: (i, 0))],
        scratch_shapes=[pltpu.VMEM((rows, 3 * RANK), BF16)],
    )(ortho, *squares, *pairs, *factors, weight)


def swap(x, axis, bit):
    size = lax.axis_size(axis)
    return lax.ppermute(x, axis, [(i, i ^ bit) for i in range(size)])


def together(*arrays):
    return lax.optimization_barrier(arrays)


def tuned(momentum, gradient, weight, right_basis):
    row = lax.axis_index("row")
    me = (2 * (row & 1) + ((row >> 1) & 1)).astype(jnp.int32)[None]
    high, low, up0, down0, up1, down1 = start(momentum[0], gradient[0], right_basis)
    buffer = (high, low)
    got0 = swap(up0, "col", 1), swap(down0, "col", 2)
    up0, down0, got0, up1, down1 = together(up0, down0, got0, up1, down1)
    for sweep in range(ITERS):
        last, scaled = sweep == ITERS - 1, sweep > 0

        up0, down0 = up0 + got0[0], down0 + got0[1]
        got0 = swap(up0, "col", 2), swap(down0, "col", 1)
        if sweep:
            up1, down1 = left_product(buffer, split1, square1)
        up0, down0, got0, up1, down1 = together(up0, down0, got0, up1, down1)

        keep0, give0, left0 = product(scaled, me, (), (up0, got0[0], down0, got0[1]), buffer)
        got1 = swap(up1, "col", 1), swap(down1, "col", 2)
        keep0, give0, left0, up1, down1, got1 = together(keep0, give0, left0, up1, down1, got1)

        part0 = keep0 + swap(give0, "row", 1)
        pair0 = swap(part0[PART:], "row", 2)
        up1, down1 = up1 + got1[0], down1 + got1[1]
        got1 = swap(up1, "col", 2), swap(down1, "col", 1)
        part0, pair0, up1, down1, got1, left0 = together(part0, pair0, up1, down1, got1, left0)

        side0 = part0[:PART] + pair0
        cross0 = swap(side0, "row", 4)
        keep1, give1, left1 = product(scaled, me, (left0,), (up1, got1[0], down1, got1[1]), buffer)
        part1 = keep1 + swap(give1, "row", 1)
        pair1 = swap(part1[PART:], "row", 2)
        side0, cross0, part1, pair1 = together(side0, cross0, part1, pair1)

        total0 = side0 + cross0
        back0 = swap(total0, "row", 2)
        side1 = part1[:PART] + pair1
        cross1 = swap(side1, "row", 4)
        total0, back0, side1, cross1 = together(total0, back0, side1, cross1)

        mine0 = jnp.concatenate([total0, back0], axis=0)
        other0 = swap(mine0, "row", 1)
        total1 = side1 + cross1
        back1 = swap(total1, "row", 2)
        first, wide, factor0, split0, square0 = first_solve(me, mine0, other0)
        total1, back1, first, wide, split0, square0 = together(total1, back1, first, wide, split0, square0)

        mine1 = jnp.concatenate([total1, back1], axis=0)
        other1 = swap(mine1, "row", 1)
        if not last:
            up0, down0 = left_product(buffer, split0, square0)
            got0 = swap(up0, "col", 1), swap(down0, "col", 2)
        inverse, factor1, split1, square1 = second_solve(me, mine1, other1, first, wide)
        if not last:
            up0, down0, got0, split1, square1 = together(up0, down0, got0, split1, square1)

    square = jnp.concatenate([square0, square1], axis=1)
    squares = (square, swap(square, "col", 1), swap(square, "col", 2), swap(square, "col", 3))
    new_momentum, ortho = momentum_update((left0, left1), inverse, (split0, split1), buffer)
    new_weight, new_basis = weight_update(ortho, squares, (split0, split1), (factor0, factor1), weight)
    return new_momentum[None], new_weight, new_basis


def general(momentum, gradient, weight, right_basis):
    replicas = lax.axis_size("rep")
    buffer = momentum[0] + gradient[0].astype(F32)
    basis, dims = right_basis, NN
    for sweep in range(ITERS):
        left = lax.psum(dot(buffer, basis, dims, HIGH) / replicas, ("col", "rep"))
        if sweep:
            left = left / rms
        gram = lax.psum(dot(left, left, ((0,), (0,)), HIGHEST), "row")
        wide = lax.psum(dot(left, buffer, ((0,), (0,)), HIGH) / replicas, ("row", "rep"))
        inverse = inverse_cholesky(gram)
        factor = dot(inverse, wide, precision=HIGHEST)
        rms = jnp.sqrt(lax.psum(jnp.sum(factor * factor, axis=1)[None, :], "col") / F32(D) + 1e-06)
        basis, dims = factor, NT
    ortho = dot(left, inverse, NT, HIGHEST)
    new_momentum = (buffer - (1.0 - beta_mom) * dot(ortho, factor, precision=HIGH))[None]
    basis = factor / rms.T
    new_weight = weight - learn_rate * jnp.sqrt(F32(D) / F32(RANK)) * dot(ortho, basis, precision=HIGH)
    return new_momentum, new_weight, basis.T


def solution(mesh):
    sizes = dict(mesh.shape)
    fits = sizes["row"] == 8 and sizes["col"] == 4 and sizes["rep"] == 1
    return jax.shard_map(
        tuned if fits else general,
        mesh=mesh,
        in_specs=(P("rep", "row", "col"), P("rep", "row", "col"), P("row", "col"), P("col", None)),
        out_specs=(P("rep", "row", "col"), P("row", "col"), P("col", None)),
        check_vma=False,
    )
```

```python
import functools

import jax
import jax.numpy as jnp
from jax import lax
from jax.experimental import pallas as pl
from jax.experimental.pallas import tpu as pltpu
from jax.sharding import PartitionSpec as P

D = 8192
RANK = 256
ITERS = 2
HALF = RANK // 2
QUARTER = RANK // 4
PART = RANK // 8
SUB = 8
TILE = 256
STEP = 512

beta_mom = 0.95
learn_rate = 0.05

F32 = jnp.float32
BF16 = jnp.bfloat16
HIGHEST = lax.Precision.HIGHEST
HIGH = lax.Precision.HIGH
NT = ((1,), (1,))
NN = ((1,), (0,))


def dot(a, b, dims=NN, precision=None):
    return lax.dot_general(a, b, (dims, ((), ())), precision=precision, preferred_element_type=F32)


def split(x):
    high = x.astype(BF16)
    return high, (x - high.astype(F32)).astype(BF16)


def dot3(a, b, dims=NN):
    return dot(a[0], b[0], dims) + (dot(a[1], b[0], dims) + dot(a[0], b[1], dims))


def call(kernel, name, flops, moved, **rest):
    rest.setdefault("compiler_params", pltpu.CompilerParams(vmem_limit_bytes=24 * 2**20))
    return pl.pallas_call(
        kernel,
        name=name,
        cost_estimate=pl.CostEstimate(flops=flops, bytes_accessed=moved, transcendentals=0),
        **rest,
    )


def shaped(*shape, dtype=F32):
    return jax.ShapeDtypeStruct(shape, dtype)


VMEM = pl.BlockSpec(memory_space=pltpu.VMEM)
HBM = pl.BlockSpec(memory_space=pltpu.HBM)
SMEM = pl.BlockSpec(memory_space=pltpu.SMEM)


def inverse_factor(block):
    shape = (SUB, HALF)
    lanes = lax.broadcasted_iota(jnp.int32, shape, 1)
    subs = lax.broadcasted_iota(jnp.int32, shape, 0)
    count = HALF // SUB

    def spread(tile, lane):
        return jnp.broadcast_to(tile[:, lane:lane + 1], shape)

    def repeat(tile, sub):
        return jnp.broadcast_to(tile[sub:sub + 1, :], shape)

    tiles = [block[SUB * i:SUB * (i + 1), :] for i in range(count)]
    for t in range(count):
        low = SUB * t
        panel = jnp.logical_and(lanes >= low, lanes < low + SUB)
        cols = [spread(tiles[t], low + j) for j in range(SUB)]
        tile = jnp.where(panel, 0.0, tiles[t])
        scale, rows, upper = [], [], {}
        for j in range(SUB):
            r = lax.rsqrt(repeat(cols[j], j))
            mult = jnp.where(subs > j, cols[j] * r, 0.0)
            for k in range(j + 1, SUB):
                upper[j, k] = repeat(cols[k], j) * r
                cols[k] = cols[k] - mult * upper[j, k]
            row = jnp.where(lanes == low + j, r, repeat(tile, j) * r)
            tile = jnp.where(subs == j, row, tile - mult * row)
            scale.append(r)
            rows.append(row)
        tiles[t] = tile
        for i in range(t + 1, count):
            cols = [spread(tiles[i], low + j) for j in range(SUB)]
            tile = jnp.where(panel, 0.0, tiles[i])
            for j in range(SUB):
                mult = cols[j] * scale[j]
                for k in range(j + 1, SUB):
                    cols[k] = cols[k] - mult * upper[j, k]
                tile = tile - mult * rows[j]
            tiles[i] = tile
    full = jnp.concatenate(tiles, axis=0)
    down = lax.broadcasted_iota(jnp.int32, (HALF, HALF), 0)
    across = lax.broadcasted_iota(jnp.int32, (HALF, HALF), 1)
    return jnp.where(across <= down, full, 0.0)


def inverse_body(gram_ref, out_ref):
    first = inverse_factor(gram_ref[:HALF, :HALF])
    side = dot(gram_ref[HALF:, :HALF], first, NT, HIGHEST)
    rest = gram_ref[HALF:, HALF:] - dot(side, side, NT, HIGHEST)
    second = inverse_factor(rest)
    out_ref[:HALF, :HALF] = first
    out_ref[:HALF, HALF:] = jnp.zeros((HALF, HALF), F32)
    out_ref[HALF:, :HALF] = -dot(second, dot(side, first, precision=HIGHEST), precision=HIGHEST)
    out_ref[HALF:, HALF:] = second


def inverse_cholesky(gram):
    return call(
        inverse_body, "inverse_cholesky", 12_000_000_000, 2 * 4 * RANK * RANK,
        out_shape=shaped(RANK, RANK), in_specs=[VMEM], out_specs=VMEM,
    )(gram)


def place(out_ref, me, mine, other):
    for b in range(4):
        block = (mine, other)[b // 2][PART * (b % 2):PART * (b % 2 + 1), :]
        out_ref[pl.ds(pl.multiple_of((me ^ b) * PART, PART), PART), :] = block


def start_kernel(me_ref, momentum_ref, gradient_ref, basis_ref, high_ref, low_ref, up0, down0, up1, down1, pair_ref):
    rows, cols = momentum_ref.shape
    count = up0.shape[0] // TILE

    def body(momentum, gradient, basis):
        step = pl.program_id(0)

        @pl.when(step == 0)
        def _():
            pair_ref[:, :RANK], pair_ref[:, RANK:] = split(basis[...])

        here = pl.ds(pl.multiple_of(step * TILE, TILE), TILE)
        high, low = split(momentum[...] + gradient[...].astype(F32))
        high_ref[here, :], low_ref[here, :] = high, low
        both = dot(high, pair_ref[...])
        part = (both[:, :RANK] + both[:, RANK:]) + dot(low, pair_ref[:, :RANK])
        there = pl.ds(pl.multiple_of(lax.rem(step, count) * TILE, TILE), TILE)

        @pl.when(step < count)
        def _():
            up0[there, :] = part[:, :HALF]
            up1[there, :] = part[:, HALF:]

        @pl.when(step >= count)
        def _():
            down0[there, :] = part[:, :HALF]
            down1[there, :] = part[:, HALF:]

    block = pl.BlockSpec((TILE, cols), lambda i: (i, 0))
    pltpu.emit_pipeline(
        body, grid=(rows // TILE,), in_specs=[block, block, pl.BlockSpec((cols, RANK), lambda i: (0, 0))],
    )(momentum_ref, gradient_ref, basis_ref)


def start(me, *args):
    rows, cols = args[0].shape
    return call(
        start_kernel, "start", 6 * rows * cols * RANK, 6 * rows * cols,
        out_shape=[pltpu.VMEM((rows, cols), BF16)] * 2 + [shaped(rows // 2, HALF)] * 4,
        in_specs=[SMEM] + [HBM] * 3, out_specs=[VMEM] * 6,
        scratch_shapes=[pltpu.VMEM((cols, 2 * RANK), BF16)],
    )(me, *(pltpu.with_memory_space_constraint(x, pltpu.HBM) for x in args))


def left_kernel(high_ref, low_ref, factor_ref, *refs):
    up_ref, down_ref = refs[-2:]
    half = down_ref.shape[0]

    for ref, base in ((up_ref, 0), (down_ref, half)):
        @pl.loop(0, half // TILE)
        def _(c):
            here = pl.ds(pl.multiple_of(base + c * TILE, TILE), TILE)
            both = dot(high_ref[here, :], factor_ref[...], NT)
            part = (both[:, :HALF] + both[:, HALF:]) + dot(low_ref[here, :], factor_ref[:HALF, :], NT)
            ref[pl.ds(pl.multiple_of(c * TILE, TILE), TILE), :] = part

    if len(refs) == 3:
        up_ref[half:, :] = refs[0][...]


def left_product(buffer, factor, square):
    rows, cols = buffer[0].shape
    return call(
        left_kernel, "left", 4 * rows * cols * RANK, 4 * rows * cols,
        out_shape=[shaped(rows // 2 + SUB, HALF), shaped(rows // 2, HALF)], in_specs=[VMEM] * 4, out_specs=[VMEM] * 2,
    )(*buffer, factor, square)


def product_kernel(first, scaled, me_ref, *refs):
    before, refs = ((), refs) if first else (refs[:1], refs[1:])
    up, up_more, down, down_more, high_ref, low_ref, keep_ref, give_ref, left_ref, plain_ref, turned_ref, pair_ref = refs
    rows = down.shape[0]
    top, bottom = up[:rows, :] + up_more[:rows, :], down[...] + down_more[...]
    if scaled:
        total = up[rows:rows + 1, :] + up_more[rows:rows + 1, :]
        scale = 1.0 / jnp.sqrt(total / F32(D) + F32(1e-06))
        top, bottom = top * scale, bottom * scale
    left_ref[:rows, :] = top
    left_ref[rows:, :] = bottom
    plain_ref[:, :rows] = top.T
    plain_ref[:, rows:] = bottom.T
    me = me_ref[0]
    for b in range(4):
        block = plain_ref[pl.ds(pl.multiple_of((me ^ b) * PART, PART), PART), :]
        turned_ref[PART * b:PART * (b + 1), :] = block
        pair_ref[PART * b:PART * (b + 1), :], pair_ref[HALF + PART * b:HALF + PART * (b + 1), :] = split(block)
    spot = 0
    for ref in (*before, left_ref):
        gram = dot(turned_ref[...], ref[...], precision=HIGHEST)
        keep_ref[:, spot:spot + HALF] = gram[:QUARTER]
        give_ref[:, spot:spot + HALF] = gram[QUARTER:]
        spot += HALF
    step = 2 * TILE
    for c in range(high_ref.shape[1] // step):
        lanes = pl.ds(c * step, step)
        both = dot(pair_ref[...], high_ref[:, lanes])
        part = (both[:HALF] + both[HALF:]) + dot(pair_ref[:HALF, :], low_ref[:, lanes])
        lanes = pl.ds(spot + c * step, step)
        keep_ref[:, lanes] = part[:QUARTER]
        give_ref[:, lanes] = part[QUARTER:]


def product(scaled, me, before, parts, buffer):
    rows, cols = buffer[0].shape
    width = HALF * (len(before) + 1) + cols
    return call(
        functools.partial(product_kernel, not before, scaled), "product", 4 * rows * width * RANK, 4 * rows * width,
        out_shape=[shaped(QUARTER, width)] * 2 + [shaped(rows, HALF)],
        in_specs=[SMEM] + [VMEM] * (6 + len(before)), out_specs=[VMEM] * 3,
        scratch_shapes=[pltpu.VMEM((HALF, rows), F32)] * 2 + [pltpu.VMEM((RANK, rows), BF16)],
    )(me, *before, *parts, *buffer)


def solved(inverse, wide_ref, out_ref, pair_ref):
    inverse = split(inverse)
    square = jnp.zeros((HALF, 1), F32)
    step = 2 * TILE
    for c in range(wide_ref.shape[1] // step):
        lanes = pl.ds(step * c, step)
        part = dot3(inverse, split(wide_ref[:, lanes]))
        out_ref[:, lanes] = part
        pair_ref[:HALF, lanes], pair_ref[HALF:, lanes] = split(part)
        square = square + jnp.sum(part * part, axis=1, keepdims=True)
    return jnp.broadcast_to(square, (HALF, HALF)).T[:SUB, :]


def first_kernel(me_ref, mine_ref, other_ref, inverse_ref, wide_ref, out_ref, pair_ref, square_ref, gram_ref):
    me = me_ref[0]
    place(gram_ref, me, mine_ref[:, :HALF], other_ref[:, :HALF])
    place(wide_ref, me, mine_ref[:, HALF:], other_ref[:, HALF:])
    inverse_ref[...] = inverse_factor(gram_ref[...])
    square_ref[...] = solved(inverse_ref[...], wide_ref, out_ref, pair_ref)


def first_solve(me, mine, other):
    cols = mine.shape[1] - HALF
    return call(
        first_kernel, "first_solve", 5_000_000_000, 20 * HALF * cols,
        out_shape=[shaped(HALF, HALF), shaped(HALF, cols), shaped(HALF, cols), shaped(RANK, cols, dtype=BF16), shaped(SUB, HALF)],
        in_specs=[SMEM, VMEM, VMEM], out_specs=[VMEM] * 5, scratch_shapes=[pltpu.VMEM((HALF, HALF), F32)],
    )(me, mine, other)


def second_kernel(me_ref, mine_ref, other_ref, first_ref, wide0_ref, inverse_ref, out_ref, pair_ref, square_ref, gram_ref, wide_ref):
    me = me_ref[0]
    place(gram_ref, me, mine_ref[:, :RANK], other_ref[:, :RANK])
    place(wide_ref.at[HALF:, :], me, mine_ref[:, RANK:], other_ref[:, RANK:])
    wide_ref[:HALF, :] = wide0_ref[...]
    first = first_ref[...]
    side = dot(gram_ref[:, :HALF], first, NT, HIGHEST)
    second = inverse_factor(gram_ref[:, HALF:] - dot(side, side, NT, HIGHEST))
    inverse_ref[:HALF, :HALF] = first
    inverse_ref[:HALF, HALF:] = jnp.zeros((HALF, HALF), F32)
    inverse_ref[HALF:, :HALF] = -dot(second, dot(side, first, precision=HIGHEST), precision=HIGHEST)
    inverse_ref[HALF:, HALF:] = second
    square_ref[...] = solved(inverse_ref[HALF:, :], wide_ref, out_ref, pair_ref)


def second_solve(me, mine, other, first, wide0):
    cols = mine.shape[1] - RANK
    return call(
        second_kernel, "second_solve", 6_000_000_000, 20 * HALF * cols,
        out_shape=[shaped(RANK, RANK), shaped(HALF, cols), shaped(RANK, cols, dtype=BF16), shaped(SUB, HALF)],
        in_specs=[SMEM] + [VMEM] * 4, out_specs=[VMEM] * 4,
        scratch_shapes=[pltpu.VMEM((HALF, RANK), F32), pltpu.VMEM((RANK, cols), F32)],
    )(me, mine, other, first, wide0)


def momentum_kernel(left0_ref, left1_ref, inverse_ref, pair0_ref, pair1_ref, high_ref, low_ref, out_ref, ortho_ref, half_ref):
    step, width = pl.program_id(0), out_ref.shape[1]

    @pl.when(step == 0)
    def _():
        left = jnp.concatenate([left0_ref[...], left1_ref[...]], axis=1)
        ortho = dot3(split(left), split(inverse_ref[...]), NT)
        ortho_ref[...] = ortho
        half_ref[...] = ortho.astype(BF16)

    lanes = pl.ds(pl.multiple_of(step * width, width), width)
    factor = jnp.concatenate([pair0_ref[:HALF, lanes], pair1_ref[:HALF, lanes]], axis=0)
    feedback = F32(1.0 - beta_mom) * dot(half_ref[...], factor)
    out_ref[...] = (high_ref[:, lanes].astype(F32) + low_ref[:, lanes].astype(F32)) - feedback


def momentum_update(lefts, inverse, pairs, buffer):
    rows, cols = buffer[0].shape
    return call(
        momentum_kernel, "momentum", 2 * rows * cols * RANK, 4 * rows * cols,
        out_shape=[shaped(rows, cols), shaped(rows, RANK)], grid=(cols // STEP,),
        in_specs=[VMEM] * 7, out_specs=[pl.BlockSpec((rows, STEP), lambda i: (0, i)), VMEM],
        scratch_shapes=[pltpu.VMEM((rows, RANK), BF16)],
    )(*lefts, inverse, *pairs, *buffer)


def weight_kernel(ortho_ref, s0, s1, s2, s3, pair0_ref, pair1_ref, factor0_ref, factor1_ref, weight_ref, out_ref, basis_ref, triple_ref):
    total = (s0[0:1, :] + s1[0:1, :]) + (s2[0:1, :] + s3[0:1, :])
    scale = 1.0 / jnp.sqrt(total / F32(D) + F32(1e-06))
    step, width = pl.program_id(0), out_ref.shape[1]

    @pl.when(step == 0)
    def _():
        high, low = split(ortho_ref[...] * (scale * F32(learn_rate * (D / RANK) ** 0.5)))
        triple_ref[:, :RANK] = high
        triple_ref[:, RANK:2 * RANK] = low
        triple_ref[:, 2 * RANK:] = high

    lanes = pl.ds(pl.multiple_of(step * width, width), width)
    high = [pair0_ref[:HALF, lanes], pair1_ref[:HALF, lanes]]
    factor = jnp.concatenate([*high, *high, pair0_ref[HALF:, lanes], pair1_ref[HALF:, lanes]], axis=0)
    out_ref[...] = weight_ref[:, lanes] - dot(triple_ref[...], factor)
    basis_ref[:, :HALF] = factor0_ref[:, lanes].T * scale[:, :HALF]
    basis_ref[:, HALF:] = factor1_ref[:, lanes].T * scale[:, HALF:]


def weight_update(ortho, squares, pairs, factors, weight):
    rows, cols = weight.shape
    return call(
        weight_kernel, "weight", 6 * rows * cols * RANK, 4 * rows * cols,
        out_shape=[shaped(rows, cols), shaped(cols, RANK)], grid=(cols // STEP,), in_specs=[VMEM] * 10,
        out_specs=[pl.BlockSpec((rows, STEP), lambda i: (0, i)), pl.BlockSpec((STEP, RANK), lambda i: (i, 0))],
        scratch_shapes=[pltpu.VMEM((rows, 3 * RANK), BF16)],
    )(ortho, *squares, *pairs, *factors, weight)


def swap(x, axis, bit):
    size = lax.axis_size(axis)
    return lax.ppermute(x, axis, [(i, i ^ bit) for i in range(size)])


def together(*arrays):
    return lax.optimization_barrier(arrays)


def tuned(momentum, gradient, weight, right_basis):
    row = lax.axis_index("row")
    me = (2 * (row & 1) + ((row >> 1) & 1)).astype(jnp.int32)[None]
    high, low, up0, down0, up1, down1 = start(me, momentum[0], gradient[0], right_basis)
    buffer = (high, low)
    got0 = swap(up0, "col", 1), swap(down0, "col", 2)
    up0, down0, got0, up1, down1 = together(up0, down0, got0, up1, down1)
    for sweep in range(ITERS):
        last, scaled = sweep == ITERS - 1, sweep > 0

        up0, down0 = up0 + got0[0], down0 + got0[1]
        got0 = swap(up0, "col", 2), swap(down0, "col", 1)
        if sweep:
            up1, down1 = left_product(buffer, split1, square1)
        up0, down0, got0, up1, down1 = together(up0, down0, got0, up1, down1)

        keep0, give0, left0 = product(scaled, me, (), (up0, got0[0], down0, got0[1]), buffer)
        got1 = swap(up1, "col", 1), swap(down1, "col", 2)
        keep0, give0, left0, up1, down1, got1 = together(keep0, give0, left0, up1, down1, got1)

        part0 = keep0 + swap(give0, "row", 1)
        pair0 = swap(part0[PART:], "row", 2)
        up1, down1 = up1 + got1[0], down1 + got1[1]
        got1 = swap(up1, "col", 2), swap(down1, "col", 1)
        keep1, give1, left1 = product(scaled, me, (left0,), (up1, got1[0], down1, got1[1]), buffer)
        part0, pair0, keep1, give1 = together(part0, pair0, keep1, give1)

        core1 = swap(give1, "row", 1)
        part0, pair0, keep1, core1 = together(part0, pair0, keep1, core1)

        side0 = part0[:PART] + pair0
        cross0 = swap(side0, "row", 4)
        part1 = keep1 + core1
        pair1 = swap(part1[PART:], "row", 2)
        side0, cross0, part1, pair1 = together(side0, cross0, part1, pair1)

        total0 = side0 + cross0
        back0 = swap(total0, "row", 2)
        side1 = part1[:PART] + pair1
        cross1 = swap(side1, "row", 4)
        total0, back0, side1, cross1 = together(total0, back0, side1, cross1)

        mine0 = jnp.concatenate([total0, back0], axis=0)
        other0 = swap(mine0, "row", 1)
        total1 = side1 + cross1
        back1 = swap(total1, "row", 2)
        first, wide, factor0, split0, square0 = first_solve(me, mine0, other0)
        total1, back1, first, wide, split0, square0 = together(total1, back1, first, wide, split0, square0)

        mine1 = jnp.concatenate([total1, back1], axis=0)
        other1 = swap(mine1, "row", 1)
        if not last:
            up0, down0 = left_product(buffer, split0, square0)
            got0 = swap(up0, "col", 1), swap(down0, "col", 2)
        inverse, factor1, split1, square1 = second_solve(me, mine1, other1, first, wide)
        if not last:
            up0, down0, got0, split1, square1 = together(up0, down0, got0, split1, square1)

    square = jnp.concatenate([square0, square1], axis=1)
    squares = (square, swap(square, "col", 1), swap(square, "col", 2), swap(square, "col", 3))
    new_momentum, ortho = momentum_update((left0, left1), inverse, (split0, split1), buffer)
    new_weight, new_basis = weight_update(ortho, squares, (split0, split1), (factor0, factor1), weight)
    return new_momentum[None], new_weight, new_basis


def general(momentum, gradient, weight, right_basis):
    replicas = lax.axis_size("rep")
    buffer = momentum[0] + gradient[0].astype(F32)
    basis, dims = right_basis, NN
    for sweep in range(ITERS):
        left = lax.psum(dot(buffer, basis, dims, HIGH) / replicas, ("col", "rep"))
        if sweep:
            left = left / rms
        gram = lax.psum(dot(left, left, ((0,), (0,)), HIGHEST), "row")
        wide = lax.psum(dot(left, buffer, ((0,), (0,)), HIGH) / replicas, ("row", "rep"))
        inverse = inverse_cholesky(gram)
        factor = dot(inverse, wide, precision=HIGHEST)
        rms = jnp.sqrt(lax.psum(jnp.sum(factor * factor, axis=1)[None, :], "col") / F32(D) + 1e-06)
        basis, dims = factor, NT
    ortho = dot(left, inverse, NT, HIGHEST)
    new_momentum = (buffer - (1.0 - beta_mom) * dot(ortho, factor, precision=HIGH))[None]
    basis = factor / rms.T
    new_weight = weight - learn_rate * jnp.sqrt(F32(D) / F32(RANK)) * dot(ortho, basis, precision=HIGH)
    return new_momentum, new_weight, basis.T


def solution(mesh):
    sizes = dict(mesh.shape)
    fits = sizes["row"] == 8 and sizes["col"] == 4 and sizes["rep"] == 1
    return jax.shard_map(
        tuned if fits else general,
        mesh=mesh,
        in_specs=(P("rep", "row", "col"), P("rep", "row", "col"), P("row", "col"), P("col", None)),
        out_specs=(P("rep", "row", "col"), P("row", "col"), P("col", None)),
        check_vma=False,
    )
```

```python
import functools

import jax
import jax.numpy as jnp
from jax import lax
from jax.experimental import pallas as pl
from jax.experimental.pallas import tpu as pltpu
from jax.sharding import PartitionSpec as P

D = 8192
RANK = 256
ITERS = 2
HALF = RANK // 2
QUARTER = RANK // 4
PART = RANK // 8
SUB = 8
TILE = 256
STEP = 512

beta_mom = 0.95
learn_rate = 0.05

F32 = jnp.float32
BF16 = jnp.bfloat16
HIGHEST = lax.Precision.HIGHEST
HIGH = lax.Precision.HIGH
NT = ((1,), (1,))
NN = ((1,), (0,))


def dot(a, b, dims=NN, precision=None):
    return lax.dot_general(a, b, (dims, ((), ())), precision=precision, preferred_element_type=F32)


def split(x):
    high = x.astype(BF16)
    return high, (x - high.astype(F32)).astype(BF16)


def dot3(a, b, dims=NN):
    return dot(a[0], b[0], dims) + (dot(a[1], b[0], dims) + dot(a[0], b[1], dims))


def call(kernel, name, flops, moved, **rest):
    rest.setdefault("compiler_params", pltpu.CompilerParams(vmem_limit_bytes=24 * 2**20))
    return pl.pallas_call(
        kernel,
        name=name,
        cost_estimate=pl.CostEstimate(flops=flops, bytes_accessed=moved, transcendentals=0),
        **rest,
    )


def shaped(*shape, dtype=F32):
    return jax.ShapeDtypeStruct(shape, dtype)


VMEM = pl.BlockSpec(memory_space=pltpu.VMEM)
HBM = pl.BlockSpec(memory_space=pltpu.HBM)
SMEM = pl.BlockSpec(memory_space=pltpu.SMEM)


def inverse_factor(block):
    shape = (SUB, HALF)
    lanes = lax.broadcasted_iota(jnp.int32, shape, 1)
    subs = lax.broadcasted_iota(jnp.int32, shape, 0)
    count = HALF // SUB

    def spread(tile, lane):
        return jnp.broadcast_to(tile[:, lane:lane + 1], shape)

    def repeat(tile, sub):
        return jnp.broadcast_to(tile[sub:sub + 1, :], shape)

    tiles = [block[SUB * i:SUB * (i + 1), :] for i in range(count)]
    for t in range(count):
        low = SUB * t
        panel = jnp.logical_and(lanes >= low, lanes < low + SUB)
        cols = [spread(tiles[t], low + j) for j in range(SUB)]
        tile = jnp.where(panel, 0.0, tiles[t])
        scale, rows, upper = [], [], {}
        for j in range(SUB):
            r = lax.rsqrt(repeat(cols[j], j))
            mult = jnp.where(subs > j, cols[j] * r, 0.0)
            for k in range(j + 1, SUB):
                upper[j, k] = repeat(cols[k], j) * r
                cols[k] = cols[k] - mult * upper[j, k]
            row = jnp.where(lanes == low + j, r, repeat(tile, j) * r)
            tile = jnp.where(subs == j, row, tile - mult * row)
            scale.append(r)
            rows.append(row)
        tiles[t] = tile
        for i in range(t + 1, count):
            cols = [spread(tiles[i], low + j) for j in range(SUB)]
            tile = jnp.where(panel, 0.0, tiles[i])
            for j in range(SUB):
                mult = cols[j] * scale[j]
                for k in range(j + 1, SUB):
                    cols[k] = cols[k] - mult * upper[j, k]
                tile = tile - mult * rows[j]
            tiles[i] = tile
    full = jnp.concatenate(tiles, axis=0)
    down = lax.broadcasted_iota(jnp.int32, (HALF, HALF), 0)
    across = lax.broadcasted_iota(jnp.int32, (HALF, HALF), 1)
    return jnp.where(across <= down, full, 0.0)


def inverse_body(gram_ref, out_ref):
    first = inverse_factor(gram_ref[:HALF, :HALF])
    side = dot(gram_ref[HALF:, :HALF], first, NT, HIGHEST)
    rest = gram_ref[HALF:, HALF:] - dot(side, side, NT, HIGHEST)
    second = inverse_factor(rest)
    out_ref[:HALF, :HALF] = first
    out_ref[:HALF, HALF:] = jnp.zeros((HALF, HALF), F32)
    out_ref[HALF:, :HALF] = -dot(second, dot(side, first, precision=HIGHEST), precision=HIGHEST)
    out_ref[HALF:, HALF:] = second


def inverse_cholesky(gram):
    return call(
        inverse_body, "inverse_cholesky", 12_000_000_000, 2 * 4 * RANK * RANK,
        out_shape=shaped(RANK, RANK), in_specs=[VMEM], out_specs=VMEM,
    )(gram)


def place(out_ref, me, mine, other):
    for b in range(4):
        block = (mine, other)[b // 2][PART * (b % 2):PART * (b % 2 + 1), :]
        out_ref[pl.ds(pl.multiple_of((me ^ b) * PART, PART), PART), :] = block


def start_kernel(me_ref, momentum_ref, gradient_ref, basis_ref, high_ref, low_ref, up_ref, down_ref, second_ref):
    rows, cols = momentum_ref.shape
    half = rows // 2

    def body(momentum, gradient, basis):
        step = pl.program_id(0)
        here = pl.ds(pl.multiple_of(step * TILE, TILE), TILE)
        bhigh, blow = split(basis[...])
        second_ref[here, :HALF], second_ref[here, HALF:] = bhigh[:, HALF:], blow[:, HALF:]
        high, low = split(momentum[...] + gradient[...].astype(F32))
        high_ref[:, here], low_ref[:, here] = high, low
        both = dot(high, jnp.concatenate([bhigh[:, :HALF], blow[:, :HALF]], axis=1))
        part = (both[:, :HALF] + both[:, HALF:]) + dot(low, bhigh[:, :HALF])

        @pl.when(step == 0)
        def _():
            up_ref[...] = part[:half]
            down_ref[...] = part[half:]

        @pl.when(step > 0)
        def _():
            up_ref[...] += part[:half]
            down_ref[...] += part[half:]

    block = pl.BlockSpec((rows, TILE), lambda i: (0, i))
    pltpu.emit_pipeline(
        body, grid=(cols // TILE,), in_specs=[block, block, pl.BlockSpec((TILE, RANK), lambda i: (i, 0))],
    )(momentum_ref, gradient_ref, basis_ref)


def start(me, *args):
    rows, cols = args[0].shape
    return call(
        start_kernel, "start", 4 * rows * cols * RANK, 6 * rows * cols,
        out_shape=[pltpu.VMEM((rows, cols), BF16)] * 2 + [shaped(rows // 2, HALF)] * 2 + [shaped(cols, RANK, dtype=BF16)],
        in_specs=[SMEM] + [HBM] * 3, out_specs=[VMEM] * 5,
    )(me, *(pltpu.with_memory_space_constraint(x, pltpu.HBM) for x in args))


def left_kernel(dims, high_ref, low_ref, factor_ref, *refs):
    up_ref, down_ref = refs[-2:]
    half = down_ref.shape[0]
    fhigh = factor_ref[:HALF, :] if dims == NT else factor_ref[:, :HALF]
    for ref, base in ((up_ref, 0), (down_ref, half)):
        both = dot(high_ref[base:base + half, :], factor_ref[...], dims)
        ref[:half, :] = (both[:, :HALF] + both[:, HALF:]) + dot(low_ref[base:base + half, :], fhigh, dims)
    if len(refs) == 3:
        up_ref[half:, :] = refs[0][...]


def left_product(buffer, factor, *square, dims=NT):
    rows, cols = buffer[0].shape
    return call(
        functools.partial(left_kernel, dims), "left", 0, 4 * rows * cols,
        out_shape=[shaped(rows // 2 + SUB * len(square), HALF), shaped(rows // 2, HALF)],
        in_specs=[VMEM] * (3 + len(square)), out_specs=[VMEM] * 2,
    )(*buffer, factor, *square)


def product_kernel(first, scaled, me_ref, *refs):
    before, refs = ((), refs) if first else (refs[:1], refs[1:])
    up, up_more, down, down_more, high_ref, low_ref, keep_ref, give_ref, left_ref, plain_ref, turned_ref, pair_ref = refs
    rows = down.shape[0]
    top, bottom = up[:rows, :] + up_more[:rows, :], down[...] + down_more[...]
    if scaled:
        total = up[rows:rows + 1, :] + up_more[rows:rows + 1, :]
        scale = 1.0 / jnp.sqrt(total / F32(D) + F32(1e-06))
        top, bottom = top * scale, bottom * scale
    left_ref[:rows, :] = top
    left_ref[rows:, :] = bottom
    plain_ref[:, :rows] = top.T
    plain_ref[:, rows:] = bottom.T
    me = me_ref[0]
    for b in range(4):
        block = plain_ref[pl.ds(pl.multiple_of((me ^ b) * PART, PART), PART), :]
        turned_ref[PART * b:PART * (b + 1), :] = block
        pair_ref[PART * b:PART * (b + 1), :], pair_ref[HALF + PART * b:HALF + PART * (b + 1), :] = split(block)
    spot = 0
    for ref in (*before, left_ref):
        gram = dot(turned_ref[...], ref[...], precision=HIGHEST)
        keep_ref[:, spot:spot + HALF] = gram[:QUARTER]
        give_ref[:, spot:spot + HALF] = gram[QUARTER:]
        spot += HALF
    step = 2 * TILE
    for c in range(high_ref.shape[1] // step):
        lanes = pl.ds(c * step, step)
        both = dot(pair_ref[...], high_ref[:, lanes])
        part = (both[:HALF] + both[HALF:]) + dot(pair_ref[:HALF, :], low_ref[:, lanes])
        lanes = pl.ds(spot + c * step, step)
        keep_ref[:, lanes] = part[:QUARTER]
        give_ref[:, lanes] = part[QUARTER:]


def product(scaled, me, before, parts, buffer):
    rows, cols = buffer[0].shape
    width = HALF * (len(before) + 1) + cols
    return call(
        functools.partial(product_kernel, not before, scaled), "product", 4 * rows * width * RANK, 4 * rows * width,
        out_shape=[shaped(QUARTER, width)] * 2 + [shaped(rows, HALF)],
        in_specs=[SMEM] + [VMEM] * (6 + len(before)), out_specs=[VMEM] * 3,
        scratch_shapes=[pltpu.VMEM((HALF, rows), F32)] * 2 + [pltpu.VMEM((RANK, rows), BF16)],
    )(me, *before, *parts, *buffer)


def solved(inverse, wide_ref, out_ref, pair_ref):
    inverse = split(inverse)
    square = jnp.zeros((HALF, 1), F32)
    step = 2 * TILE
    for c in range(wide_ref.shape[1] // step):
        lanes = pl.ds(step * c, step)
        part = dot3(inverse, split(wide_ref[:, lanes]))
        out_ref[:, lanes] = part
        pair_ref[:HALF, lanes], pair_ref[HALF:, lanes] = split(part)
        square = square + jnp.sum(part * part, axis=1, keepdims=True)
    return jnp.broadcast_to(square, (HALF, HALF)).T[:SUB, :]


def first_kernel(me_ref, mine_ref, other_ref, inverse_ref, wide_ref, out_ref, pair_ref, square_ref, gram_ref):
    me = me_ref[0]
    place(gram_ref, me, mine_ref[:, :HALF], other_ref[:, :HALF])
    place(wide_ref, me, mine_ref[:, HALF:], other_ref[:, HALF:])
    inverse_ref[...] = inverse_factor(gram_ref[...])
    square_ref[...] = solved(inverse_ref[...], wide_ref, out_ref, pair_ref)


def first_solve(me, mine, other):
    cols = mine.shape[1] - HALF
    return call(
        first_kernel, "first_solve", 5_000_000_000, 20 * HALF * cols,
        out_shape=[shaped(HALF, HALF), shaped(HALF, cols), shaped(HALF, cols), shaped(RANK, cols, dtype=BF16), shaped(SUB, HALF)],
        in_specs=[SMEM, VMEM, VMEM], out_specs=[VMEM] * 5, scratch_shapes=[pltpu.VMEM((HALF, HALF), F32)],
    )(me, mine, other)


def second_kernel(me_ref, mine_ref, other_ref, first_ref, wide0_ref, inverse_ref, out_ref, pair_ref, square_ref, gram_ref, wide_ref):
    me = me_ref[0]
    place(gram_ref, me, mine_ref[:, :RANK], other_ref[:, :RANK])
    place(wide_ref.at[HALF:, :], me, mine_ref[:, RANK:], other_ref[:, RANK:])
    wide_ref[:HALF, :] = wide0_ref[...]
    first = first_ref[...]
    side = dot(gram_ref[:, :HALF], first, NT, HIGHEST)
    second = inverse_factor(gram_ref[:, HALF:] - dot(side, side, NT, HIGHEST))
    inverse_ref[:HALF, :HALF] = first
    inverse_ref[:HALF, HALF:] = jnp.zeros((HALF, HALF), F32)
    inverse_ref[HALF:, :HALF] = -dot(second, dot(side, first, precision=HIGHEST), precision=HIGHEST)
    inverse_ref[HALF:, HALF:] = second
    square_ref[...] = solved(inverse_ref[HALF:, :], wide_ref, out_ref, pair_ref)


def second_solve(me, mine, other, first, wide0):
    cols = mine.shape[1] - RANK
    return call(
        second_kernel, "second_solve", 6_000_000_000, 20 * HALF * cols,
        out_shape=[shaped(RANK, RANK), shaped(HALF, cols), shaped(RANK, cols, dtype=BF16), shaped(SUB, HALF)],
        in_specs=[SMEM] + [VMEM] * 4, out_specs=[VMEM] * 4,
        scratch_shapes=[pltpu.VMEM((HALF, RANK), F32), pltpu.VMEM((RANK, cols), F32)],
    )(me, mine, other, first, wide0)


def momentum_kernel(left0_ref, left1_ref, inverse_ref, pair0_ref, pair1_ref, high_ref, low_ref, out_ref, ortho_ref, half_ref):
    step, width = pl.program_id(0), out_ref.shape[1]

    @pl.when(step == 0)
    def _():
        left = jnp.concatenate([left0_ref[...], left1_ref[...]], axis=1)
        ortho = dot3(split(left), split(inverse_ref[...]), NT)
        ortho_ref[...] = ortho
        half_ref[...] = ortho.astype(BF16)

    lanes = pl.ds(pl.multiple_of(step * width, width), width)
    factor = jnp.concatenate([pair0_ref[:HALF, lanes], pair1_ref[:HALF, lanes]], axis=0)
    feedback = F32(1.0 - beta_mom) * dot(half_ref[...], factor)
    out_ref[...] = (high_ref[:, lanes].astype(F32) + low_ref[:, lanes].astype(F32)) - feedback


def momentum_update(lefts, inverse, pairs, buffer):
    rows, cols = buffer[0].shape
    return call(
        momentum_kernel, "momentum", 2 * rows * cols * RANK, 4 * rows * cols,
        out_shape=[shaped(rows, cols), shaped(rows, RANK)], grid=(cols // STEP,),
        in_specs=[VMEM] * 7, out_specs=[pl.BlockSpec((rows, STEP), lambda i: (0, i)), VMEM],
        scratch_shapes=[pltpu.VMEM((rows, RANK), BF16)],
    )(*lefts, inverse, *pairs, *buffer)


def weight_kernel(ortho_ref, s0, s1, s2, s3, pair0_ref, pair1_ref, factor0_ref, factor1_ref, weight_ref, out_ref, basis_ref, triple_ref):
    total = (s0[0:1, :] + s1[0:1, :]) + (s2[0:1, :] + s3[0:1, :])
    scale = 1.0 / jnp.sqrt(total / F32(D) + F32(1e-06))
    step, width = pl.program_id(0), out_ref.shape[1]

    @pl.when(step == 0)
    def _():
        high, low = split(ortho_ref[...] * (scale * F32(learn_rate * (D / RANK) ** 0.5)))
        triple_ref[:, :RANK] = high
        triple_ref[:, RANK:2 * RANK] = low
        triple_ref[:, 2 * RANK:] = high

    lanes = pl.ds(pl.multiple_of(step * width, width), width)
    high = [pair0_ref[:HALF, lanes], pair1_ref[:HALF, lanes]]
    factor = jnp.concatenate([*high, *high, pair0_ref[HALF:, lanes], pair1_ref[HALF:, lanes]], axis=0)
    out_ref[...] = weight_ref[:, lanes] - dot(triple_ref[...], factor)
    basis_ref[:, :HALF] = factor0_ref[:, lanes].T * scale[:, :HALF]
    basis_ref[:, HALF:] = factor1_ref[:, lanes].T * scale[:, HALF:]


def weight_update(ortho, squares, pairs, factors, weight):
    rows, cols = weight.shape
    return call(
        weight_kernel, "weight", 6 * rows * cols * RANK, 4 * rows * cols,
        out_shape=[shaped(rows, cols), shaped(cols, RANK)], grid=(cols // STEP,), in_specs=[VMEM] * 10,
        out_specs=[pl.BlockSpec((rows, STEP), lambda i: (0, i)), pl.BlockSpec((STEP, RANK), lambda i: (i, 0))],
        scratch_shapes=[pltpu.VMEM((rows, 3 * RANK), BF16)],
    )(ortho, *squares, *pairs, *factors, weight)


def swap(x, axis, bit):
    size = lax.axis_size(axis)
    return lax.ppermute(x, axis, [(i, i ^ bit) for i in range(size)])


def together(*arrays):
    return lax.optimization_barrier(arrays)


def tuned(momentum, gradient, weight, right_basis):
    row = lax.axis_index("row")
    me = (2 * (row & 1) + ((row >> 1) & 1)).astype(jnp.int32)[None]
    high, low, up0, down0, second = start(me, momentum[0], gradient[0], right_basis)
    buffer = (high, low)
    got0 = swap(up0, "col", 1), swap(down0, "col", 2)
    up1, down1 = left_product(buffer, second, dims=NN)
    up0, down0, got0, up1, down1 = together(up0, down0, got0, up1, down1)
    for sweep in range(ITERS):
        last, scaled = sweep == ITERS - 1, sweep > 0

        up0, down0 = up0 + got0[0], down0 + got0[1]
        got0 = swap(up0, "col", 2), swap(down0, "col", 1)
        if sweep:
            up1, down1 = left_product(buffer, split1, square1)
        up0, down0, got0, up1, down1 = together(up0, down0, got0, up1, down1)

        keep0, give0, left0 = product(scaled, me, (), (up0, got0[0], down0, got0[1]), buffer)
        got1 = swap(up1, "col", 1), swap(down1, "col", 2)
        keep0, give0, left0, up1, down1, got1 = together(keep0, give0, left0, up1, down1, got1)

        part0 = keep0 + swap(give0, "row", 1)
        pair0 = swap(part0[PART:], "row", 2)
        up1, down1 = up1 + got1[0], down1 + got1[1]
        got1 = swap(up1, "col", 2), swap(down1, "col", 1)
        keep1, give1, left1 = product(scaled, me, (left0,), (up1, got1[0], down1, got1[1]), buffer)
        part0, pair0, keep1, give1 = together(part0, pair0, keep1, give1)

        core1 = swap(give1, "row", 1)
        part0, pair0, keep1, core1 = together(part0, pair0, keep1, core1)

        side0 = part0[:PART] + pair0
        cross0 = swap(side0, "row", 4)
        part1 = keep1 + core1
        pair1 = swap(part1[PART:], "row", 2)
        side0, cross0, part1, pair1 = together(side0, cross0, part1, pair1)

        total0 = side0 + cross0
        back0 = swap(total0, "row", 2)
        side1 = part1[:PART] + pair1
        cross1 = swap(side1, "row", 4)
        total0, back0, side1, cross1 = together(total0, back0, side1, cross1)

        mine0 = jnp.concatenate([total0, back0], axis=0)
        other0 = swap(mine0, "row", 1)
        total1 = side1 + cross1
        back1 = swap(total1, "row", 2)
        first, wide, factor0, split0, square0 = first_solve(me, mine0, other0)
        if not last:
            up0, down0 = left_product(buffer, split0, square0)
        total1, back1, first, wide, split0, square0, up0, down0 = together(total1, back1, first, wide, split0, square0, up0, down0)

        mine1 = jnp.concatenate([total1, back1], axis=0)
        other1 = swap(mine1, "row", 1)
        if not last:
            got0 = swap(up0, "col", 1), swap(down0, "col", 2)
        inverse, factor1, split1, square1 = second_solve(me, mine1, other1, first, wide)
        if not last:
            up0, down0, got0, split1, square1 = together(up0, down0, got0, split1, square1)

    square = jnp.concatenate([square0, square1], axis=1)
    squares = (square, swap(square, "col", 1), swap(square, "col", 2), swap(square, "col", 3))
    new_momentum, ortho = momentum_update((left0, left1), inverse, (split0, split1), buffer)
    new_weight, new_basis = weight_update(ortho, squares, (split0, split1), (factor0, factor1), weight)
    return new_momentum[None], new_weight, new_basis


def general(momentum, gradient, weight, right_basis):
    replicas = lax.axis_size("rep")
    buffer = momentum[0] + gradient[0].astype(F32)
    basis, dims = right_basis, NN
    for sweep in range(ITERS):
        left = lax.psum(dot(buffer, basis, dims, HIGH) / replicas, ("col", "rep"))
        if sweep:
            left = left / rms
        gram = lax.psum(dot(left, left, ((0,), (0,)), HIGHEST), "row")
        wide = lax.psum(dot(left, buffer, ((0,), (0,)), HIGH) / replicas, ("row", "rep"))
        inverse = inverse_cholesky(gram)
        factor = dot(inverse, wide, precision=HIGHEST)
        rms = jnp.sqrt(lax.psum(jnp.sum(factor * factor, axis=1)[None, :], "col") / F32(D) + 1e-06)
        basis, dims = factor, NT
    ortho = dot(left, inverse, NT, HIGHEST)
    new_momentum = (buffer - (1.0 - beta_mom) * dot(ortho, factor, precision=HIGH))[None]
    basis = factor / rms.T
    new_weight = weight - learn_rate * jnp.sqrt(F32(D) / F32(RANK)) * dot(ortho, basis, precision=HIGH)
    return new_momentum, new_weight, basis.T


def solution(mesh):
    sizes = dict(mesh.shape)
    fits = sizes["row"] == 8 and sizes["col"] == 4 and sizes["rep"] == 1
    return jax.shard_map(
        tuned if fits else general,
        mesh=mesh,
        in_specs=(P("rep", "row", "col"), P("rep", "row", "col"), P("row", "col"), P("col", None)),
        out_specs=(P("rep", "row", "col"), P("row", "col"), P("col", None)),
        check_vma=False,
    )
```

```python
import functools

import jax
import jax.numpy as jnp
from jax import lax
from jax.experimental import pallas as pl
from jax.experimental.pallas import tpu as pltpu
from jax.sharding import PartitionSpec as P

D = 8192
RANK = 256
ITERS = 2
HALF = RANK // 2
QUARTER = RANK // 4
PART = RANK // 8
SUB = 8
TILE = 256
STEP = 512

beta_mom = 0.95
learn_rate = 0.05

F32 = jnp.float32
BF16 = jnp.bfloat16
HIGHEST = lax.Precision.HIGHEST
HIGH = lax.Precision.HIGH
NT = ((1,), (1,))
NN = ((1,), (0,))


def dot(a, b, dims=NN, precision=None):
    return lax.dot_general(a, b, (dims, ((), ())), precision=precision, preferred_element_type=F32)


def split(x):
    high = x.astype(BF16)
    return high, (x - high.astype(F32)).astype(BF16)


def dot3(a, b, dims=NN):
    return dot(a[0], b[0], dims) + (dot(a[1], b[0], dims) + dot(a[0], b[1], dims))


def call(kernel, name, flops, moved, **rest):
    rest.setdefault("compiler_params", pltpu.CompilerParams(vmem_limit_bytes=24 * 2**20))
    return pl.pallas_call(
        kernel,
        name=name,
        cost_estimate=pl.CostEstimate(flops=flops, bytes_accessed=moved, transcendentals=0),
        **rest,
    )


def shaped(*shape, dtype=F32):
    return jax.ShapeDtypeStruct(shape, dtype)


VMEM = pl.BlockSpec(memory_space=pltpu.VMEM)
HBM = pl.BlockSpec(memory_space=pltpu.HBM)
SMEM = pl.BlockSpec(memory_space=pltpu.SMEM)


def inverse_factor(block):
    shape = (SUB, HALF)
    lanes = lax.broadcasted_iota(jnp.int32, shape, 1)
    subs = lax.broadcasted_iota(jnp.int32, shape, 0)
    count = HALF // SUB

    def spread(tile, lane):
        return jnp.broadcast_to(tile[:, lane:lane + 1], shape)

    def repeat(tile, sub):
        return jnp.broadcast_to(tile[sub:sub + 1, :], shape)

    tiles = [block[SUB * i:SUB * (i + 1), :] for i in range(count)]
    for t in range(count):
        low = SUB * t
        panel = jnp.logical_and(lanes >= low, lanes < low + SUB)
        cols = [spread(tiles[t], low + j) for j in range(SUB)]
        tile = jnp.where(panel, 0.0, tiles[t])
        scale, rows, upper = [], [], {}
        for j in range(SUB):
            r = lax.rsqrt(repeat(cols[j], j))
            mult = jnp.where(subs > j, cols[j] * r, 0.0)
            for k in range(j + 1, SUB):
                upper[j, k] = repeat(cols[k], j) * r
                cols[k] = cols[k] - mult * upper[j, k]
            row = jnp.where(lanes == low + j, r, repeat(tile, j) * r)
            tile = jnp.where(subs == j, row, tile - mult * row)
            scale.append(r)
            rows.append(row)
        tiles[t] = tile
        for i in range(t + 1, count):
            cols = [spread(tiles[i], low + j) for j in range(SUB)]
            tile = jnp.where(panel, 0.0, tiles[i])
            for j in range(SUB):
                mult = cols[j] * scale[j]
                for k in range(j + 1, SUB):
                    cols[k] = cols[k] - mult * upper[j, k]
                tile = tile - mult * rows[j]
            tiles[i] = tile
    full = jnp.concatenate(tiles, axis=0)
    down = lax.broadcasted_iota(jnp.int32, (HALF, HALF), 0)
    across = lax.broadcasted_iota(jnp.int32, (HALF, HALF), 1)
    return jnp.where(across <= down, full, 0.0)


def inverse_body(gram_ref, out_ref):
    first = inverse_factor(gram_ref[:HALF, :HALF])
    side = dot(gram_ref[HALF:, :HALF], first, NT, HIGHEST)
    rest = gram_ref[HALF:, HALF:] - dot(side, side, NT, HIGHEST)
    second = inverse_factor(rest)
    out_ref[:HALF, :HALF] = first
    out_ref[:HALF, HALF:] = jnp.zeros((HALF, HALF), F32)
    out_ref[HALF:, :HALF] = -dot(second, dot(side, first, precision=HIGHEST), precision=HIGHEST)
    out_ref[HALF:, HALF:] = second


def inverse_cholesky(gram):
    return call(
        inverse_body, "inverse_cholesky", 12_000_000_000, 2 * 4 * RANK * RANK,
        out_shape=shaped(RANK, RANK), in_specs=[VMEM], out_specs=VMEM,
    )(gram)


def place(out_ref, me, mine, other):
    for b in range(4):
        block = (mine, other)[b // 2][PART * (b % 2):PART * (b % 2 + 1), :]
        out_ref[pl.ds(pl.multiple_of((me ^ b) * PART, PART), PART), :] = block


def start_kernel(me_ref, momentum_ref, gradient_ref, basis_ref, high_ref, low_ref, up_ref, down_ref, second_ref):
    rows, cols = momentum_ref.shape
    half = rows // 2

    def body(momentum, gradient, basis):
        step = pl.program_id(0)
        here = pl.ds(pl.multiple_of(step * STEP, STEP), STEP)
        bhigh, blow = split(basis[...])
        second_ref[here, :HALF], second_ref[here, HALF:] = bhigh[:, HALF:], blow[:, HALF:]
        high, low = split(momentum[...] + gradient[...].astype(F32))
        high_ref[:, here], low_ref[:, here] = high, low
        both = dot(high, jnp.concatenate([bhigh[:, :HALF], blow[:, :HALF]], axis=1))
        part = (both[:, :HALF] + both[:, HALF:]) + dot(low, bhigh[:, :HALF])

        @pl.when(step == 0)
        def _():
            up_ref[...] = part[:half]
            down_ref[...] = part[half:]

        @pl.when(step > 0)
        def _():
            up_ref[...] += part[:half]
            down_ref[...] += part[half:]

    block = pl.BlockSpec((rows, STEP), lambda i: (0, i))
    pltpu.emit_pipeline(
        body, grid=(cols // STEP,), in_specs=[block, block, pl.BlockSpec((STEP, RANK), lambda i: (i, 0))],
    )(momentum_ref, gradient_ref, basis_ref)


def start(me, *args):
    rows, cols = args[0].shape
    return call(
        start_kernel, "start", 4 * rows * cols * RANK, 6 * rows * cols,
        out_shape=[pltpu.VMEM((rows, cols), BF16)] * 2 + [shaped(rows // 2, HALF)] * 2 + [shaped(cols, RANK, dtype=BF16)],
        in_specs=[SMEM] + [HBM] * 3, out_specs=[VMEM] * 5,
    )(me, *(pltpu.with_memory_space_constraint(x, pltpu.HBM) for x in args))


def left_kernel(dims, high_ref, low_ref, factor_ref, *refs):
    up_ref, down_ref = refs[-2:]
    half = down_ref.shape[0]

    @pl.loop(0, 2 * half // TILE)
    def _(c):
        here = pl.ds(pl.multiple_of(c * TILE, TILE), TILE)
        both = dot(high_ref[here, :], factor_ref[...], dims)
        fhigh = factor_ref[:HALF, :] if dims == NT else factor_ref[:, :HALF]
        part = (both[:, :HALF] + both[:, HALF:]) + dot(low_ref[here, :], fhigh, dims)
        there = pl.ds(pl.multiple_of(lax.rem(c * TILE, half), TILE), TILE)

        @pl.when(c < half // TILE)
        def _():
            up_ref[there, :] = part

        @pl.when(c >= half // TILE)
        def _():
            down_ref[there, :] = part

    if len(refs) == 3:
        up_ref[half:, :] = refs[0][...]


def left_product(buffer, factor, *square, dims=NT):
    rows, cols = buffer[0].shape
    return call(
        functools.partial(left_kernel, dims), "left", 0, 4 * rows * cols,
        out_shape=[shaped(rows // 2 + SUB * len(square), HALF), shaped(rows // 2, HALF)],
        in_specs=[VMEM] * (3 + len(square)), out_specs=[VMEM] * 2,
    )(*buffer, factor, *square)


def product_kernel(first, scaled, me_ref, *refs):
    before, refs = ((), refs) if first else (refs[:1], refs[1:])
    up, up_more, down, down_more, high_ref, low_ref, keep_ref, give_ref, left_ref, plain_ref, turned_ref, pair_ref = refs
    rows = down.shape[0]
    top, bottom = up[:rows, :] + up_more[:rows, :], down[...] + down_more[...]
    if scaled:
        total = up[rows:rows + 1, :] + up_more[rows:rows + 1, :]
        scale = 1.0 / jnp.sqrt(total / F32(D) + F32(1e-06))
        top, bottom = top * scale, bottom * scale
    left_ref[:rows, :] = top
    left_ref[rows:, :] = bottom
    plain_ref[:, :rows] = top.T
    plain_ref[:, rows:] = bottom.T
    me = me_ref[0]
    for b in range(4):
        block = plain_ref[pl.ds(pl.multiple_of((me ^ b) * PART, PART), PART), :]
        turned_ref[PART * b:PART * (b + 1), :] = block
        pair_ref[PART * b:PART * (b + 1), :], pair_ref[HALF + PART * b:HALF + PART * (b + 1), :] = split(block)
    spot = 0
    for ref in (*before, left_ref):
        gram = dot(turned_ref[...], ref[...], precision=HIGHEST)
        keep_ref[:, spot:spot + HALF] = gram[:QUARTER]
        give_ref[:, spot:spot + HALF] = gram[QUARTER:]
        spot += HALF
    step = 2 * TILE
    for c in range(high_ref.shape[1] // step):
        lanes = pl.ds(c * step, step)
        both = dot(pair_ref[...], high_ref[:, lanes])
        part = (both[:HALF] + both[HALF:]) + dot(pair_ref[:HALF, :], low_ref[:, lanes])
        lanes = pl.ds(spot + c * step, step)
        keep_ref[:, lanes] = part[:QUARTER]
        give_ref[:, lanes] = part[QUARTER:]


def product(scaled, me, before, parts, buffer):
    rows, cols = buffer[0].shape
    width = HALF * (len(before) + 1) + cols
    return call(
        functools.partial(product_kernel, not before, scaled), "product", 4 * rows * width * RANK, 4 * rows * width,
        out_shape=[shaped(QUARTER, width)] * 2 + [shaped(rows, HALF)],
        in_specs=[SMEM] + [VMEM] * (6 + len(before)), out_specs=[VMEM] * 3,
        scratch_shapes=[pltpu.VMEM((HALF, rows), F32)] * 2 + [pltpu.VMEM((RANK, rows), BF16)],
    )(me, *before, *parts, *buffer)


def solved(inverse, wide_ref, out_ref, pair_ref):
    inverse = split(inverse)
    square = jnp.zeros((HALF, 1), F32)
    step = 2 * TILE
    for c in range(wide_ref.shape[1] // step):
        lanes = pl.ds(step * c, step)
        part = dot3(inverse, split(wide_ref[:, lanes]))
        out_ref[:, lanes] = part
        pair_ref[:HALF, lanes], pair_ref[HALF:, lanes] = split(part)
        square = square + jnp.sum(part * part, axis=1, keepdims=True)
    return jnp.broadcast_to(square, (HALF, HALF)).T[:SUB, :]


def first_kernel(me_ref, mine_ref, other_ref, inverse_ref, wide_ref, out_ref, pair_ref, square_ref, gram_ref):
    me = me_ref[0]
    place(gram_ref, me, mine_ref[:, :HALF], other_ref[:, :HALF])
    place(wide_ref, me, mine_ref[:, HALF:], other_ref[:, HALF:])
    inverse_ref[...] = inverse_factor(gram_ref[...])
    square_ref[...] = solved(inverse_ref[...], wide_ref, out_ref, pair_ref)


def first_solve(me, mine, other):
    cols = mine.shape[1] - HALF
    return call(
        first_kernel, "first_solve", 5_000_000_000, 20 * HALF * cols,
        out_shape=[shaped(HALF, HALF), shaped(HALF, cols), shaped(HALF, cols), shaped(RANK, cols, dtype=BF16), shaped(SUB, HALF)],
        in_specs=[SMEM, VMEM, VMEM], out_specs=[VMEM] * 5, scratch_shapes=[pltpu.VMEM((HALF, HALF), F32)],
    )(me, mine, other)


def second_kernel(me_ref, mine_ref, other_ref, first_ref, wide0_ref, inverse_ref, out_ref, pair_ref, square_ref, gram_ref, wide_ref):
    me = me_ref[0]
    place(gram_ref, me, mine_ref[:, :RANK], other_ref[:, :RANK])
    place(wide_ref.at[HALF:, :], me, mine_ref[:, RANK:], other_ref[:, RANK:])
    wide_ref[:HALF, :] = wide0_ref[...]
    first = first_ref[...]
    side = dot(gram_ref[:, :HALF], first, NT, HIGHEST)
    second = inverse_factor(gram_ref[:, HALF:] - dot(side, side, NT, HIGHEST))
    inverse_ref[:HALF, :HALF] = first
    inverse_ref[:HALF, HALF:] = jnp.zeros((HALF, HALF), F32)
    inverse_ref[HALF:, :HALF] = -dot(second, dot(side, first, precision=HIGHEST), precision=HIGHEST)
    inverse_ref[HALF:, HALF:] = second
    square_ref[...] = solved(inverse_ref[HALF:, :], wide_ref, out_ref, pair_ref)


def second_solve(me, mine, other, first, wide0):
    cols = mine.shape[1] - RANK
    return call(
        second_kernel, "second_solve", 6_000_000_000, 20 * HALF * cols,
        out_shape=[shaped(RANK, RANK), shaped(HALF, cols), shaped(RANK, cols, dtype=BF16), shaped(SUB, HALF)],
        in_specs=[SMEM] + [VMEM] * 4, out_specs=[VMEM] * 4,
        scratch_shapes=[pltpu.VMEM((HALF, RANK), F32), pltpu.VMEM((RANK, cols), F32)],
    )(me, mine, other, first, wide0)


def ortho_kernel(left0_ref, left1_ref, inverse_ref, out_ref):
    left = jnp.concatenate([left0_ref[...], left1_ref[...]], axis=1)
    out_ref[...] = dot3(split(left), split(inverse_ref[...]), NT)


def ortho_product(left0, left1, inverse):
    rows = left0.shape[0]
    return call(
        ortho_kernel, "ortho", 6 * rows * RANK * RANK, 8 * rows * RANK,
        out_shape=shaped(rows, RANK), in_specs=[VMEM] * 3, out_specs=VMEM,
    )(left0, left1, inverse)


def update_kernel(ortho_ref, s0, s1, s2, s3, pair0_ref, pair1_ref, factor0_ref, factor1_ref, high_ref, low_ref, weight_ref, *refs):
    momentum_ref, out_ref, basis_ref, half_ref, triple_ref = refs
    total = (s0[0:1, :] + s1[0:1, :]) + (s2[0:1, :] + s3[0:1, :])
    scale = 1.0 / jnp.sqrt(total / F32(D) + F32(1e-06))
    step, width = pl.program_id(0), out_ref.shape[1]

    @pl.when(step == 0)
    def _():
        half_ref[...] = (F32(1.0 - beta_mom) * ortho_ref[...]).astype(BF16)
        high, low = split(ortho_ref[...] * (scale * F32(learn_rate * (D / RANK) ** 0.5)))
        triple_ref[:, :RANK] = high
        triple_ref[:, RANK:2 * RANK] = low
        triple_ref[:, 2 * RANK:] = high

    lanes = pl.ds(pl.multiple_of(step * width, width), width)
    high = [pair0_ref[:HALF, lanes], pair1_ref[:HALF, lanes]]
    feedback = dot(half_ref[...], jnp.concatenate(high, axis=0))
    momentum_ref[...] = (high_ref[:, lanes].astype(F32) + low_ref[:, lanes].astype(F32)) - feedback
    factor = jnp.concatenate([*high, *high, pair0_ref[HALF:, lanes], pair1_ref[HALF:, lanes]], axis=0)
    out_ref[...] = weight_ref[:, lanes] - dot(triple_ref[...], factor)
    basis_ref[:, :HALF] = factor0_ref[:, lanes].T * scale[:, :HALF]
    basis_ref[:, HALF:] = factor1_ref[:, lanes].T * scale[:, HALF:]


def update(ortho, squares, pairs, factors, buffer, weight):
    rows, cols = weight.shape
    tall = pl.BlockSpec((rows, TILE), lambda i: (0, i))
    return call(
        update_kernel, "update", 8 * rows * cols * RANK, 8 * rows * cols,
        out_shape=[shaped(rows, cols)] * 2 + [shaped(cols, RANK)], grid=(cols // TILE,), in_specs=[VMEM] * 12,
        out_specs=[tall, tall, pl.BlockSpec((TILE, RANK), lambda i: (i, 0))],
        scratch_shapes=[pltpu.VMEM((rows, RANK), BF16), pltpu.VMEM((rows, 3 * RANK), BF16)],
    )(ortho, *squares, *pairs, *factors, *buffer, weight)


def swap(x, axis, bit):
    size = lax.axis_size(axis)
    return lax.ppermute(x, axis, [(i, i ^ bit) for i in range(size)])


def together(*arrays):
    return lax.optimization_barrier(arrays)


def tuned(momentum, gradient, weight, right_basis):
    row = lax.axis_index("row")
    me = (2 * (row & 1) + ((row >> 1) & 1)).astype(jnp.int32)[None]
    high, low, up0, down0, second = start(me, momentum[0], gradient[0], right_basis)
    buffer = (high, low)
    got0 = swap(up0, "col", 1), swap(down0, "col", 2)
    up1, down1 = left_product(buffer, second, dims=NN)
    up0, down0, got0, up1, down1 = together(up0, down0, got0, up1, down1)
    for sweep in range(ITERS):
        last, scaled = sweep == ITERS - 1, sweep > 0

        up0, down0 = up0 + got0[0], down0 + got0[1]
        got0 = swap(up0, "col", 2), swap(down0, "col", 1)
        if sweep:
            up1, down1 = left_product(buffer, split1, square1)
        up0, down0, got0, up1, down1 = together(up0, down0, got0, up1, down1)

        keep0, give0, left0 = product(scaled, me, (), (up0, got0[0], down0, got0[1]), buffer)
        got1 = swap(up1, "col", 1), swap(down1, "col", 2)
        keep0, give0, left0, up1, down1, got1 = together(keep0, give0, left0, up1, down1, got1)

        part0 = keep0 + swap(give0, "row", 1)
        pair0 = swap(part0[PART:], "row", 2)
        up1, down1 = up1 + got1[0], down1 + got1[1]
        got1 = swap(up1, "col", 2), swap(down1, "col", 1)
        keep1, give1, left1 = product(scaled, me, (left0,), (up1, got1[0], down1, got1[1]), buffer)
        part0, pair0, keep1, give1 = together(part0, pair0, keep1, give1)

        core1 = swap(give1, "row", 1)
        part0, pair0, keep1, core1 = together(part0, pair0, keep1, core1)

        side0 = part0[:PART] + pair0
        cross0 = swap(side0, "row", 4)
        part1 = keep1 + core1
        pair1 = swap(part1[PART:], "row", 2)
        side0, cross0, part1, pair1 = together(side0, cross0, part1, pair1)

        total0 = side0 + cross0
        back0 = swap(total0, "row", 2)
        side1 = part1[:PART] + pair1
        cross1 = swap(side1, "row", 4)
        total0, back0, side1, cross1 = together(total0, back0, side1, cross1)

        mine0 = jnp.concatenate([total0, back0], axis=0)
        other0 = swap(mine0, "row", 1)
        total1 = side1 + cross1
        back1 = swap(total1, "row", 2)
        first, wide, factor0, split0, square0 = first_solve(me, mine0, other0)
        if not last:
            up0, down0 = left_product(buffer, split0, square0)
        total1, back1, first, wide, split0, square0, up0, down0 = together(total1, back1, first, wide, split0, square0, up0, down0)

        mine1 = jnp.concatenate([total1, back1], axis=0)
        other1 = swap(mine1, "row", 1)
        if not last:
            got0 = swap(up0, "col", 1), swap(down0, "col", 2)
        inverse, factor1, split1, square1 = second_solve(me, mine1, other1, first, wide)
        if not last:
            up0, down0, got0, split1, square1 = together(up0, down0, got0, split1, square1)

    square = jnp.concatenate([square0, square1], axis=1)
    squares = (square, swap(square, "col", 1), swap(square, "col", 2), swap(square, "col", 3))
    ortho = ortho_product(left0, left1, inverse)
    squares = together(*squares, ortho)[:4]
    new_momentum, new_weight, new_basis = update(ortho, squares, (split0, split1), (factor0, factor1), buffer, weight)
    return new_momentum[None], new_weight, new_basis


def general(momentum, gradient, weight, right_basis):
    replicas = lax.axis_size("rep")
    buffer = momentum[0] + gradient[0].astype(F32)
    basis, dims = right_basis, NN
    for sweep in range(ITERS):
        left = lax.psum(dot(buffer, basis, dims, HIGH) / replicas, ("col", "rep"))
        if sweep:
            left = left / rms
        gram = lax.psum(dot(left, left, ((0,), (0,)), HIGHEST), "row")
        wide = lax.psum(dot(left, buffer, ((0,), (0,)), HIGH) / replicas, ("row", "rep"))
        inverse = inverse_cholesky(gram)
        factor = dot(inverse, wide, precision=HIGHEST)
        rms = jnp.sqrt(lax.psum(jnp.sum(factor * factor, axis=1)[None, :], "col") / F32(D) + 1e-06)
        basis, dims = factor, NT
    ortho = dot(left, inverse, NT, HIGHEST)
    new_momentum = (buffer - (1.0 - beta_mom) * dot(ortho, factor, precision=HIGH))[None]
    basis = factor / rms.T
    new_weight = weight - learn_rate * jnp.sqrt(F32(D) / F32(RANK)) * dot(ortho, basis, precision=HIGH)
    return new_momentum, new_weight, basis.T


def solution(mesh):
    sizes = dict(mesh.shape)
    fits = sizes["row"] == 8 and sizes["col"] == 4 and sizes["rep"] == 1
    return jax.shard_map(
        tuned if fits else general,
        mesh=mesh,
        in_specs=(P("rep", "row", "col"), P("rep", "row", "col"), P("row", "col"), P("col", None)),
        out_specs=(P("rep", "row", "col"), P("row", "col"), P("col", None)),
        check_vma=False,
    )
```

```python
import functools

import jax
import jax.numpy as jnp
from jax import lax
from jax.experimental import pallas as pl
from jax.experimental.pallas import tpu as pltpu
from jax.sharding import PartitionSpec as P

D = 8192
RANK = 256
ITERS = 2
HALF = RANK // 2
QUARTER = RANK // 4
PART = RANK // 8
SUB = 8
TILE = 256
STEP = 512

beta_mom = 0.95
learn_rate = 0.05

F32 = jnp.float32
BF16 = jnp.bfloat16
HIGHEST = lax.Precision.HIGHEST
HIGH = lax.Precision.HIGH
NT = ((1,), (1,))
NN = ((1,), (0,))


def dot(a, b, dims=NN, precision=None):
    return lax.dot_general(a, b, (dims, ((), ())), precision=precision, preferred_element_type=F32)


def split(x):
    high = x.astype(BF16)
    return high, (x - high.astype(F32)).astype(BF16)


def dot3(a, b, dims=NN):
    return dot(a[0], b[0], dims) + (dot(a[1], b[0], dims) + dot(a[0], b[1], dims))


def call(kernel, name, flops, moved, **rest):
    rest.setdefault("compiler_params", pltpu.CompilerParams(vmem_limit_bytes=24 * 2**20))
    return pl.pallas_call(
        kernel,
        name=name,
        cost_estimate=pl.CostEstimate(flops=flops, bytes_accessed=moved, transcendentals=0),
        **rest,
    )


def shaped(*shape, dtype=F32):
    return jax.ShapeDtypeStruct(shape, dtype)


VMEM = pl.BlockSpec(memory_space=pltpu.VMEM)
HBM = pl.BlockSpec(memory_space=pltpu.HBM)
SMEM = pl.BlockSpec(memory_space=pltpu.SMEM)


def inverse_factor(block):
    shape = (SUB, HALF)
    lanes = lax.broadcasted_iota(jnp.int32, shape, 1)
    subs = lax.broadcasted_iota(jnp.int32, shape, 0)
    count = HALF // SUB

    def spread(tile, lane):
        return jnp.broadcast_to(tile[:, lane:lane + 1], shape)

    def repeat(tile, sub):
        return jnp.broadcast_to(tile[sub:sub + 1, :], shape)

    tiles = [block[SUB * i:SUB * (i + 1), :] for i in range(count)]
    for t in range(count):
        low = SUB * t
        panel = jnp.logical_and(lanes >= low, lanes < low + SUB)
        cols = [spread(tiles[t], low + j) for j in range(SUB)]
        tile = jnp.where(panel, 0.0, tiles[t])
        scale, rows, upper = [], [], {}
        for j in range(SUB):
            r = lax.rsqrt(repeat(cols[j], j))
            mult = jnp.where(subs > j, cols[j] * r, 0.0)
            for k in range(j + 1, SUB):
                upper[j, k] = repeat(cols[k], j) * r
                cols[k] = cols[k] - mult * upper[j, k]
            row = jnp.where(lanes == low + j, r, repeat(tile, j) * r)
            tile = jnp.where(subs == j, row, tile - mult * row)
            scale.append(r)
            rows.append(row)
        tiles[t] = tile
        for i in range(t + 1, count):
            cols = [spread(tiles[i], low + j) for j in range(SUB)]
            tile = jnp.where(panel, 0.0, tiles[i])
            for j in range(SUB):
                mult = cols[j] * scale[j]
                for k in range(j + 1, SUB):
                    cols[k] = cols[k] - mult * upper[j, k]
                tile = tile - mult * rows[j]
            tiles[i] = tile
    full = jnp.concatenate(tiles, axis=0)
    down = lax.broadcasted_iota(jnp.int32, (HALF, HALF), 0)
    across = lax.broadcasted_iota(jnp.int32, (HALF, HALF), 1)
    return jnp.where(across <= down, full, 0.0)


def inverse_body(gram_ref, out_ref):
    first = inverse_factor(gram_ref[:HALF, :HALF])
    side = dot(gram_ref[HALF:, :HALF], first, NT, HIGHEST)
    rest = gram_ref[HALF:, HALF:] - dot(side, side, NT, HIGHEST)
    second = inverse_factor(rest)
    out_ref[:HALF, :HALF] = first
    out_ref[:HALF, HALF:] = jnp.zeros((HALF, HALF), F32)
    out_ref[HALF:, :HALF] = -dot(second, dot(side, first, precision=HIGHEST), precision=HIGHEST)
    out_ref[HALF:, HALF:] = second


def inverse_cholesky(gram):
    return call(
        inverse_body, "inverse_cholesky", 12_000_000_000, 2 * 4 * RANK * RANK,
        out_shape=shaped(RANK, RANK), in_specs=[VMEM], out_specs=VMEM,
    )(gram)


def place(out_ref, me, mine, other):
    for b in range(4):
        block = (mine, other)[b // 2][PART * (b % 2):PART * (b % 2 + 1), :]
        out_ref[pl.ds(pl.multiple_of((me ^ b) * PART, PART), PART), :] = block


def start_kernel(me_ref, momentum_ref, gradient_ref, basis_ref, high_ref, low_ref, up_ref, down_ref, second_ref):
    rows, cols = momentum_ref.shape
    half = rows // 2

    def body(momentum, gradient, basis):
        step = pl.program_id(0)
        here = pl.ds(pl.multiple_of(step * STEP, STEP), STEP)
        bhigh, blow = split(basis[...])
        second_ref[here, :HALF], second_ref[here, HALF:] = bhigh[:, HALF:], blow[:, HALF:]
        high, low = split(momentum[...] + gradient[...].astype(F32))
        high_ref[:, here], low_ref[:, here] = high, low
        both = dot(high, jnp.concatenate([bhigh[:, :HALF], blow[:, :HALF]], axis=1))
        part = (both[:, :HALF] + both[:, HALF:]) + dot(low, bhigh[:, :HALF])

        @pl.when(step == 0)
        def _():
            up_ref[...] = part[:half]
            down_ref[...] = part[half:]

        @pl.when(step > 0)
        def _():
            up_ref[...] += part[:half]
            down_ref[...] += part[half:]

    block = pl.BlockSpec((rows, STEP), lambda i: (0, i))
    pltpu.emit_pipeline(
        body, grid=(cols // STEP,), in_specs=[block, block, pl.BlockSpec((STEP, RANK), lambda i: (i, 0))],
    )(momentum_ref, gradient_ref, basis_ref)


def start(me, *args):
    rows, cols = args[0].shape
    return call(
        start_kernel, "start", 4 * rows * cols * RANK, 6 * rows * cols,
        out_shape=[pltpu.VMEM((rows, cols), BF16)] * 2 + [shaped(rows // 2, HALF)] * 2 + [shaped(cols, RANK, dtype=BF16)],
        in_specs=[SMEM] + [HBM] * 3, out_specs=[VMEM] * 5,
    )(me, *(pltpu.with_memory_space_constraint(x, pltpu.HBM) for x in args))


def left_kernel(dims, high_ref, low_ref, factor_ref, *refs):
    up_ref, down_ref = refs[-2:]
    half = down_ref.shape[0]

    @pl.loop(0, 2 * half // TILE)
    def _(c):
        here = pl.ds(pl.multiple_of(c * TILE, TILE), TILE)
        both = dot(high_ref[here, :], factor_ref[...], dims)
        fhigh = factor_ref[:HALF, :] if dims == NT else factor_ref[:, :HALF]
        part = (both[:, :HALF] + both[:, HALF:]) + dot(low_ref[here, :], fhigh, dims)
        there = pl.ds(pl.multiple_of(lax.rem(c * TILE, half), TILE), TILE)

        @pl.when(c < half // TILE)
        def _():
            up_ref[there, :] = part

        @pl.when(c >= half // TILE)
        def _():
            down_ref[there, :] = part

    if len(refs) == 3:
        up_ref[half:, :] = refs[0][...]


def left_product(buffer, factor, *square, dims=NT):
    rows, cols = buffer[0].shape
    return call(
        functools.partial(left_kernel, dims), "left", 0, 4 * rows * cols,
        out_shape=[shaped(rows // 2 + SUB * len(square), HALF), shaped(rows // 2, HALF)],
        in_specs=[VMEM] * (3 + len(square)), out_specs=[VMEM] * 2,
    )(*buffer, factor, *square)


def product_kernel(first, scaled, me_ref, *refs):
    before, refs = ((), refs) if first else (refs[:1], refs[1:])
    up, up_more, down, down_more, high_ref, low_ref, keep_ref, give_ref, left_ref, plain_ref, turned_ref, pair_ref = refs
    rows = down.shape[0]
    top, bottom = up[:rows, :] + up_more[:rows, :], down[...] + down_more[...]
    if scaled:
        total = up[rows:rows + 1, :] + up_more[rows:rows + 1, :]
        scale = 1.0 / jnp.sqrt(total / F32(D) + F32(1e-06))
        top, bottom = top * scale, bottom * scale
    left_ref[:rows, :] = top
    left_ref[rows:, :] = bottom
    plain_ref[:, :rows] = top.T
    plain_ref[:, rows:] = bottom.T
    me = me_ref[0]
    for b in range(4):
        block = plain_ref[pl.ds(pl.multiple_of((me ^ b) * PART, PART), PART), :]
        turned_ref[PART * b:PART * (b + 1), :] = block
        pair_ref[PART * b:PART * (b + 1), :], pair_ref[HALF + PART * b:HALF + PART * (b + 1), :] = split(block)
    spot = 0
    for ref in (*before, left_ref):
        gram = dot(turned_ref[...], ref[...], precision=HIGHEST)
        keep_ref[:, spot:spot + HALF] = gram[:QUARTER]
        give_ref[:, spot:spot + HALF] = gram[QUARTER:]
        spot += HALF
    step = 2 * TILE
    for c in range(high_ref.shape[1] // step):
        lanes = pl.ds(c * step, step)
        both = dot(pair_ref[...], high_ref[:, lanes])
        part = (both[:HALF] + both[HALF:]) + dot(pair_ref[:HALF, :], low_ref[:, lanes])
        lanes = pl.ds(spot + c * step, step)
        keep_ref[:, lanes] = part[:QUARTER]
        give_ref[:, lanes] = part[QUARTER:]


def product(scaled, me, before, parts, buffer):
    rows, cols = buffer[0].shape
    width = HALF * (len(before) + 1) + cols
    return call(
        functools.partial(product_kernel, not before, scaled), "product", 4 * rows * width * RANK, 4 * rows * width,
        out_shape=[shaped(QUARTER, width)] * 2 + [shaped(rows, HALF)],
        in_specs=[SMEM] + [VMEM] * (6 + len(before)), out_specs=[VMEM] * 3,
        scratch_shapes=[pltpu.VMEM((HALF, rows), F32)] * 2 + [pltpu.VMEM((RANK, rows), BF16)],
    )(me, *before, *parts, *buffer)


def solved(inverse, wide_ref, out_ref, pair_ref):
    inverse = split(inverse)
    square = jnp.zeros((HALF, 1), F32)
    step = 2 * TILE
    for c in range(wide_ref.shape[1] // step):
        lanes = pl.ds(step * c, step)
        part = dot3(inverse, split(wide_ref[:, lanes]))
        out_ref[:, lanes] = part
        pair_ref[:HALF, lanes], pair_ref[HALF:, lanes] = split(part)
        square = square + jnp.sum(part * part, axis=1, keepdims=True)
    return jnp.broadcast_to(square, (HALF, HALF)).T[:SUB, :]


def first_kernel(me_ref, mine_ref, other_ref, inverse_ref, wide_ref, out_ref, pair_ref, square_ref, gram_ref):
    me = me_ref[0]
    place(gram_ref, me, mine_ref[:, :HALF], other_ref[:, :HALF])
    place(wide_ref, me, mine_ref[:, HALF:], other_ref[:, HALF:])
    inverse_ref[...] = inverse_factor(gram_ref[...])
    square_ref[...] = solved(inverse_ref[...], wide_ref, out_ref, pair_ref)


def first_solve(me, mine, other):
    cols = mine.shape[1] - HALF
    return call(
        first_kernel, "first_solve", 5_000_000_000, 20 * HALF * cols,
        out_shape=[shaped(HALF, HALF), shaped(HALF, cols), shaped(HALF, cols), shaped(RANK, cols, dtype=BF16), shaped(SUB, HALF)],
        in_specs=[SMEM, VMEM, VMEM], out_specs=[VMEM] * 5, scratch_shapes=[pltpu.VMEM((HALF, HALF), F32)],
    )(me, mine, other)


def second_kernel(me_ref, mine_ref, other_ref, first_ref, wide0_ref, inverse_ref, out_ref, pair_ref, square_ref, gram_ref, wide_ref):
    me = me_ref[0]
    place(gram_ref, me, mine_ref[:, :RANK], other_ref[:, :RANK])
    place(wide_ref.at[HALF:, :], me, mine_ref[:, RANK:], other_ref[:, RANK:])
    wide_ref[:HALF, :] = wide0_ref[...]
    first = first_ref[...]
    side = dot(gram_ref[:, :HALF], first, NT, HIGHEST)
    second = inverse_factor(gram_ref[:, HALF:] - dot(side, side, NT, HIGHEST))
    inverse_ref[:HALF, :HALF] = first
    inverse_ref[:HALF, HALF:] = jnp.zeros((HALF, HALF), F32)
    inverse_ref[HALF:, :HALF] = -dot(second, dot(side, first, precision=HIGHEST), precision=HIGHEST)
    inverse_ref[HALF:, HALF:] = second
    square_ref[...] = solved(inverse_ref[HALF:, :], wide_ref, out_ref, pair_ref)


def second_solve(me, mine, other, first, wide0):
    cols = mine.shape[1] - RANK
    return call(
        second_kernel, "second_solve", 6_000_000_000, 20 * HALF * cols,
        out_shape=[shaped(RANK, RANK), shaped(HALF, cols), shaped(RANK, cols, dtype=BF16), shaped(SUB, HALF)],
        in_specs=[SMEM] + [VMEM] * 4, out_specs=[VMEM] * 4,
        scratch_shapes=[pltpu.VMEM((HALF, RANK), F32), pltpu.VMEM((RANK, cols), F32)],
    )(me, mine, other, first, wide0)


def ortho_kernel(left0_ref, left1_ref, inverse_ref, out_ref):
    left = jnp.concatenate([left0_ref[...], left1_ref[...]], axis=1)
    out_ref[...] = dot3(split(left), split(inverse_ref[...]), NT)


def ortho_product(left0, left1, inverse):
    rows = left0.shape[0]
    return call(
        ortho_kernel, "ortho", 6 * rows * RANK * RANK, 8 * rows * RANK,
        out_shape=shaped(rows, RANK), in_specs=[VMEM] * 3, out_specs=VMEM,
    )(left0, left1, inverse)


def update_kernel(ortho_ref, s0, s1, pair0_ref, pair1_ref, factor0_ref, factor1_ref, high_ref, low_ref, weight_ref, *refs):
    momentum_ref, out_ref, basis_ref, half_ref, triple_ref = refs
    total = s0[0:1, :] + s1[0:1, :]
    scale = 1.0 / jnp.sqrt(total / F32(D) + F32(1e-06))
    step, width = pl.program_id(0), out_ref.shape[1]

    @pl.when(step == 0)
    def _():
        half_ref[...] = (F32(1.0 - beta_mom) * ortho_ref[...]).astype(BF16)
        high, low = split(ortho_ref[...] * (scale * F32(learn_rate * (D / RANK) ** 0.5)))
        triple_ref[:, :RANK] = high
        triple_ref[:, RANK:2 * RANK] = low
        triple_ref[:, 2 * RANK:] = high

    lanes = pl.ds(pl.multiple_of(step * width, width), width)
    high = [pair0_ref[:HALF, lanes], pair1_ref[:HALF, lanes]]
    feedback = dot(half_ref[...], jnp.concatenate(high, axis=0))
    momentum_ref[...] = (high_ref[:, lanes].astype(F32) + low_ref[:, lanes].astype(F32)) - feedback
    factor = jnp.concatenate([*high, *high, pair0_ref[HALF:, lanes], pair1_ref[HALF:, lanes]], axis=0)
    out_ref[...] = weight_ref[:, lanes] - dot(triple_ref[...], factor)
    basis_ref[:, :HALF] = factor0_ref[:, lanes].T * scale[:, :HALF]
    basis_ref[:, HALF:] = factor1_ref[:, lanes].T * scale[:, HALF:]


def update(ortho, squares, pairs, factors, buffer, weight):
    rows, cols = weight.shape
    tall = pl.BlockSpec((rows, TILE), lambda i: (0, i))
    return call(
        update_kernel, "update", 8 * rows * cols * RANK, 8 * rows * cols,
        out_shape=[shaped(rows, cols)] * 2 + [shaped(cols, RANK)], grid=(cols // TILE,), in_specs=[VMEM] * 10,
        out_specs=[tall, tall, pl.BlockSpec((TILE, RANK), lambda i: (i, 0))],
        scratch_shapes=[pltpu.VMEM((rows, RANK), BF16), pltpu.VMEM((rows, 3 * RANK), BF16)],
    )(ortho, *squares, *pairs, *factors, *buffer, weight)


def swap(x, axis, bit):
    size = lax.axis_size(axis)
    return lax.ppermute(x, axis, [(i, i ^ bit) for i in range(size)])


def together(*arrays):
    return lax.optimization_barrier(arrays)


def tuned(momentum, gradient, weight, right_basis):
    row = lax.axis_index("row")
    me = (2 * (row & 1) + ((row >> 1) & 1)).astype(jnp.int32)[None]
    high, low, up0, down0, second = start(me, momentum[0], gradient[0], right_basis)
    buffer = (high, low)
    got0 = swap(up0, "col", 1), swap(down0, "col", 2)
    up1, down1 = left_product(buffer, second, dims=NN)
    up0, down0, got0, up1, down1 = together(up0, down0, got0, up1, down1)
    for sweep in range(ITERS):
        last, scaled = sweep == ITERS - 1, sweep > 0

        up0, down0 = up0 + got0[0], down0 + got0[1]
        got0 = swap(up0, "col", 2), swap(down0, "col", 1)
        if sweep:
            up1, down1 = left_product(buffer, split1, square1)
        up0, down0, got0, up1, down1 = together(up0, down0, got0, up1, down1)

        keep0, give0, left0 = product(scaled, me, (), (up0, got0[0], down0, got0[1]), buffer)
        got1 = swap(up1, "col", 1), swap(down1, "col", 2)
        keep0, give0, left0, up1, down1, got1 = together(keep0, give0, left0, up1, down1, got1)

        part0 = keep0 + swap(give0, "row", 1)
        pair0 = swap(part0[PART:], "row", 2)
        up1, down1 = up1 + got1[0], down1 + got1[1]
        got1 = swap(up1, "col", 2), swap(down1, "col", 1)
        keep1, give1, left1 = product(scaled, me, (left0,), (up1, got1[0], down1, got1[1]), buffer)
        part0, pair0, keep1, give1 = together(part0, pair0, keep1, give1)

        side0 = part0[:PART] + pair0
        cross0 = swap(side0, "row", 4)
        part1 = keep1 + swap(give1, "row", 1)
        pair1 = [swap(part1[rows], "row", 2) for rows in (slice(PART, PART + PART // 2), slice(PART + PART // 2, None))]
        side0, cross0, part1, pair1 = together(side0, cross0, part1, pair1)

        total0 = side0 + cross0
        back0 = swap(total0, "row", 2)
        side1 = part1[:PART] + jnp.concatenate(pair1, axis=0)
        cross1 = swap(side1, "row", 4)
        total0, back0, side1, cross1 = together(total0, back0, side1, cross1)

        mine0 = jnp.concatenate([total0, back0], axis=0)
        other0 = swap(mine0, "row", 1)
        total1 = side1 + cross1
        back1 = swap(total1, "row", 2)
        first, wide, factor0, split0, square0 = first_solve(me, mine0, other0)
        if not last:
            up0, down0 = left_product(buffer, split0, square0)
        total1, back1, first, wide, split0, square0, up0, down0 = together(total1, back1, first, wide, split0, square0, up0, down0)

        mine1 = jnp.concatenate([total1, back1], axis=0)
        other1 = swap(mine1, "row", 1)
        if not last:
            got0 = swap(up0, "col", 1), swap(down0, "col", 2)
        inverse, factor1, split1, square1 = second_solve(me, mine1, other1, first, wide)
        if not last:
            up0, down0, got0, split1, square1 = together(up0, down0, got0, split1, square1)

    square = jnp.concatenate([square0, square1], axis=1)
    other = swap(square, "col", 1)
    ortho = ortho_product(left0, left1, inverse)
    square, other, ortho = together(square, other, ortho)
    square = square + other
    new_momentum, new_weight, new_basis = update(ortho, (square, swap(square, "col", 2)), (split0, split1), (factor0, factor1), buffer, weight)
    return new_momentum[None], new_weight, new_basis


def general(momentum, gradient, weight, right_basis):
    replicas = lax.axis_size("rep")
    buffer = momentum[0] + gradient[0].astype(F32)
    basis, dims = right_basis, NN
    for sweep in range(ITERS):
        left = lax.psum(dot(buffer, basis, dims, HIGH) / replicas, ("col", "rep"))
        if sweep:
            left = left / rms
        gram = lax.psum(dot(left, left, ((0,), (0,)), HIGHEST), "row")
        wide = lax.psum(dot(left, buffer, ((0,), (0,)), HIGH) / replicas, ("row", "rep"))
        inverse = inverse_cholesky(gram)
        factor = dot(inverse, wide, precision=HIGHEST)
        rms = jnp.sqrt(lax.psum(jnp.sum(factor * factor, axis=1)[None, :], "col") / F32(D) + 1e-06)
        basis, dims = factor, NT
    ortho = dot(left, inverse, NT, HIGHEST)
    new_momentum = (buffer - (1.0 - beta_mom) * dot(ortho, factor, precision=HIGH))[None]
    basis = factor / rms.T
    new_weight = weight - learn_rate * jnp.sqrt(F32(D) / F32(RANK)) * dot(ortho, basis, precision=HIGH)
    return new_momentum, new_weight, basis.T


def solution(mesh):
    sizes = dict(mesh.shape)
    fits = sizes["row"] == 8 and sizes["col"] == 4 and sizes["rep"] == 1
    return jax.shard_map(
        tuned if fits else general,
        mesh=mesh,
        in_specs=(P("rep", "row", "col"), P("rep", "row", "col"), P("row", "col"), P("col", None)),
        out_specs=(P("rep", "row", "col"), P("row", "col"), P("col", None)),
        check_vma=False,
    )
```

```python
import functools

import jax
import jax.numpy as jnp
from jax import lax
from jax.experimental import pallas as pl
from jax.experimental.pallas import tpu as pltpu
from jax.sharding import PartitionSpec as P

D = 8192
RANK = 256
ITERS = 2
HALF = RANK // 2
QUARTER = RANK // 4
PART = RANK // 8
SUB = 8
TILE = 256
STEP = 512

beta_mom = 0.95
learn_rate = 0.05

F32 = jnp.float32
BF16 = jnp.bfloat16
HIGHEST = lax.Precision.HIGHEST
HIGH = lax.Precision.HIGH
NT = ((1,), (1,))
NN = ((1,), (0,))


def dot(a, b, dims=NN, precision=None):
    return lax.dot_general(a, b, (dims, ((), ())), precision=precision, preferred_element_type=F32)


def split(x):
    high = x.astype(BF16)
    return high, (x - high.astype(F32)).astype(BF16)


def dot3(a, b, dims=NN):
    return dot(a[0], b[0], dims) + (dot(a[1], b[0], dims) + dot(a[0], b[1], dims))


def call(kernel, name, flops, moved, **rest):
    rest.setdefault("compiler_params", pltpu.CompilerParams(vmem_limit_bytes=24 * 2**20))
    return pl.pallas_call(
        kernel,
        name=name,
        cost_estimate=pl.CostEstimate(flops=flops, bytes_accessed=moved, transcendentals=0),
        **rest,
    )


def shaped(*shape, dtype=F32):
    return jax.ShapeDtypeStruct(shape, dtype)


VMEM = pl.BlockSpec(memory_space=pltpu.VMEM)
HBM = pl.BlockSpec(memory_space=pltpu.HBM)
SMEM = pl.BlockSpec(memory_space=pltpu.SMEM)


def inverse_factor(block):
    shape = (SUB, HALF)
    lanes = lax.broadcasted_iota(jnp.int32, shape, 1)
    subs = lax.broadcasted_iota(jnp.int32, shape, 0)
    count = HALF // SUB

    def spread(tile, lane):
        return jnp.broadcast_to(tile[:, lane:lane + 1], shape)

    def repeat(tile, sub):
        return jnp.broadcast_to(tile[sub:sub + 1, :], shape)

    tiles = [block[SUB * i:SUB * (i + 1), :] for i in range(count)]
    for t in range(count):
        low = SUB * t
        panel = jnp.logical_and(lanes >= low, lanes < low + SUB)
        cols = [spread(tiles[t], low + j) for j in range(SUB)]
        tile = jnp.where(panel, 0.0, tiles[t])
        scale, rows, upper = [], [], {}
        for j in range(SUB):
            r = lax.rsqrt(repeat(cols[j], j))
            mult = jnp.where(subs > j, cols[j] * r, 0.0)
            for k in range(j + 1, SUB):
                upper[j, k] = repeat(cols[k], j) * r
                cols[k] = cols[k] - mult * upper[j, k]
            row = jnp.where(lanes == low + j, r, repeat(tile, j) * r)
            tile = jnp.where(subs == j, row, tile - mult * row)
            scale.append(r)
            rows.append(row)
        tiles[t] = tile
        for i in range(t + 1, count):
            cols = [spread(tiles[i], low + j) for j in range(SUB)]
            tile = jnp.where(panel, 0.0, tiles[i])
            for j in range(SUB):
                mult = cols[j] * scale[j]
                for k in range(j + 1, SUB):
                    cols[k] = cols[k] - mult * upper[j, k]
                tile = tile - mult * rows[j]
            tiles[i] = tile
    full = jnp.concatenate(tiles, axis=0)
    down = lax.broadcasted_iota(jnp.int32, (HALF, HALF), 0)
    across = lax.broadcasted_iota(jnp.int32, (HALF, HALF), 1)
    return jnp.where(across <= down, full, 0.0)


def inverse_body(gram_ref, out_ref):
    first = inverse_factor(gram_ref[:HALF, :HALF])
    side = dot(gram_ref[HALF:, :HALF], first, NT, HIGHEST)
    rest = gram_ref[HALF:, HALF:] - dot(side, side, NT, HIGHEST)
    second = inverse_factor(rest)
    out_ref[:HALF, :HALF] = first
    out_ref[:HALF, HALF:] = jnp.zeros((HALF, HALF), F32)
    out_ref[HALF:, :HALF] = -dot(second, dot(side, first, precision=HIGHEST), precision=HIGHEST)
    out_ref[HALF:, HALF:] = second


def inverse_cholesky(gram):
    return call(
        inverse_body, "inverse_cholesky", 12_000_000_000, 2 * 4 * RANK * RANK,
        out_shape=shaped(RANK, RANK), in_specs=[VMEM], out_specs=VMEM,
    )(gram)


def place(out_ref, me, blocks):
    for b, block in enumerate(blocks):
        out_ref[pl.ds(pl.multiple_of((me ^ b) * PART, PART), PART), :] = block


def start_kernel(me_ref, momentum_ref, gradient_ref, basis_ref, high_ref, low_ref, up_ref, down_ref, second_ref):
    rows, cols = momentum_ref.shape
    half = rows // 2

    def body(momentum, gradient, basis):
        step = pl.program_id(0)
        here = pl.ds(pl.multiple_of(step * STEP, STEP), STEP)
        bhigh, blow = split(basis[...])
        second_ref[here, :HALF], second_ref[here, HALF:] = bhigh[:, HALF:], blow[:, HALF:]
        high, low = split(momentum[...] + gradient[...].astype(F32))
        high_ref[:, here], low_ref[:, here] = high, low
        both = dot(high, jnp.concatenate([bhigh[:, :HALF], blow[:, :HALF]], axis=1))
        part = (both[:, :HALF] + both[:, HALF:]) + dot(low, bhigh[:, :HALF])

        @pl.when(step == 0)
        def _():
            up_ref[...] = part[:half]
            down_ref[...] = part[half:]

        @pl.when(step > 0)
        def _():
            up_ref[...] += part[:half]
            down_ref[...] += part[half:]

    block = pl.BlockSpec((rows, STEP), lambda i: (0, i), pipeline_mode=pl.Buffered(3))
    pltpu.emit_pipeline(
        body, grid=(cols // STEP,), in_specs=[block, block, pl.BlockSpec((STEP, RANK), lambda i: (i, 0))],
    )(momentum_ref, gradient_ref, basis_ref)


def start(me, *args):
    rows, cols = args[0].shape
    return call(
        start_kernel, "start", 4 * rows * cols * RANK, 6 * rows * cols,
        out_shape=[pltpu.VMEM((rows, cols), BF16)] * 2 + [shaped(rows // 2, HALF)] * 2 + [shaped(cols, RANK, dtype=BF16)],
        in_specs=[SMEM] + [HBM] * 3, out_specs=[VMEM] * 5,
    )(me, *(pltpu.with_memory_space_constraint(x, pltpu.HBM) for x in args))


def left_kernel(dims, high_ref, low_ref, factor_ref, *refs):
    up_ref, down_ref = refs[-2:]
    half = down_ref.shape[0]

    @pl.loop(0, 2 * half // TILE)
    def _(c):
        here = pl.ds(pl.multiple_of(c * TILE, TILE), TILE)
        both = dot(high_ref[here, :], factor_ref[...], dims)
        fhigh = factor_ref[:HALF, :] if dims == NT else factor_ref[:, :HALF]
        part = (both[:, :HALF] + both[:, HALF:]) + dot(low_ref[here, :], fhigh, dims)
        there = pl.ds(pl.multiple_of(lax.rem(c * TILE, half), TILE), TILE)

        @pl.when(c < half // TILE)
        def _():
            up_ref[there, :] = part

        @pl.when(c >= half // TILE)
        def _():
            down_ref[there, :] = part

    if len(refs) == 3:
        up_ref[half:, :] = refs[0][...]


def left_product(buffer, factor, *square, dims=NT):
    rows, cols = buffer[0].shape
    return call(
        functools.partial(left_kernel, dims), "left", 0, 4 * rows * cols,
        out_shape=[shaped(rows // 2 + SUB * len(square), HALF), shaped(rows // 2, HALF)],
        in_specs=[VMEM] * (3 + len(square)), out_specs=[VMEM] * 2,
    )(*buffer, factor, *square)


def product_kernel(first, scaled, me_ref, *refs):
    before, refs = ((), refs) if first else (refs[:1], refs[1:])
    up, up_more, down, down_more, high_ref, low_ref, keep_ref, give_ref, left_ref, plain_ref, turned_ref, pair_ref = refs
    rows = down.shape[0]
    top, bottom = up[:rows, :] + up_more[:rows, :], down[...] + down_more[...]
    if scaled:
        total = up[rows:rows + 1, :] + up_more[rows:rows + 1, :]
        scale = 1.0 / jnp.sqrt(total / F32(D) + F32(1e-06))
        top, bottom = top * scale, bottom * scale
    left_ref[:rows, :] = top
    left_ref[rows:, :] = bottom
    plain_ref[:, :rows] = top.T
    plain_ref[:, rows:] = bottom.T
    me = me_ref[0]
    for b in range(4):
        block = plain_ref[pl.ds(pl.multiple_of((me ^ b) * PART, PART), PART), :]
        turned_ref[PART * b:PART * (b + 1), :] = block
        pair_ref[PART * b:PART * (b + 1), :], pair_ref[HALF + PART * b:HALF + PART * (b + 1), :] = split(block)
    spot = 0
    for ref in (*before, left_ref):
        gram = dot(turned_ref[...], ref[...], precision=HIGHEST)
        keep_ref[:, spot:spot + HALF] = gram[:QUARTER]
        give_ref[:, spot:spot + HALF] = gram[QUARTER:]
        spot += HALF
    step = 2 * TILE
    for c in range(high_ref.shape[1] // step):
        lanes = pl.ds(c * step, step)
        both = dot(pair_ref[...], high_ref[:, lanes])
        part = (both[:HALF] + both[HALF:]) + dot(pair_ref[:HALF, :], low_ref[:, lanes])
        lanes = pl.ds(spot + c * step, step)
        keep_ref[:, lanes] = part[:QUARTER]
        give_ref[:, lanes] = part[QUARTER:]


def product(scaled, me, before, parts, buffer):
    rows, cols = buffer[0].shape
    width = HALF * (len(before) + 1) + cols
    return call(
        functools.partial(product_kernel, not before, scaled), "product", 4 * rows * width * RANK, 4 * rows * width,
        out_shape=[shaped(QUARTER, width)] * 2 + [shaped(rows, HALF)],
        in_specs=[SMEM] + [VMEM] * (6 + len(before)), out_specs=[VMEM] * 3,
        scratch_shapes=[pltpu.VMEM((HALF, rows), F32)] * 2 + [pltpu.VMEM((RANK, rows), BF16)],
    )(me, *before, *parts, *buffer)


def solved(inverse, wide_ref, out_ref, pair_ref):
    inverse = split(inverse)
    square = jnp.zeros((HALF, 1), F32)
    step = 2 * TILE
    for c in range(wide_ref.shape[1] // step):
        lanes = pl.ds(step * c, step)
        part = dot3(inverse, split(wide_ref[:, lanes]))
        out_ref[:, lanes] = part
        pair_ref[:HALF, lanes], pair_ref[HALF:, lanes] = split(part)
        square = square + jnp.sum(part * part, axis=1, keepdims=True)
    return jnp.broadcast_to(square, (HALF, HALF)).T[:SUB, :]


def first_kernel(me_ref, *refs):
    blocks, (inverse_ref, wide_ref, out_ref, pair_ref, square_ref, gram_ref) = refs[:4], refs[4:]
    me = me_ref[0]
    place(gram_ref, me, [ref[:, :HALF] for ref in blocks])
    place(wide_ref, me, [ref[:, HALF:] for ref in blocks])
    inverse_ref[...] = inverse_factor(gram_ref[...])
    square_ref[...] = solved(inverse_ref[...], wide_ref, out_ref, pair_ref)


def first_solve(me, blocks):
    cols = blocks[0].shape[1] - HALF
    return call(
        first_kernel, "first_solve", 5_000_000_000, 20 * HALF * cols,
        out_shape=[shaped(HALF, HALF), shaped(HALF, cols), shaped(HALF, cols), shaped(RANK, cols, dtype=BF16), shaped(SUB, HALF)],
        in_specs=[SMEM] + [VMEM] * 4, out_specs=[VMEM] * 5, scratch_shapes=[pltpu.VMEM((HALF, HALF), F32)],
    )(me, *blocks)


def second_kernel(me_ref, *refs):
    blocks, (first_ref, wide0_ref, inverse_ref, out_ref, pair_ref, square_ref, gram_ref, wide_ref) = refs[:4], refs[4:]
    me = me_ref[0]
    place(gram_ref, me, [ref[:, :RANK] for ref in blocks])
    place(wide_ref.at[HALF:, :], me, [ref[:, RANK:] for ref in blocks])
    wide_ref[:HALF, :] = wide0_ref[...]
    first = first_ref[...]
    side = dot(gram_ref[:, :HALF], first, NT, HIGHEST)
    second = inverse_factor(gram_ref[:, HALF:] - dot(side, side, NT, HIGHEST))
    inverse_ref[:HALF, :HALF] = first
    inverse_ref[:HALF, HALF:] = jnp.zeros((HALF, HALF), F32)
    inverse_ref[HALF:, :HALF] = -dot(second, dot(side, first, precision=HIGHEST), precision=HIGHEST)
    inverse_ref[HALF:, HALF:] = second
    square_ref[...] = solved(inverse_ref[HALF:, :], wide_ref, out_ref, pair_ref)


def second_solve(me, blocks, first, wide0):
    cols = blocks[0].shape[1] - RANK
    return call(
        second_kernel, "second_solve", 6_000_000_000, 20 * HALF * cols,
        out_shape=[shaped(RANK, RANK), shaped(HALF, cols), shaped(RANK, cols, dtype=BF16), shaped(SUB, HALF)],
        in_specs=[SMEM] + [VMEM] * 6, out_specs=[VMEM] * 4,
        scratch_shapes=[pltpu.VMEM((HALF, RANK), F32), pltpu.VMEM((RANK, cols), F32)],
    )(me, *blocks, first, wide0)


def ortho_kernel(left0_ref, left1_ref, inverse_ref, out_ref):
    left = jnp.concatenate([left0_ref[...], left1_ref[...]], axis=1)
    out_ref[...] = dot3(split(left), split(inverse_ref[...]), NT)


def ortho_product(left0, left1, inverse):
    rows = left0.shape[0]
    return call(
        ortho_kernel, "ortho", 6 * rows * RANK * RANK, 8 * rows * RANK,
        out_shape=shaped(rows, RANK), in_specs=[VMEM] * 3, out_specs=VMEM,
    )(left0, left1, inverse)


def update_kernel(ortho_ref, s0, s1, s2, s3, pair0_ref, pair1_ref, factor0_ref, factor1_ref, high_ref, low_ref, weight_ref, *refs):
    momentum_ref, out_ref, basis_ref, half_ref, triple_ref = refs
    total = (s0[0:1, :] + s1[0:1, :]) + (s2[0:1, :] + s3[0:1, :])
    scale = 1.0 / jnp.sqrt(total / F32(D) + F32(1e-06))
    step, width = pl.program_id(0), out_ref.shape[1]

    @pl.when(step == 0)
    def _():
        half_ref[...] = (F32(1.0 - beta_mom) * ortho_ref[...]).astype(BF16)
        high, low = split(ortho_ref[...] * (scale * F32(learn_rate * (D / RANK) ** 0.5)))
        triple_ref[:, :RANK] = high
        triple_ref[:, RANK:2 * RANK] = low
        triple_ref[:, 2 * RANK:] = high

    lanes = pl.ds(pl.multiple_of(step * width, width), width)
    high = [pair0_ref[:HALF, lanes], pair1_ref[:HALF, lanes]]
    feedback = dot(half_ref[...], jnp.concatenate(high, axis=0))
    momentum_ref[...] = (high_ref[:, lanes].astype(F32) + low_ref[:, lanes].astype(F32)) - feedback
    factor = jnp.concatenate([*high, *high, pair0_ref[HALF:, lanes], pair1_ref[HALF:, lanes]], axis=0)
    out_ref[...] = weight_ref[:, lanes] - dot(triple_ref[...], factor)
    basis_ref[:, :HALF] = factor0_ref[:, lanes].T * scale[:, :HALF]
    basis_ref[:, HALF:] = factor1_ref[:, lanes].T * scale[:, HALF:]


def update(ortho, squares, pairs, factors, buffer, weight):
    rows, cols = weight.shape
    tall = pl.BlockSpec((rows, TILE), lambda i: (0, i))
    return call(
        update_kernel, "update", 8 * rows * cols * RANK, 8 * rows * cols,
        out_shape=[shaped(rows, cols)] * 2 + [shaped(cols, RANK)], grid=(cols // TILE,), in_specs=[VMEM] * 12,
        out_specs=[tall, tall, pl.BlockSpec((TILE, RANK), lambda i: (i, 0))],
        scratch_shapes=[pltpu.VMEM((rows, RANK), BF16), pltpu.VMEM((rows, 3 * RANK), BF16)],
    )(ortho, *squares, *pairs, *factors, *buffer, weight)


def swap(x, axis, bit):
    size = lax.axis_size(axis)
    return lax.ppermute(x, axis, [(i, i ^ bit) for i in range(size)])


def together(*arrays):
    return lax.optimization_barrier(arrays)


def tuned(momentum, gradient, weight, right_basis):
    row = lax.axis_index("row")
    me = (2 * (row & 1) + ((row >> 1) & 1)).astype(jnp.int32)[None]
    high, low, up0, down0, second = start(me, momentum[0], gradient[0], right_basis)
    buffer = (high, low)
    got0 = swap(up0, "col", 1), swap(down0, "col", 2)
    up1, down1 = left_product(buffer, second, dims=NN)
    up0, down0, got0, up1, down1 = together(up0, down0, got0, up1, down1)
    for sweep in range(ITERS):
        last, scaled = sweep == ITERS - 1, sweep > 0

        up0, down0 = up0 + got0[0], down0 + got0[1]
        got0 = swap(up0, "col", 2), swap(down0, "col", 1)
        if sweep:
            up1, down1 = left_product(buffer, split1, square1)
        up0, down0, got0, up1, down1 = together(up0, down0, got0, up1, down1)

        keep0, give0, left0 = product(scaled, me, (), (up0, got0[0], down0, got0[1]), buffer)
        got1 = swap(up1, "col", 1), swap(down1, "col", 2)
        keep0, give0, left0, up1, down1, got1 = together(keep0, give0, left0, up1, down1, got1)

        part0 = keep0 + swap(give0, "row", 1)
        pair0 = swap(part0[PART:], "row", 2)
        up1, down1 = up1 + got1[0], down1 + got1[1]
        got1 = swap(up1, "col", 2), swap(down1, "col", 1)
        keep1, give1, left1 = product(scaled, me, (left0,), (up1, got1[0], down1, got1[1]), buffer)
        part0, pair0, keep1, give1 = together(part0, pair0, keep1, give1)

        side0 = part0[:PART] + pair0
        cross0 = swap(side0, "row", 4)
        part1 = keep1 + swap(give1, "row", 1)
        pair1 = [swap(part1[rows], "row", 2) for rows in (slice(PART, PART + PART // 2), slice(PART + PART // 2, None))]
        side0, cross0, part1, pair1 = together(side0, cross0, part1, pair1)

        total0 = side0 + cross0
        back0 = swap(total0, "row", 2)
        others0 = swap(total0, "row", 1), swap(back0, "row", 1)
        side1 = part1[:PART] + jnp.concatenate(pair1, axis=0)
        cross1 = swap(side1, "row", 4)
        total0, back0, others0, side1, cross1 = together(total0, back0, others0, side1, cross1)

        total1 = side1 + cross1
        back1, other1 = swap(total1, "row", 2), swap(total1, "row", 1)
        first, wide, factor0, split0, square0 = first_solve(me, (total0, back0, *others0))
        if not last:
            up0, down0 = left_product(buffer, split0, square0)
        total1, back1, other1, first, wide, split0, square0, up0, down0 = together(
            total1, back1, other1, first, wide, split0, square0, up0, down0
        )

        if not last:
            got0 = swap(up0, "col", 1), swap(down0, "col", 2)
        inverse, factor1, split1, square1 = second_solve(me, (total1, back1, other1, swap(back1, "row", 1)), first, wide)
        if not last:
            up0, down0, got0, split1, square1 = together(up0, down0, got0, split1, square1)

    square = jnp.concatenate([square0, square1], axis=1)
    squares = (square, swap(square, "col", 1), swap(square, "col", 2), swap(square, "col", 3))
    ortho = ortho_product(left0, left1, inverse)
    squares = together(*squares, ortho)[:4]
    new_momentum, new_weight, new_basis = update(ortho, squares, (split0, split1), (factor0, factor1), buffer, weight)
    return new_momentum[None], new_weight, new_basis


def general(momentum, gradient, weight, right_basis):
    replicas = lax.axis_size("rep")
    buffer = momentum[0] + gradient[0].astype(F32)
    basis, dims = right_basis, NN
    for sweep in range(ITERS):
        left = lax.psum(dot(buffer, basis, dims, HIGH) / replicas, ("col", "rep"))
        if sweep:
            left = left / rms
        gram = lax.psum(dot(left, left, ((0,), (0,)), HIGHEST), "row")
        wide = lax.psum(dot(left, buffer, ((0,), (0,)), HIGH) / replicas, ("row", "rep"))
        inverse = inverse_cholesky(gram)
        factor = dot(inverse, wide, precision=HIGHEST)
        rms = jnp.sqrt(lax.psum(jnp.sum(factor * factor, axis=1)[None, :], "col") / F32(D) + 1e-06)
        basis, dims = factor, NT
    ortho = dot(left, inverse, NT, HIGHEST)
    new_momentum = (buffer - (1.0 - beta_mom) * dot(ortho, factor, precision=HIGH))[None]
    basis = factor / rms.T
    new_weight = weight - learn_rate * jnp.sqrt(F32(D) / F32(RANK)) * dot(ortho, basis, precision=HIGH)
    return new_momentum, new_weight, basis.T


def solution(mesh):
    sizes = dict(mesh.shape)
    fits = sizes["row"] == 8 and sizes["col"] == 4 and sizes["rep"] == 1
    return jax.shard_map(
        tuned if fits else general,
        mesh=mesh,
        in_specs=(P("rep", "row", "col"), P("rep", "row", "col"), P("row", "col"), P("col", None)),
        out_specs=(P("rep", "row", "col"), P("row", "col"), P("col", None)),
        check_vma=False,
    )
```

```python
import functools

import jax
import jax.numpy as jnp
from jax import lax
from jax.experimental import pallas as pl
from jax.experimental.pallas import tpu as pltpu
from jax.sharding import PartitionSpec as P

D = 8192
RANK = 256
ITERS = 2
HALF = RANK // 2
QUARTER = RANK // 4
PART = RANK // 8
SUB = 8
TILE = 256
STEP = 512

beta_mom = 0.95
learn_rate = 0.05

F32 = jnp.float32
BF16 = jnp.bfloat16
HIGHEST = lax.Precision.HIGHEST
HIGH = lax.Precision.HIGH
NT = ((1,), (1,))
NN = ((1,), (0,))


def dot(a, b, dims=NN, precision=None):
    return lax.dot_general(a, b, (dims, ((), ())), precision=precision, preferred_element_type=F32)


def split(x):
    high = x.astype(BF16)
    return high, (x - high.astype(F32)).astype(BF16)


def dot3(a, b, dims=NN):
    return dot(a[0], b[0], dims) + (dot(a[1], b[0], dims) + dot(a[0], b[1], dims))


def call(kernel, name, flops, moved, **rest):
    rest.setdefault("compiler_params", pltpu.CompilerParams(vmem_limit_bytes=24 * 2**20))
    return pl.pallas_call(
        kernel,
        name=name,
        cost_estimate=pl.CostEstimate(flops=flops, bytes_accessed=moved, transcendentals=0),
        **rest,
    )


def shaped(*shape, dtype=F32):
    return jax.ShapeDtypeStruct(shape, dtype)


VMEM = pl.BlockSpec(memory_space=pltpu.VMEM)
HBM = pl.BlockSpec(memory_space=pltpu.HBM)
SMEM = pl.BlockSpec(memory_space=pltpu.SMEM)


def inverse_factor(block):
    shape = (SUB, HALF)
    lanes = lax.broadcasted_iota(jnp.int32, shape, 1)
    subs = lax.broadcasted_iota(jnp.int32, shape, 0)
    count = HALF // SUB

    def spread(tile, lane):
        return jnp.broadcast_to(tile[:, lane:lane + 1], shape)

    def repeat(tile, sub):
        return jnp.broadcast_to(tile[sub:sub + 1, :], shape)

    tiles = [block[SUB * i:SUB * (i + 1), :] for i in range(count)]
    for t in range(count):
        low = SUB * t
        panel = jnp.logical_and(lanes >= low, lanes < low + SUB)
        cols = [spread(tiles[t], low + j) for j in range(SUB)]
        tile = jnp.where(panel, 0.0, tiles[t])
        scale, rows, upper = [], [], {}
        for j in range(SUB):
            r = lax.rsqrt(repeat(cols[j], j))
            mult = jnp.where(subs > j, cols[j] * r, 0.0)
            for k in range(j + 1, SUB):
                upper[j, k] = repeat(cols[k], j) * r
                cols[k] = cols[k] - mult * upper[j, k]
            row = jnp.where(lanes == low + j, r, repeat(tile, j) * r)
            tile = jnp.where(subs == j, row, tile - mult * row)
            scale.append(r)
            rows.append(row)
        tiles[t] = tile
        for i in range(t + 1, count):
            cols = [spread(tiles[i], low + j) for j in range(SUB)]
            tile = jnp.where(panel, 0.0, tiles[i])
            for j in range(SUB):
                mult = cols[j] * scale[j]
                for k in range(j + 1, SUB):
                    cols[k] = cols[k] - mult * upper[j, k]
                tile = tile - mult * rows[j]
            tiles[i] = tile
    full = jnp.concatenate(tiles, axis=0)
    down = lax.broadcasted_iota(jnp.int32, (HALF, HALF), 0)
    across = lax.broadcasted_iota(jnp.int32, (HALF, HALF), 1)
    return jnp.where(across <= down, full, 0.0)


def inverse_body(gram_ref, out_ref):
    first = inverse_factor(gram_ref[:HALF, :HALF])
    side = dot(gram_ref[HALF:, :HALF], first, NT, HIGHEST)
    rest = gram_ref[HALF:, HALF:] - dot(side, side, NT, HIGHEST)
    second = inverse_factor(rest)
    out_ref[:HALF, :HALF] = first
    out_ref[:HALF, HALF:] = jnp.zeros((HALF, HALF), F32)
    out_ref[HALF:, :HALF] = -dot(second, dot(side, first, precision=HIGHEST), precision=HIGHEST)
    out_ref[HALF:, HALF:] = second


def inverse_cholesky(gram):
    return call(
        inverse_body, "inverse_cholesky", 12_000_000_000, 2 * 4 * RANK * RANK,
        out_shape=shaped(RANK, RANK), in_specs=[VMEM], out_specs=VMEM,
    )(gram)


def place(out_ref, me, blocks):
    for b, block in enumerate(blocks):
        out_ref[pl.ds(pl.multiple_of((me ^ b) * PART, PART), PART), :] = block


def start_kernel(me_ref, momentum_ref, gradient_ref, basis_ref, high_ref, low_ref, up_ref, down_ref, second_ref):
    rows, cols = momentum_ref.shape
    half = rows // 2

    def body(momentum, gradient, basis):
        step = pl.program_id(0)
        here = pl.ds(pl.multiple_of(step * STEP, STEP), STEP)
        bhigh, blow = split(basis[...])
        second_ref[here, :HALF], second_ref[here, HALF:] = bhigh[:, HALF:], blow[:, HALF:]
        high, low = split(momentum[...] + gradient[...].astype(F32))
        high_ref[:, here], low_ref[:, here] = high, low
        both = dot(high, jnp.concatenate([bhigh[:, :HALF], blow[:, :HALF]], axis=1))
        part = (both[:, :HALF] + both[:, HALF:]) + dot(low, bhigh[:, :HALF])

        @pl.when(step == 0)
        def _():
            up_ref[...] = part[:half]
            down_ref[...] = part[half:]

        @pl.when(step > 0)
        def _():
            up_ref[...] += part[:half]
            down_ref[...] += part[half:]

    block = pl.BlockSpec((rows, STEP), lambda i: (0, i))
    pltpu.emit_pipeline(
        body, grid=(cols // STEP,), in_specs=[block, block, pl.BlockSpec((STEP, RANK), lambda i: (i, 0))],
    )(momentum_ref, gradient_ref, basis_ref)


def start(me, *args):
    rows, cols = args[0].shape
    return call(
        start_kernel, "start", 4 * rows * cols * RANK, 6 * rows * cols,
        out_shape=[pltpu.VMEM((rows, cols), BF16)] * 2 + [shaped(rows // 2, HALF)] * 2 + [shaped(cols, RANK, dtype=BF16)],
        in_specs=[SMEM] + [HBM] * 3, out_specs=[VMEM] * 5,
    )(me, *(pltpu.with_memory_space_constraint(x, pltpu.HBM) for x in args))


def left_kernel(dims, tile, high_ref, low_ref, factor_ref, *refs):
    up_ref, down_ref = refs[-2:]
    half = down_ref.shape[0]

    @pl.loop(0, 2 * half // tile)
    def _(c):
        here = pl.ds(pl.multiple_of(c * tile, tile), tile)
        both = dot(high_ref[here, :], factor_ref[...], dims)
        fhigh = factor_ref[:HALF, :] if dims == NT else factor_ref[:, :HALF]
        part = (both[:, :HALF] + both[:, HALF:]) + dot(low_ref[here, :], fhigh, dims)
        there = pl.ds(pl.multiple_of(lax.rem(c * tile, half), tile), tile)

        @pl.when(c < half // tile)
        def _():
            up_ref[there, :] = part

        @pl.when(c >= half // tile)
        def _():
            down_ref[there, :] = part

    if len(refs) == 3:
        up_ref[half:, :] = refs[0][...]


def left_product(buffer, factor, *square, dims=NT, tile=TILE):
    rows, cols = buffer[0].shape
    return call(
        functools.partial(left_kernel, dims, tile), "left", 0, 4 * rows * cols,
        out_shape=[shaped(rows // 2 + SUB * len(square), HALF), shaped(rows // 2, HALF)],
        in_specs=[VMEM] * (3 + len(square)), out_specs=[VMEM] * 2,
    )(*buffer, factor, *square)


def product_kernel(first, scaled, me_ref, *refs):
    before, refs = ((), refs) if first else (refs[:1], refs[1:])
    up, up_more, down, down_more, high_ref, low_ref, keep_ref, give_ref, left_ref, plain_ref, turned_ref, pair_ref = refs
    rows = down.shape[0]
    top, bottom = up[:rows, :] + up_more[:rows, :], down[...] + down_more[...]
    if scaled:
        total = up[rows:rows + 1, :] + up_more[rows:rows + 1, :]
        scale = 1.0 / jnp.sqrt(total / F32(D) + F32(1e-06))
        top, bottom = top * scale, bottom * scale
    left_ref[:rows, :] = top
    left_ref[rows:, :] = bottom
    plain_ref[:, :rows] = top.T
    plain_ref[:, rows:] = bottom.T
    me = me_ref[0]
    for b in range(4):
        block = plain_ref[pl.ds(pl.multiple_of((me ^ b) * PART, PART), PART), :]
        turned_ref[PART * b:PART * (b + 1), :] = block
        pair_ref[PART * b:PART * (b + 1), :], pair_ref[HALF + PART * b:HALF + PART * (b + 1), :] = split(block)
    spot = 0
    for ref in (*before, left_ref):
        gram = dot(turned_ref[...], ref[...], precision=HIGHEST)
        keep_ref[:, spot:spot + HALF] = gram[:QUARTER]
        give_ref[:, spot:spot + HALF] = gram[QUARTER:]
        spot += HALF
    step = 2 * TILE
    for c in range(high_ref.shape[1] // step):
        lanes = pl.ds(c * step, step)
        both = dot(pair_ref[...], high_ref[:, lanes])
        part = (both[:HALF] + both[HALF:]) + dot(pair_ref[:HALF, :], low_ref[:, lanes])
        lanes = pl.ds(spot + c * step, step)
        keep_ref[:, lanes] = part[:QUARTER]
        give_ref[:, lanes] = part[QUARTER:]


def product(scaled, me, before, parts, buffer):
    rows, cols = buffer[0].shape
    width = HALF * (len(before) + 1) + cols
    return call(
        functools.partial(product_kernel, not before, scaled), "product", 4 * rows * width * RANK, 4 * rows * width,
        out_shape=[shaped(QUARTER, width)] * 2 + [shaped(rows, HALF)],
        in_specs=[SMEM] + [VMEM] * (6 + len(before)), out_specs=[VMEM] * 3,
        scratch_shapes=[pltpu.VMEM((HALF, rows), F32)] * 2 + [pltpu.VMEM((RANK, rows), BF16)],
    )(me, *before, *parts, *buffer)


def solved(inverse, wide_ref, out_ref, pair_ref):
    inverse = split(inverse)
    square = jnp.zeros((HALF, 1), F32)
    step = 2 * TILE
    for c in range(wide_ref.shape[1] // step):
        lanes = pl.ds(step * c, step)
        part = dot3(inverse, split(wide_ref[:, lanes]))
        out_ref[:, lanes] = part
        pair_ref[:HALF, lanes], pair_ref[HALF:, lanes] = split(part)
        square = square + jnp.sum(part * part, axis=1, keepdims=True)
    return jnp.broadcast_to(square, (HALF, HALF)).T[:SUB, :]


def first_kernel(me_ref, *refs):
    halves, (inverse_ref, wide_ref, out_ref, pair_ref, square_ref, gram_ref) = refs[:2], refs[2:]
    blocks = [ref.at[PART * b:PART * (b + 1), :] for ref in halves for b in range(2)]
    me = me_ref[0]
    place(gram_ref, me, [ref[:, :HALF] for ref in blocks])
    place(wide_ref, me, [ref[:, HALF:] for ref in blocks])
    inverse_ref[...] = inverse_factor(gram_ref[...])
    square_ref[...] = solved(inverse_ref[...], wide_ref, out_ref, pair_ref)


def first_solve(me, mine, other):
    cols = mine.shape[1] - HALF
    return call(
        first_kernel, "first_solve", 5_000_000_000, 20 * HALF * cols,
        out_shape=[shaped(HALF, HALF), shaped(HALF, cols), shaped(HALF, cols), shaped(RANK, cols, dtype=BF16), shaped(SUB, HALF)],
        in_specs=[SMEM] + [VMEM] * 2, out_specs=[VMEM] * 5, scratch_shapes=[pltpu.VMEM((HALF, HALF), F32)],
    )(me, mine, other)


def second_kernel(me_ref, *refs):
    blocks, (first_ref, wide0_ref, inverse_ref, out_ref, pair_ref, square_ref, gram_ref, wide_ref) = refs[:4], refs[4:]
    me = me_ref[0]
    place(gram_ref, me, [ref[:, :RANK] for ref in blocks])
    place(wide_ref.at[HALF:, :], me, [ref[:, RANK:] for ref in blocks])
    wide_ref[:HALF, :] = wide0_ref[...]
    first = first_ref[...]
    side = dot(gram_ref[:, :HALF], first, NT, HIGHEST)
    second = inverse_factor(gram_ref[:, HALF:] - dot(side, side, NT, HIGHEST))
    inverse_ref[:HALF, :HALF] = first
    inverse_ref[:HALF, HALF:] = jnp.zeros((HALF, HALF), F32)
    inverse_ref[HALF:, :HALF] = -dot(second, dot(side, first, precision=HIGHEST), precision=HIGHEST)
    inverse_ref[HALF:, HALF:] = second
    square_ref[...] = solved(inverse_ref[HALF:, :], wide_ref, out_ref, pair_ref)


def second_solve(me, blocks, first, wide0):
    cols = blocks[0].shape[1] - RANK
    return call(
        second_kernel, "second_solve", 6_000_000_000, 20 * HALF * cols,
        out_shape=[shaped(RANK, RANK), shaped(HALF, cols), shaped(RANK, cols, dtype=BF16), shaped(SUB, HALF)],
        in_specs=[SMEM] + [VMEM] * 6, out_specs=[VMEM] * 4,
        scratch_shapes=[pltpu.VMEM((HALF, RANK), F32), pltpu.VMEM((RANK, cols), F32)],
    )(me, *blocks, first, wide0)


def ortho_kernel(left0_ref, left1_ref, inverse_ref, out_ref):
    left = jnp.concatenate([left0_ref[...], left1_ref[...]], axis=1)
    out_ref[...] = dot3(split(left), split(inverse_ref[...]), NT)


def ortho_product(left0, left1, inverse):
    rows = left0.shape[0]
    return call(
        ortho_kernel, "ortho", 6 * rows * RANK * RANK, 8 * rows * RANK,
        out_shape=shaped(rows, RANK), in_specs=[VMEM] * 3, out_specs=VMEM,
    )(left0, left1, inverse)


def update_kernel(ortho_ref, s0, s1, s2, s3, pair0_ref, pair1_ref, factor0_ref, factor1_ref, high_ref, low_ref, weight_ref, *refs):
    momentum_ref, out_ref, basis_ref, half_ref, triple_ref = refs
    total = (s0[0:1, :] + s1[0:1, :]) + (s2[0:1, :] + s3[0:1, :])
    scale = 1.0 / jnp.sqrt(total / F32(D) + F32(1e-06))
    step, width = pl.program_id(0), out_ref.shape[1]

    @pl.when(step == 0)
    def _():
        half_ref[...] = (F32(1.0 - beta_mom) * ortho_ref[...]).astype(BF16)
        high, low = split(ortho_ref[...] * (scale * F32(learn_rate * (D / RANK) ** 0.5)))
        triple_ref[:, :RANK] = high
        triple_ref[:, RANK:2 * RANK] = low
        triple_ref[:, 2 * RANK:] = high

    lanes = pl.ds(pl.multiple_of(step * width, width), width)
    high = [pair0_ref[:HALF, lanes], pair1_ref[:HALF, lanes]]
    feedback = dot(half_ref[...], jnp.concatenate(high, axis=0))
    momentum_ref[...] = (high_ref[:, lanes].astype(F32) + low_ref[:, lanes].astype(F32)) - feedback
    factor = jnp.concatenate([*high, *high, pair0_ref[HALF:, lanes], pair1_ref[HALF:, lanes]], axis=0)
    out_ref[...] = weight_ref[:, lanes] - dot(triple_ref[...], factor)
    basis_ref[:, :HALF] = factor0_ref[:, lanes].T * scale[:, :HALF]
    basis_ref[:, HALF:] = factor1_ref[:, lanes].T * scale[:, HALF:]


def update(ortho, squares, pairs, factors, buffer, weight):
    rows, cols = weight.shape
    tall = pl.BlockSpec((rows, TILE), lambda i: (0, i))
    return call(
        update_kernel, "update", 8 * rows * cols * RANK, 8 * rows * cols,
        out_shape=[shaped(rows, cols)] * 2 + [shaped(cols, RANK)], grid=(cols // TILE,), in_specs=[VMEM] * 12,
        out_specs=[tall, tall, pl.BlockSpec((TILE, RANK), lambda i: (i, 0))],
        scratch_shapes=[pltpu.VMEM((rows, RANK), BF16), pltpu.VMEM((rows, 3 * RANK), BF16)],
    )(ortho, *squares, *pairs, *factors, *buffer, weight)


def swap(x, axis, bit):
    size = lax.axis_size(axis)
    return lax.ppermute(x, axis, [(i, i ^ bit) for i in range(size)])


def together(*arrays):
    return lax.optimization_barrier(arrays)


def tuned(momentum, gradient, weight, right_basis):
    row = lax.axis_index("row")
    me = (2 * (row & 1) + ((row >> 1) & 1)).astype(jnp.int32)[None]
    high, low, up0, down0, second = start(me, momentum[0], gradient[0], right_basis)
    buffer = (high, low)
    got0 = swap(up0, "col", 1), swap(down0, "col", 2)
    up1, down1 = left_product(buffer, second, dims=NN)
    up0, down0, got0, up1, down1 = together(up0, down0, got0, up1, down1)
    for sweep in range(ITERS):
        last, scaled = sweep == ITERS - 1, sweep > 0

        up0, down0 = up0 + got0[0], down0 + got0[1]
        got0 = swap(up0, "col", 2), swap(down0, "col", 1)
        if sweep:
            up1, down1 = left_product(buffer, split1, square1)
        up0, down0, got0, up1, down1 = together(up0, down0, got0, up1, down1)

        keep0, give0, left0 = product(scaled, me, (), (up0, got0[0], down0, got0[1]), buffer)
        got1 = swap(up1, "col", 1), swap(down1, "col", 2)
        keep0, give0, left0, up1, down1, got1 = together(keep0, give0, left0, up1, down1, got1)

        part0 = keep0 + swap(give0, "row", 1)
        pair0 = swap(part0[PART:], "row", 2)
        up1, down1 = up1 + got1[0], down1 + got1[1]
        got1 = swap(up1, "col", 2), swap(down1, "col", 1)
        keep1, give1, left1 = product(scaled, me, (left0,), (up1, got1[0], down1, got1[1]), buffer)
        part0, pair0, keep1, give1 = together(part0, pair0, keep1, give1)

        side0 = part0[:PART] + pair0
        cross0 = swap(side0, "row", 4)
        part1 = keep1 + swap(give1, "row", 1)
        pair1 = [swap(part1[rows], "row", 2) for rows in (slice(PART, PART + PART // 2), slice(PART + PART // 2, None))]
        side0, cross0, part1, pair1 = together(side0, cross0, part1, pair1)

        total0 = side0 + cross0
        back0 = swap(total0, "row", 2)
        side1 = part1[:PART] + jnp.concatenate(pair1, axis=0)
        cross1 = swap(side1, "row", 4)
        total0, back0, side1, cross1 = together(total0, back0, side1, cross1)

        mine0 = jnp.concatenate([total0, back0], axis=0)
        total1 = side1 + cross1
        back1, other1 = swap(total1, "row", 2), swap(total1, "row", 1)
        first, wide, factor0, split0, square0 = first_solve(me, mine0, swap(mine0, "row", 1))
        if not last:
            up0, down0 = left_product(buffer, split0, square0, tile=STEP)
        total1, back1, other1, first, wide, split0, square0, up0, down0 = together(
            total1, back1, other1, first, wide, split0, square0, up0, down0
        )

        if not last:
            got0 = swap(up0, "col", 1), swap(down0, "col", 2)
        inverse, factor1, split1, square1 = second_solve(me, (total1, back1, other1, swap(back1, "row", 1)), first, wide)
        if not last:
            up0, down0, got0, split1, square1 = together(up0, down0, got0, split1, square1)

    square = jnp.concatenate([square0, square1], axis=1)
    squares = (square, swap(square, "col", 1), swap(square, "col", 2), swap(square, "col", 3))
    ortho = ortho_product(left0, left1, inverse)
    squares = together(*squares, ortho)[:4]
    new_momentum, new_weight, new_basis = update(ortho, squares, (split0, split1), (factor0, factor1), buffer, weight)
    return new_momentum[None], new_weight, new_basis


def general(momentum, gradient, weight, right_basis):
    replicas = lax.axis_size("rep")
    buffer = momentum[0] + gradient[0].astype(F32)
    basis, dims = right_basis, NN
    for sweep in range(ITERS):
        left = lax.psum(dot(buffer, basis, dims, HIGH) / replicas, ("col", "rep"))
        if sweep:
            left = left / rms
        gram = lax.psum(dot(left, left, ((0,), (0,)), HIGHEST), "row")
        wide = lax.psum(dot(left, buffer, ((0,), (0,)), HIGH) / replicas, ("row", "rep"))
        inverse = inverse_cholesky(gram)
        factor = dot(inverse, wide, precision=HIGHEST)
        rms = jnp.sqrt(lax.psum(jnp.sum(factor * factor, axis=1)[None, :], "col") / F32(D) + 1e-06)
        basis, dims = factor, NT
    ortho = dot(left, inverse, NT, HIGHEST)
    new_momentum = (buffer - (1.0 - beta_mom) * dot(ortho, factor, precision=HIGH))[None]
    basis = factor / rms.T
    new_weight = weight - learn_rate * jnp.sqrt(F32(D) / F32(RANK)) * dot(ortho, basis, precision=HIGH)
    return new_momentum, new_weight, basis.T


def solution(mesh):
    sizes = dict(mesh.shape)
    fits = sizes["row"] == 8 and sizes["col"] == 4 and sizes["rep"] == 1
    return jax.shard_map(
        tuned if fits else general,
        mesh=mesh,
        in_specs=(P("rep", "row", "col"), P("rep", "row", "col"), P("row", "col"), P("col", None)),
        out_specs=(P("rep", "row", "col"), P("row", "col"), P("col", None)),
        check_vma=False,
    )
```

```python
import functools

import jax
import jax.numpy as jnp
from jax import lax
from jax.experimental import pallas as pl
from jax.experimental.pallas import tpu as pltpu
from jax.sharding import PartitionSpec as P

D = 8192
RANK = 256
ITERS = 2
HALF = RANK // 2
QUARTER = RANK // 4
PART = RANK // 8
SUB = 8
TILE = 256
STEP = 512

beta_mom = 0.95
learn_rate = 0.05

F32 = jnp.float32
BF16 = jnp.bfloat16
HIGHEST = lax.Precision.HIGHEST
HIGH = lax.Precision.HIGH
NT = ((1,), (1,))
NN = ((1,), (0,))


def dot(a, b, dims=NN, precision=None):
    return lax.dot_general(a, b, (dims, ((), ())), precision=precision, preferred_element_type=F32)


def split(x):
    high = x.astype(BF16)
    return high, (x - high.astype(F32)).astype(BF16)


def dot3(a, b, dims=NN):
    return dot(a[0], b[0], dims) + (dot(a[1], b[0], dims) + dot(a[0], b[1], dims))


def call(kernel, name, flops, moved, **rest):
    rest.setdefault("compiler_params", pltpu.CompilerParams(vmem_limit_bytes=24 * 2**20))
    return pl.pallas_call(
        kernel,
        name=name,
        cost_estimate=pl.CostEstimate(flops=flops, bytes_accessed=moved, transcendentals=0),
        **rest,
    )


def shaped(*shape, dtype=F32):
    return jax.ShapeDtypeStruct(shape, dtype)


VMEM = pl.BlockSpec(memory_space=pltpu.VMEM)
HBM = pl.BlockSpec(memory_space=pltpu.HBM)
SMEM = pl.BlockSpec(memory_space=pltpu.SMEM)


def inverse_factor(block):
    shape = (SUB, HALF)
    lanes = lax.broadcasted_iota(jnp.int32, shape, 1)
    subs = lax.broadcasted_iota(jnp.int32, shape, 0)
    count = HALF // SUB

    def spread(tile, lane):
        return jnp.broadcast_to(tile[:, lane:lane + 1], shape)

    def repeat(tile, sub):
        return jnp.broadcast_to(tile[sub:sub + 1, :], shape)

    def pivot(t, tile):
        low = SUB * t
        cols = [spread(tile, low + j) for j in range(SUB)]
        tile = jnp.where(within(t), 0.0, tile)
        scale, rows, upper = [], [], {}
        for j in range(SUB):
            r = lax.rsqrt(repeat(cols[j], j))
            mult = jnp.where(subs > j, cols[j] * r, 0.0)
            for k in range(j + 1, SUB):
                upper[j, k] = repeat(cols[k], j) * r
                cols[k] = cols[k] - mult * upper[j, k]
            row = jnp.where(lanes == low + j, r, repeat(tile, j) * r)
            tile = jnp.where(subs == j, row, tile - mult * row)
            scale.append(r)
            rows.append(row)
        return tile, (t, scale, rows, upper)

    def eliminate(tile, t, scale, rows, upper):
        cols = [spread(tile, SUB * t + j) for j in range(SUB)]
        tile = jnp.where(within(t), 0.0, tile)
        for j in range(SUB):
            mult = cols[j] * scale[j]
            for k in range(j + 1, SUB):
                cols[k] = cols[k] - mult * upper[j, k]
            tile = tile - mult * rows[j]
        return tile

    def within(t):
        return jnp.logical_and(lanes >= SUB * t, lanes < SUB * (t + 1))

    tiles = [block[SUB * i:SUB * (i + 1), :] for i in range(count)]
    before = None
    for t in range(count):
        if before is not None:
            tiles[t] = eliminate(tiles[t], *before)
        tiles[t], panel = pivot(t, tiles[t])
        if before is not None:
            for i in range(t + 1, count):
                tiles[i] = eliminate(tiles[i], *before)
        before = panel
    full = jnp.concatenate(tiles, axis=0)
    down = lax.broadcasted_iota(jnp.int32, (HALF, HALF), 0)
    across = lax.broadcasted_iota(jnp.int32, (HALF, HALF), 1)
    return jnp.where(across <= down, full, 0.0)


def inverse_body(gram_ref, out_ref):
    first = inverse_factor(gram_ref[:HALF, :HALF])
    side = dot(gram_ref[HALF:, :HALF], first, NT, HIGHEST)
    rest = gram_ref[HALF:, HALF:] - dot(side, side, NT, HIGHEST)
    second = inverse_factor(rest)
    out_ref[:HALF, :HALF] = first
    out_ref[:HALF, HALF:] = jnp.zeros((HALF, HALF), F32)
    out_ref[HALF:, :HALF] = -dot(second, dot(side, first, precision=HIGHEST), precision=HIGHEST)
    out_ref[HALF:, HALF:] = second


def inverse_cholesky(gram):
    return call(
        inverse_body, "inverse_cholesky", 12_000_000_000, 2 * 4 * RANK * RANK,
        out_shape=shaped(RANK, RANK), in_specs=[VMEM], out_specs=VMEM,
    )(gram)


def place(out_ref, me, blocks):
    for b, block in enumerate(blocks):
        out_ref[pl.ds(pl.multiple_of((me ^ b) * PART, PART), PART), :] = block


def start_kernel(me_ref, momentum_ref, gradient_ref, basis_ref, high_ref, low_ref, up_ref, down_ref, second_ref):
    rows, cols = momentum_ref.shape
    half = rows // 2

    def body(momentum, gradient, basis):
        step = pl.program_id(0)
        here = pl.ds(pl.multiple_of(step * STEP, STEP), STEP)
        bhigh, blow = split(basis[...])
        second_ref[here, :HALF], second_ref[here, HALF:] = bhigh[:, HALF:], blow[:, HALF:]
        high, low = split(momentum[...] + gradient[...].astype(F32))
        high_ref[:, here], low_ref[:, here] = high, low
        both = dot(high, jnp.concatenate([bhigh[:, :HALF], blow[:, :HALF]], axis=1))
        part = (both[:, :HALF] + both[:, HALF:]) + dot(low, bhigh[:, :HALF])

        @pl.when(step == 0)
        def _():
            up_ref[...] = part[:half]
            down_ref[...] = part[half:]

        @pl.when(step > 0)
        def _():
            up_ref[...] += part[:half]
            down_ref[...] += part[half:]

    block = pl.BlockSpec((rows, STEP), lambda i: (0, i))
    pltpu.emit_pipeline(
        body, grid=(cols // STEP,), in_specs=[block, block, pl.BlockSpec((STEP, RANK), lambda i: (i, 0))],
    )(momentum_ref, gradient_ref, basis_ref)


def start(me, *args):
    rows, cols = args[0].shape
    return call(
        start_kernel, "start", 4 * rows * cols * RANK, 6 * rows * cols,
        out_shape=[pltpu.VMEM((rows, cols), BF16)] * 2 + [shaped(rows // 2, HALF)] * 2 + [shaped(cols, RANK, dtype=BF16)],
        in_specs=[SMEM] + [HBM] * 3, out_specs=[VMEM] * 5,
    )(me, *(pltpu.with_memory_space_constraint(x, pltpu.HBM) for x in args))


def left_kernel(dims, tile, high_ref, low_ref, factor_ref, *refs):
    up_ref, down_ref = refs[-2:]
    half = down_ref.shape[0]

    @pl.loop(0, 2 * half // tile)
    def _(c):
        here = pl.ds(pl.multiple_of(c * tile, tile), tile)
        both = dot(high_ref[here, :], factor_ref[...], dims)
        fhigh = factor_ref[:HALF, :] if dims == NT else factor_ref[:, :HALF]
        part = (both[:, :HALF] + both[:, HALF:]) + dot(low_ref[here, :], fhigh, dims)
        there = pl.ds(pl.multiple_of(lax.rem(c * tile, half), tile), tile)

        @pl.when(c < half // tile)
        def _():
            up_ref[there, :] = part

        @pl.when(c >= half // tile)
        def _():
            down_ref[there, :] = part

    if len(refs) == 3:
        up_ref[half:, :] = refs[0][...]


def left_product(buffer, factor, *square, dims=NT, tile=TILE):
    rows, cols = buffer[0].shape
    return call(
        functools.partial(left_kernel, dims, tile), "left", 0, 4 * rows * cols,
        out_shape=[shaped(rows // 2 + SUB * len(square), HALF), shaped(rows // 2, HALF)],
        in_specs=[VMEM] * (3 + len(square)), out_specs=[VMEM] * 2,
    )(*buffer, factor, *square)


def product_kernel(first, scaled, me_ref, *refs):
    before, refs = ((), refs) if first else (refs[:1], refs[1:])
    up, up_more, down, down_more, high_ref, low_ref, keep_ref, give_ref, left_ref, plain_ref, turned_ref, pair_ref = refs
    rows = down.shape[0]
    top, bottom = up[:rows, :] + up_more[:rows, :], down[...] + down_more[...]
    if scaled:
        total = up[rows:rows + 1, :] + up_more[rows:rows + 1, :]
        scale = 1.0 / jnp.sqrt(total / F32(D) + F32(1e-06))
        top, bottom = top * scale, bottom * scale
    left_ref[:rows, :] = top
    left_ref[rows:, :] = bottom
    plain_ref[:, :rows] = top.T
    plain_ref[:, rows:] = bottom.T
    me = me_ref[0]
    for b in range(4):
        block = plain_ref[pl.ds(pl.multiple_of((me ^ b) * PART, PART), PART), :]
        turned_ref[PART * b:PART * (b + 1), :] = block
        pair_ref[PART * b:PART * (b + 1), :], pair_ref[HALF + PART * b:HALF + PART * (b + 1), :] = split(block)
    spot = 0
    for ref in (*before, left_ref):
        gram = dot(turned_ref[...], ref[...], precision=HIGHEST)
        keep_ref[:, spot:spot + HALF] = gram[:QUARTER]
        give_ref[:, spot:spot + HALF] = gram[QUARTER:]
        spot += HALF
    step = 2 * TILE
    for c in range(high_ref.shape[1] // step):
        lanes = pl.ds(c * step, step)
        both = dot(pair_ref[...], high_ref[:, lanes])
        part = (both[:HALF] + both[HALF:]) + dot(pair_ref[:HALF, :], low_ref[:, lanes])
        lanes = pl.ds(spot + c * step, step)
        keep_ref[:, lanes] = part[:QUARTER]
        give_ref[:, lanes] = part[QUARTER:]


def product(scaled, me, before, parts, buffer):
    rows, cols = buffer[0].shape
    width = HALF * (len(before) + 1) + cols
    return call(
        functools.partial(product_kernel, not before, scaled), "product", 4 * rows * width * RANK, 4 * rows * width,
        out_shape=[shaped(QUARTER, width)] * 2 + [shaped(rows, HALF)],
        in_specs=[SMEM] + [VMEM] * (6 + len(before)), out_specs=[VMEM] * 3,
        scratch_shapes=[pltpu.VMEM((HALF, rows), F32)] * 2 + [pltpu.VMEM((RANK, rows), BF16)],
    )(me, *before, *parts, *buffer)


def solved(inverse, wide_ref, out_ref, pair_ref):
    inverse = split(inverse)
    square = jnp.zeros((HALF, 1), F32)
    step = 2 * TILE
    for c in range(wide_ref.shape[1] // step):
        lanes = pl.ds(step * c, step)
        part = dot3(inverse, split(wide_ref[:, lanes]))
        out_ref[:, lanes] = part
        pair_ref[:HALF, lanes], pair_ref[HALF:, lanes] = split(part)
        square = square + jnp.sum(part * part, axis=1, keepdims=True)
    return jnp.broadcast_to(square, (HALF, HALF)).T[:SUB, :]


def first_kernel(me_ref, *refs):
    halves, (inverse_ref, wide_ref, out_ref, pair_ref, square_ref, gram_ref) = refs[:2], refs[2:]
    blocks = [ref.at[PART * b:PART * (b + 1), :] for ref in halves for b in range(2)]
    me = me_ref[0]
    place(gram_ref, me, [ref[:, :HALF] for ref in blocks])
    place(wide_ref, me, [ref[:, HALF:] for ref in blocks])
    inverse_ref[...] = inverse_factor(gram_ref[...])
    square_ref[...] = solved(inverse_ref[...], wide_ref, out_ref, pair_ref)


def first_solve(me, mine, other):
    cols = mine.shape[1] - HALF
    return call(
        first_kernel, "first_solve", 5_000_000_000, 20 * HALF * cols,
        out_shape=[shaped(HALF, HALF), shaped(HALF, cols), shaped(HALF, cols), shaped(RANK, cols, dtype=BF16), shaped(SUB, HALF)],
        in_specs=[SMEM] + [VMEM] * 2, out_specs=[VMEM] * 5, scratch_shapes=[pltpu.VMEM((HALF, HALF), F32)],
    )(me, mine, other)


def second_kernel(me_ref, *refs):
    blocks, (first_ref, wide0_ref, inverse_ref, out_ref, pair_ref, square_ref, gram_ref, wide_ref) = refs[:4], refs[4:]
    me = me_ref[0]
    place(gram_ref, me, [ref[:, :RANK] for ref in blocks])
    place(wide_ref.at[HALF:, :], me, [ref[:, RANK:] for ref in blocks])
    wide_ref[:HALF, :] = wide0_ref[...]
    first = first_ref[...]
    side = dot(gram_ref[:, :HALF], first, NT, HIGHEST)
    second = inverse_factor(gram_ref[:, HALF:] - dot(side, side, NT, HIGHEST))
    inverse_ref[:HALF, :HALF] = first
    inverse_ref[:HALF, HALF:] = jnp.zeros((HALF, HALF), F32)
    inverse_ref[HALF:, :HALF] = -dot(second, dot(side, first, precision=HIGHEST), precision=HIGHEST)
    inverse_ref[HALF:, HALF:] = second
    square_ref[...] = solved(inverse_ref[HALF:, :], wide_ref, out_ref, pair_ref)


def second_solve(me, blocks, first, wide0):
    cols = blocks[0].shape[1] - RANK
    return call(
        second_kernel, "second_solve", 6_000_000_000, 20 * HALF * cols,
        out_shape=[shaped(RANK, RANK), shaped(HALF, cols), shaped(RANK, cols, dtype=BF16), shaped(SUB, HALF)],
        in_specs=[SMEM] + [VMEM] * 6, out_specs=[VMEM] * 4,
        scratch_shapes=[pltpu.VMEM((HALF, RANK), F32), pltpu.VMEM((RANK, cols), F32)],
    )(me, *blocks, first, wide0)


def ortho_kernel(left0_ref, left1_ref, inverse_ref, out_ref):
    left = jnp.concatenate([left0_ref[...], left1_ref[...]], axis=1)
    out_ref[...] = dot3(split(left), split(inverse_ref[...]), NT)


def ortho_product(left0, left1, inverse):
    rows = left0.shape[0]
    return call(
        ortho_kernel, "ortho", 6 * rows * RANK * RANK, 8 * rows * RANK,
        out_shape=shaped(rows, RANK), in_specs=[VMEM] * 3, out_specs=VMEM,
    )(left0, left1, inverse)


def update_kernel(ortho_ref, s0, s1, s2, s3, pair0_ref, pair1_ref, factor0_ref, factor1_ref, high_ref, low_ref, weight_ref, *refs):
    momentum_ref, out_ref, basis_ref, half_ref, triple_ref = refs
    total = (s0[0:1, :] + s1[0:1, :]) + (s2[0:1, :] + s3[0:1, :])
    scale = 1.0 / jnp.sqrt(total / F32(D) + F32(1e-06))
    step, width = pl.program_id(0), out_ref.shape[1]

    @pl.when(step == 0)
    def _():
        half_ref[...] = (F32(1.0 - beta_mom) * ortho_ref[...]).astype(BF16)
        high, low = split(ortho_ref[...] * (scale * F32(learn_rate * (D / RANK) ** 0.5)))
        triple_ref[:, :RANK] = high
        triple_ref[:, RANK:2 * RANK] = low
        triple_ref[:, 2 * RANK:] = high

    lanes = pl.ds(pl.multiple_of(step * width, width), width)
    high = [pair0_ref[:HALF, lanes], pair1_ref[:HALF, lanes]]
    feedback = dot(half_ref[...], jnp.concatenate(high, axis=0))
    momentum_ref[...] = (high_ref[:, lanes].astype(F32) + low_ref[:, lanes].astype(F32)) - feedback
    factor = jnp.concatenate([*high, *high, pair0_ref[HALF:, lanes], pair1_ref[HALF:, lanes]], axis=0)
    out_ref[...] = weight_ref[:, lanes] - dot(triple_ref[...], factor)
    basis_ref[:, :HALF] = factor0_ref[:, lanes].T * scale[:, :HALF]
    basis_ref[:, HALF:] = factor1_ref[:, lanes].T * scale[:, HALF:]


def update(ortho, squares, pairs, factors, buffer, weight):
    rows, cols = weight.shape
    tall = pl.BlockSpec((rows, TILE), lambda i: (0, i))
    return call(
        update_kernel, "update", 8 * rows * cols * RANK, 8 * rows * cols,
        out_shape=[shaped(rows, cols)] * 2 + [shaped(cols, RANK)], grid=(cols // TILE,), in_specs=[VMEM] * 12,
        out_specs=[tall, tall, pl.BlockSpec((TILE, RANK), lambda i: (i, 0))],
        scratch_shapes=[pltpu.VMEM((rows, RANK), BF16), pltpu.VMEM((rows, 3 * RANK), BF16)],
    )(ortho, *squares, *pairs, *factors, *buffer, weight)


def swap(x, axis, bit):
    size = lax.axis_size(axis)
    return lax.ppermute(x, axis, [(i, i ^ bit) for i in range(size)])


def together(*arrays):
    return lax.optimization_barrier(arrays)


def tuned(momentum, gradient, weight, right_basis):
    row = lax.axis_index("row")
    me = (2 * (row & 1) + ((row >> 1) & 1)).astype(jnp.int32)[None]
    high, low, up0, down0, second = start(me, momentum[0], gradient[0], right_basis)
    buffer = (high, low)
    got0 = swap(up0, "col", 1), swap(down0, "col", 2)
    up1, down1 = left_product(buffer, second, dims=NN)
    up0, down0, got0, up1, down1 = together(up0, down0, got0, up1, down1)
    for sweep in range(ITERS):
        last, scaled = sweep == ITERS - 1, sweep > 0

        up0, down0 = up0 + got0[0], down0 + got0[1]
        got0 = swap(up0, "col", 2), swap(down0, "col", 1)
        if sweep:
            up1, down1 = left_product(buffer, split1, square1)
        up0, down0, got0, up1, down1 = together(up0, down0, got0, up1, down1)

        keep0, give0, left0 = product(scaled, me, (), (up0, got0[0], down0, got0[1]), buffer)
        got1 = swap(up1, "col", 1), swap(down1, "col", 2)
        keep0, give0, left0, up1, down1, got1 = together(keep0, give0, left0, up1, down1, got1)

        part0 = keep0 + swap(give0, "row", 1)
        pair0 = swap(part0[PART:], "row", 2)
        up1, down1 = up1 + got1[0], down1 + got1[1]
        got1 = swap(up1, "col", 2), swap(down1, "col", 1)
        keep1, give1, left1 = product(scaled, me, (left0,), (up1, got1[0], down1, got1[1]), buffer)
        part0, pair0, keep1, give1 = together(part0, pair0, keep1, give1)

        side0 = part0[:PART] + pair0
        cross0 = swap(side0, "row", 4)
        part1 = keep1 + swap(give1, "row", 1)
        pair1 = [swap(part1[rows], "row", 2) for rows in (slice(PART, PART + PART // 2), slice(PART + PART // 2, None))]
        side0, cross0, part1, pair1 = together(side0, cross0, part1, pair1)

        total0 = side0 + cross0
        back0 = swap(total0, "row", 2)
        side1 = part1[:PART] + jnp.concatenate(pair1, axis=0)
        cross1 = swap(side1, "row", 4)
        total0, back0, side1, cross1 = together(total0, back0, side1, cross1)

        mine0 = jnp.concatenate([total0, back0], axis=0)
        total1 = side1 + cross1
        back1, other1 = swap(total1, "row", 2), swap(total1, "row", 1)
        first, wide, factor0, split0, square0 = first_solve(me, mine0, swap(mine0, "row", 1))
        if not last:
            up0, down0 = left_product(buffer, split0, square0, tile=STEP)
        total1, back1, other1, first, wide, split0, square0, up0, down0 = together(
            total1, back1, other1, first, wide, split0, square0, up0, down0
        )

        if not last:
            got0 = swap(up0, "col", 1), swap(down0, "col", 2)
        inverse, factor1, split1, square1 = second_solve(me, (total1, back1, other1, swap(back1, "row", 1)), first, wide)
        if not last:
            up0, down0, got0, split1, square1 = together(up0, down0, got0, split1, square1)

    square = jnp.concatenate([square0, square1], axis=1)
    squares = (square, swap(square, "col", 1), swap(square, "col", 2), swap(square, "col", 3))
    ortho = ortho_product(left0, left1, inverse)
    squares = together(*squares, ortho)[:4]
    new_momentum, new_weight, new_basis = update(ortho, squares, (split0, split1), (factor0, factor1), buffer, weight)
    return new_momentum[None], new_weight, new_basis


def general(momentum, gradient, weight, right_basis):
    replicas = lax.axis_size("rep")
    buffer = momentum[0] + gradient[0].astype(F32)
    basis, dims = right_basis, NN
    for sweep in range(ITERS):
        left = lax.psum(dot(buffer, basis, dims, HIGH) / replicas, ("col", "rep"))
        if sweep:
            left = left / rms
        gram = lax.psum(dot(left, left, ((0,), (0,)), HIGHEST), "row")
        wide = lax.psum(dot(left, buffer, ((0,), (0,)), HIGH) / replicas, ("row", "rep"))
        inverse = inverse_cholesky(gram)
        factor = dot(inverse, wide, precision=HIGHEST)
        rms = jnp.sqrt(lax.psum(jnp.sum(factor * factor, axis=1)[None, :], "col") / F32(D) + 1e-06)
        basis, dims = factor, NT
    ortho = dot(left, inverse, NT, HIGHEST)
    new_momentum = (buffer - (1.0 - beta_mom) * dot(ortho, factor, precision=HIGH))[None]
    basis = factor / rms.T
    new_weight = weight - learn_rate * jnp.sqrt(F32(D) / F32(RANK)) * dot(ortho, basis, precision=HIGH)
    return new_momentum, new_weight, basis.T


def solution(mesh):
    sizes = dict(mesh.shape)
    fits = sizes["row"] == 8 and sizes["col"] == 4 and sizes["rep"] == 1
    return jax.shard_map(
        tuned if fits else general,
        mesh=mesh,
        in_specs=(P("rep", "row", "col"), P("rep", "row", "col"), P("row", "col"), P("col", None)),
        out_specs=(P("rep", "row", "col"), P("row", "col"), P("col", None)),
        check_vma=False,
    )
```
